32 devices in a mesh: mode: 2 (over y), dp: 4 (over z), depth: 4 (over x, core).
Axes of the slice: x: 2, y: 2, z: 4, core: 2. Of those that a mesh axis runs over, the one named last changes fastest.
Arguments:
- probe: float32 [2, 2, 192, 192], P('mode'), may hold values from -6 to 6
- object_slices: float32 [4, 2, 768, 256], P('depth', None, ('dp', 'mode')), as said below
- propagator_phase: float32 [192, 192], replicated, may hold values from -3.140625 to 3.140625
- positions: int32 [12, 2], P('dp'), may hold values from 0 to 768, as said below
- measured: float32 [12, 192, 192], P('dp'), may hold values from 0.2 to 3
Outputs:
- object_gradient: float32 [4, 2, 768, 256], P('depth', None, ('dp', 'mode'))
The draws below stay inside these ranges and needn't reach their ends.
Inputs may be any that keep to these rules, and one draw needn't show every extreme that they name: `positions`: position p belongs to data group p // 3; its row offset lies between that group's first row, group * 192, and 192 rows further, both included; its column offset lies between 0 and 64. In every group one position has row offset group * 192 + 192 and column 0, another row offset group * 192 and column 64. `object_slices`: real parts lie between 0.7 and 1.2, imaginary parts within 1.0 of zero.
All inputs are finite; a program needn't handle non-finite values.
Results may differ from the reference program's by a relative error of at most 0.0003.
Values sent between devices are 32-bit elements; how exact they have to be, the bound alone decides.
A program may use at most 64 MiB of HBM per device.

```python
import math
import jax
import jax.numpy as jnp
from jax import lax

W = 192
MODES = 2
SLICES = 4
POS_DEV = 3
POSITIONS = 12
OX = 256
OY = 768
N_DP = 4


def draw_object_slices(key, part):
    key = jax.random.fold_in(key, 11)
    key_real, key_imag = jax.random.split(key)
    real_part = jax.random.uniform(key_real, (SLICES, 1, OY, OX), jnp.float32, 0.7, 1.2)
    imag_part = 0.25 * jax.random.truncated_normal(key_imag, -4.0, 4.0, (SLICES, 1, OY, OX), jnp.float32)
    return jnp.concatenate([real_part, imag_part], 1)


def draw_positions(key, part):
    key = jax.random.fold_in(key, 23)
    key_rows, key_cols, key_turn = jax.random.split(key, 3)
    series = jnp.arange(POSITIONS, dtype=jnp.int32)
    group_of = series // POS_DEV
    turns = jax.random.randint(key_turn, (N_DP,), 0, POS_DEV, dtype=jnp.int32)
    slot_of = (series % POS_DEV + turns[group_of]) % POS_DEV
    row_offset = jax.random.randint(key_rows, (POSITIONS,), 0, W + 1, dtype=jnp.int32)
    col_offset = jax.random.randint(key_cols, (POSITIONS,), 0, OX - W + 1, dtype=jnp.int32)
    row_offset = jnp.where(slot_of == 0, W, jnp.where(slot_of == 1, 0, row_offset))
    col_offset = jnp.where(slot_of == 0, 0, jnp.where(slot_of == 1, OX - W, col_offset))
    return jnp.stack([group_of * W + row_offset, col_offset], 1).astype(jnp.int32)


def levels(rng, dims, shards, least, top_value):
    level, own = 1.0, jax.random.fold_in(rng, 6)
    for dim, blocks in shards:
        steps = jnp.exp(jax.random.uniform(jax.random.fold_in(own, dim), (blocks,), jnp.float32, least / len(shards), top_value / len(shards)))
        level = level * jnp.repeat(steps, dims[dim] // blocks).reshape([-1 if axis == dim else 1 for axis in range(len(dims))])
    return level


def normal_values(own_key, shape, deviation, reach, cuts=(), held_as=jnp.bfloat16):
    drawn = deviation * jax.random.normal(own_key, shape, jnp.float32)
    if cuts:
        drawn = drawn * levels(own_key, shape, cuts, -0.22, 0.18)
    return jnp.clip(drawn, -reach, reach).astype(held_as)


def setup_inputs(seed: int = 0) -> dict:
    seeds = jax.random.split(jax.random.key(seed), 6)
    return {
        "probe": normal_values(seeds[0], (MODES, 2, W, W), 0.4, 6.0, ((0, 2),), jnp.float32),
        "object_slices": draw_object_slices(jax.random.fold_in(seeds[5], 71), 0),
        "propagator_phase": jnp.clip(jax.random.uniform(seeds[2], (W, W), jnp.float32, -3.140625, 3.140625), -3.140625, 3.140625),
        "positions": draw_positions(jax.random.fold_in(seeds[5], 71), 0),
        "measured": jnp.clip(jnp.exp(math.log(3.0) - 2.7080502 * jax.random.uniform(seeds[4], (POSITIONS, W, W), jnp.float32) ** levels(seeds[4], (POSITIONS, W, W), ((0, 4),), -0.2, 0.2)), 0.2, 3.0),
    }


def reference(probe, object_slices, propagator_phase, positions, measured):
    kernel = jnp.cos(propagator_phase) + 1j * jnp.sin(propagator_phase)
    probe_modes = probe[:, 0] + 1j * probe[:, 1]
    window_width = probe.shape[-1]
    object_rows = object_slices.shape[2]
    extended = jnp.concatenate([object_slices, object_slices[:, :, :window_width]], axis=2)

    def loss_of(window, target):
        transmit = window[:, 0] + 1j * window[:, 1]
        wavefield = probe_modes
        for slice_at in range(transmit.shape[0]):
            spectrum = jnp.fft.fft2(wavefield * transmit[slice_at], norm='ortho')
            wavefield = jnp.fft.ifft2(spectrum * kernel, norm='ortho')
        far_field = jnp.fft.fft2(wavefield, norm='ortho')
        power_sum = lax.optimization_barrier(jnp.sum(jnp.real(far_field) ** 2 + jnp.imag(far_field) ** 2, axis=0))
        return 0.5 * jnp.sum((power_sum - target) ** 2)
    gradient_of = jax.grad(loss_of)

    def visit_one(running, record):
        corner_at, target = record
        anchor = jnp.zeros((), jnp.int32)
        corner = (anchor, anchor, corner_at[0].astype(jnp.int32), corner_at[1].astype(jnp.int32))
        window = lax.dynamic_slice(extended, corner, (SLICES, 2, window_width, window_width))
        window_grad = gradient_of(window, target)
        current = lax.dynamic_slice(running, corner, window_grad.shape)
        return (lax.dynamic_update_slice(running, current + window_grad, corner), None)
    running = jnp.zeros(extended.shape, extended.dtype)
    running, _ = lax.scan(visit_one, running, (positions, measured))
    return running[:, :, :object_rows].at[:, :, :window_width].add(running[:, :, object_rows:])
```

```python
import functools
import math

import jax
import jax.numpy as jnp
import ml_dtypes
import numpy as np
from jax import lax
from jax.experimental import pallas as pl
from jax.experimental.pallas import tpu as pltpu
from jax.sharding import PartitionSpec as P

MESH = pl.DeviceIdType.MESH
LANES = 128
F32 = jnp.float32
BF16 = jnp.bfloat16


def dft_tables(width, wide):
    series = np.arange(width)
    angles = (series[:, None] * series[None, :] % width) * (2.0 * math.pi / width)
    cosine = np.cos(angles) / math.sqrt(width)
    sine = np.sin(angles) / math.sqrt(width)
    rows_forward = np.block([[cosine, sine], [-sine, cosine]])
    rows_inverse = np.block([[cosine, -sine], [sine, cosine]])
    columns = np.zeros((wide, 2 * wide))
    columns[:width, :width] = cosine
    columns[:width, wide : wide + width] = sine
    tables = []
    for table in (rows_forward, rows_inverse, columns):
        head = table.astype(np.float32).astype(ml_dtypes.bfloat16)
        rest = (table - head.astype(np.float64)).astype(np.float32)
        tables += [head, rest.astype(ml_dtypes.bfloat16)]
    return tables


def split(value):
    head = value.astype(BF16)
    return head, (value - head.astype(F32)).astype(BF16)


def mm(a, b):
    return jnp.dot(a, b, preferred_element_type=F32)


def dot3(a_head, a_rest, b_head, b_rest):
    return mm(a_head, b_head) + (mm(a_head, b_rest) + mm(a_rest, b_head))


def kernel(
    M, N, D, POS, W, H, WIDE,
    pos_ref, probe_ref, obj_ref, phase_ref, meas_ref,
    lf_h, lf_l, li_h, li_l, rt_h, rt_l,
    out_ref,
    rim, probe_in, fr, win, psi, kr, ki, inten, far, up, gs, pg, og, rg_out, rg_in,
    rim_s, rim_r, prb_s, prb_r, fr_s, win_r, fwd_s, fwd_r, int_s, int_r,
    pg_s, pg_r, og_s, og_r, rg_s, rg_r,
):
    m = lax.axis_index("mode")
    g = lax.axis_index("dp")
    d = lax.axis_index("depth")
    c = d % 2
    half = M // 2
    u = (d // 2) * M + m
    p = u % D
    mu = 2 * (u // D) + c
    active = p < POS
    partner = (m, g, d + 1 - 2 * c)
    tail = W - LANES
    before = (m, (g + N - 1) % N, d)
    after = (m, (g + 1) % N, d)

    def handler(pos, mode):
        at = D * (mode // 2) + pos
        return at % M, 2 * (at // M) + mode % 2

    def remote(src, dst, s_sem, r_sem, device):
        return pltpu.make_async_remote_copy(
            src_ref=src, dst_ref=dst, send_sem=s_sem, recv_sem=r_sem,
            device_id=device, device_id_type=MESH,
        )

    def arrived(ref, sem):
        pltpu.make_async_copy(ref, ref, sem).wait()

    barrier = pltpu.get_barrier_semaphore()
    me = d * M + m
    for step in range(1, M * D):
        other = (me + step) % (M * D)
        pl.semaphore_signal(
            barrier, inc=1, device_id=(other % M, g, other // M), device_id_type=MESH
        )
    for device in (before, after):
        pl.semaphore_signal(barrier, inc=1, device_id=device, device_id_type=MESH)
    pl.semaphore_wait(barrier, M * D + 1)

    rim_copy = remote(obj_ref.at[0], rim, rim_s, rim_r, before)
    rim_copy.start()

    def probe_needed(mode_at):
        return 2 * (((d // 2) * M + mode_at) // D) + c

    def probe_copy(step):
        return remote(
            probe_ref.at[0], probe_in, prb_s.at[step - 1], prb_r, ((m + step) % M, g, d)
        )

    def probe_goes(step):
        target = (m + step) % M
        return (probe_needed(target) == m) & (((d // 2) * M + target) % D < POS)

    for step in range(1, M):
        @pl.when(probe_goes(step))
        def _():
            probe_copy(step).start()

    lane = lax.broadcasted_iota(jnp.int32, (1, LANES), 1)
    low = lane < tail

    def pack(re, im, put):
        put(0, re[:, :LANES])
        put(1, im[:, :LANES])
        put(2, jnp.where(low, re[:, LANES:], pltpu.roll(im[:, LANES:], tail, 1)))

    def unpack(a, b, t):
        re_tail = jnp.where(low, t, 0.0)
        im_tail = jnp.where(low, pltpu.roll(t, LANES - tail, 1), 0.0)
        return (
            jnp.concatenate([a, re_tail], axis=1),
            jnp.concatenate([b, im_tail], axis=1),
        )

    @pl.when(active)
    def _():
        kr[...] = jnp.zeros_like(kr)
        ki[...] = jnp.zeros_like(ki)
        phase = phase_ref[...]
        kr[:, :W] = jnp.cos(phase)
        ki[:, :W] = jnp.sin(phase)

    rim_copy.wait_recv()
    row_id = lax.broadcasted_iota(jnp.int32, (H, 1), 0) + m * H
    col_id = lax.broadcasted_iota(jnp.int32, (1, WIDE), 1)

    def frame_copy(pos, k):
        to_m, _ = handler(pos, 2 * k)
        to_d = 2 * ((D * k + pos) // M) + c
        place = win.at[d, :, pl.ds(pl.multiple_of(m * H, 8), H), :]
        own = (m == to_m) & (d == to_d)
        far_copy = remote(fr.at[pos], place, fr_s.at[pos, k], win_r.at[d, m], (to_m, g, to_d))
        near_copy = pltpu.make_async_copy(fr.at[pos], place, win_r.at[d, m])
        return own, far_copy, near_copy

    for pos in range(POS):
        row_off = pos_ref[pos, 0] - g * W
        col_off = pos_ref[pos, 1]
        parts = []
        for part in range(2):
            chosen = jnp.where(row_id >= row_off, obj_ref[0, part], rim[part])
            wrapped = pltpu.roll(chosen, WIDE - W, 1)
            parts.append(jnp.where(col_id >= col_off, chosen, wrapped))

        def put(at, value, pos=pos):
            fr[pos, at] = value

        pack(parts[0], parts[1], put)
        for k in range(half):
            own, far_copy, near_copy = frame_copy(pos, k)

            @pl.when(own)
            def _():
                near_copy.start()

            @pl.when(jnp.logical_not(own))
            def _():
                far_copy.start()

    def left(x, inverse):
        head, rest = split(x)
        if inverse:
            return dot3(li_h[...], li_l[...], head, rest)
        return dot3(lf_h[...], lf_l[...], head, rest)

    def right(x, inverse):
        head, rest = split(x)
        both = dot3(head, rest, rt_h[...], rt_l[...])
        cr, ci = both[:W, :WIDE], both[W:, :WIDE]
        sr, si = both[:W, WIDE:], both[W:, WIDE:]
        if inverse:
            return cr - si, ci + sr
        return cr + si, ci - sr

    def stack(re, im):
        return jnp.concatenate([re, im], axis=0)

    def dft(re, im):
        return right(left(stack(re, im), False), False)

    def idft(re, im):
        out = left(stack(*right(stack(re, im), True)), True)
        return out[:W], out[W:]

    def mul(ar, ai, br, bi):
        return ar * br - ai * bi, ar * bi + ai * br

    def cmul(ar, ai, br, bi):
        return ar * br + ai * bi, ar * bi - ai * br

    def window(s):
        return unpack(win[s, 0], win[s, 1], win[s, 2])

    def fwd_copy(s):
        return remote(win.at[s], win.at[s], fwd_s.at[s], fwd_r.at[s], partner)

    def int_copy(step):
        to_m, to_d = handler(p, (mu + step) % M)
        return remote(
            inten.at[0], inten.at[step], int_s.at[step - 1], int_r.at[step - 1], (to_m, g, to_d)
        )

    def pair_copy(s):
        return remote(gs.at[s], pg.at[s], pg_s.at[s], pg_r.at[s], partner)

    slot = p * half + mu // 2

    def owner_copy(s, to_m):
        place = gs.at[s, :, pl.ds(to_m * H, H), :]
        own = (m == to_m) & (d == s)
        far_copy = remote(place, og.at[slot], og_s.at[s, to_m], og_r.at[slot], (to_m, g, s))
        near_copy = pltpu.make_async_copy(place, og.at[slot], og_r.at[slot])
        return own, far_copy, near_copy

    def send_gradient(s, re, im):
        def put(at, value):
            gs[s, at] = value

        pack(re, im, put)

        @pl.when(s % 2 != c)
        def _():
            pair_copy(s).start()

    def finish_gradient(s):
        @pl.when(s % 2 == c)
        def _():
            arrived(pg.at[s], pg_r.at[s])
            gs[s] = gs[s] + pg[s]
            for to_m in range(M):
                own, far_copy, near_copy = owner_copy(s, to_m)

                @pl.when(own)
                def _():
                    near_copy.start()

                @pl.when(jnp.logical_not(own))
                def _():
                    far_copy.start()

    @pl.when(active)
    def _():
        @pl.when(mu != m)
        def _():
            arrived(probe_in, prb_r)

        @pl.when(mu == m)
        def _():
            probe_in[...] = probe_ref[0]

        row_off = pos_ref[p, 0] - g * W
        col_off = pos_ref[p, 1]
        i = lax.broadcasted_iota(jnp.int32, (W, W), 0) - row_off
        j = lax.broadcasted_iota(jnp.int32, (W, W), 1)
        rows_hot = jnp.where((i == j) | (i + W == j), 1.0, 0.0).astype(BF16)
        j = lax.broadcasted_iota(jnp.int32, (W, WIDE), 0)
        b = lax.broadcasted_iota(jnp.int32, (W, WIDE), 1)
        hit = ((b - col_off == j) | (b - col_off + W == j)) & (b < W)
        cols_hot = jnp.where(hit, 1.0, 0.0).astype(BF16)

        def thirds(x):
            first = x.astype(BF16)
            x = x - first.astype(F32)
            second = x.astype(BF16)
            return first, second, (x - second.astype(F32)).astype(BF16)

        for part in range(2):
            a0, a1, a2 = thirds(probe_in[part])
            moved = mm(a0, cols_hot) + (mm(a1, cols_hot) + mm(a2, cols_hot))
            b0, b1, b2 = thirds(moved)
            moved = mm(rows_hot, b0) + (mm(rows_hot, b1) + mm(rows_hot, b2))
            psi[0, part * W : (part + 1) * W, :] = moved

        def pass_on(at, carry):
            s = 2 * at + c
            for from_m in range(M):
                arrived(win.at[s, :, pl.ds(from_m * H, H), :], win_r.at[s, from_m])
            fwd_copy(s).start()
            return carry

        lax.fori_loop(0, D // 2, pass_on, 0)

        def await_window(s):
            @pl.when(s % 2 != c)
            def _():
                arrived(win.at[s], fwd_r.at[s])

        def forward(s, carry):
            await_window(s)
            wr, wi = window(s)
            fr_, fi_ = dft(*mul(psi[s, :W, :], psi[s, W:, :], wr, wi))
            nr, ni = idft(*mul(kr[...], ki[...], fr_, fi_))
            psi[s + 1, :W, :] = nr
            psi[s + 1, W:, :] = ni
            return carry

        lax.fori_loop(0, D - 1, forward, 0)
        last = D - 1
        await_window(last)
        wr, wi = window(last)
        fr_, fi_ = dft(*mul(psi[last, :W, :], psi[last, W:, :], wr, wi))
        fr_, fi_ = mul(kr[...], ki[...], fr_, fi_)
        far[:W, :] = fr_
        far[W:, :] = fi_
        inten[0] = fr_ * fr_ + fi_ * fi_
        for step in range(1, M):
            int_copy(step).start()
        for step in range(1, M):
            arrived(inten.at[step], int_r.at[step - 1])
        total = inten[0]
        for step in range(1, M):
            total = total + inten[step]
        far_r, far_i = far[:W, :], far[W:, :]
        up[...] = jnp.zeros_like(up)
        up[:W, :W] = meas_ref[p]
        weight = 2.0 * (total - up[:W, :])
        inc_r, inc_i = idft(*cmul(kr[...], ki[...], weight * far_r, weight * far_i))
        send_gradient(last, *cmul(psi[last, :W, :], psi[last, W:, :], inc_r, inc_i))
        up_r, up_i = cmul(wr, wi, inc_r, inc_i)
        up[:W, :] = up_r
        up[W:, :] = up_i

        def backward(at, carry):
            s = D - 2 - at
            gr, gi = dft(up[:W, :], up[W:, :])
            inc_r, inc_i = idft(*cmul(kr[...], ki[...], gr, gi))
            send_gradient(s, *cmul(psi[s, :W, :], psi[s, W:, :], inc_r, inc_i))
            finish_gradient(s + 1)
            wr, wi = window(s)
            up_r, up_i = cmul(wr, wi, inc_r, inc_i)
            up[:W, :] = up_r
            up[W:, :] = up_i
            return carry

        lax.fori_loop(0, D - 1, backward, 0)
        finish_gradient(jnp.int32(0))

    for part in range(2):
        rg_out[part] = jnp.zeros((H, WIDE), F32)
        out_ref[0, part] = jnp.zeros((H, WIDE), F32)
    for pos in range(POS):
        row_off = pos_ref[pos, 0] - g * W
        col_off = pos_ref[pos, 1]
        for k in range(half):
            arrived(og.at[pos * half + k], og_r.at[pos * half + k])
        parts = [og[pos * half, at] for at in range(3)]
        for k in range(1, half):
            parts = [parts[at] + og[pos * half + k, at] for at in range(3)]
        both = unpack(*parts)
        for part in range(2):
            inside = jnp.where(col_id >= col_off, both[part], 0.0)
            outside = jnp.where(col_id < col_off, both[part], 0.0)
            placed = inside + pltpu.roll(outside, W, 1)
            out_ref[0, part] += jnp.where(row_id >= row_off, placed, 0.0)
            rg_out[part] += jnp.where(row_id >= row_off, 0.0, placed)
    rg_copy = remote(rg_out, rg_in, rg_s, rg_r, after)
    rg_copy.start()
    rg_copy.wait_recv()
    for part in range(2):
        out_ref[0, part] += rg_in[part]

    rg_copy.wait_send()
    rim_copy.wait_send()
    for step in range(1, M):
        @pl.when(probe_goes(step))
        def _():
            probe_copy(step).wait_send()
    for pos in range(POS):
        for k in range(half):
            own, far_copy, _ = frame_copy(pos, k)

            @pl.when(jnp.logical_not(own))
            def _():
                far_copy.wait_send()

    @pl.when(active)
    def _():
        for step in range(1, M):
            int_copy(step).wait_send()
        for s in range(D):
            @pl.when(s % 2 == c)
            def _():
                fwd_copy(s).wait_send()
                for to_m in range(M):
                    own, far_copy, _ = owner_copy(s, to_m)

                    @pl.when(jnp.logical_not(own))
                    def _():
                        far_copy.wait_send()

            @pl.when(s % 2 != c)
            def _():
                pair_copy(s).wait_send()


def solution(mesh):
    M, N, D = mesh.shape["mode"], mesh.shape["dp"], mesh.shape["depth"]

    def body(probe, object_slices, propagator_phase, positions, measured):
        W = probe.shape[-1]
        H, WIDE = object_slices.shape[2], object_slices.shape[3]
        POS = positions.shape[0]
        assert object_slices.shape[0] == 1 and probe.shape[0] == 1
        assert H * M == W and POS <= D and WIDE == 2 * LANES and WIDE - W <= W - LANES
        half = M // 2
        tables = [jnp.asarray(table) for table in dft_tables(W, WIDE)]
        vmem = pl.BlockSpec(memory_space=pltpu.VMEM)
        dma = pltpu.SemaphoreType.DMA
        return pl.pallas_call(
            functools.partial(kernel, M, N, D, POS, W, H, WIDE),
            out_shape=jax.ShapeDtypeStruct(object_slices.shape, F32),
            in_specs=[pl.BlockSpec(memory_space=pltpu.SMEM)] + [vmem] * 10,
            out_specs=vmem,
            scratch_shapes=[
                pltpu.VMEM((2, H, WIDE), F32),
                pltpu.VMEM((2, W, W), F32),
                pltpu.VMEM((POS, 3, H, LANES), F32),
                pltpu.VMEM((D, 3, W, LANES), F32),
                pltpu.VMEM((D, 2 * W, WIDE), F32),
                pltpu.VMEM((W, WIDE), F32),
                pltpu.VMEM((W, WIDE), F32),
                pltpu.VMEM((M, W, WIDE), F32),
                pltpu.VMEM((2 * W, WIDE), F32),
                pltpu.VMEM((2 * W, WIDE), F32),
                pltpu.VMEM((D, 3, W, LANES), F32),
                pltpu.VMEM((D, 3, W, LANES), F32),
                pltpu.VMEM((POS * half, 3, H, LANES), F32),
                pltpu.VMEM((2, H, WIDE), F32),
                pltpu.VMEM((2, H, WIDE), F32),
                dma, dma,
                dma((M - 1,)), dma,
                dma((POS, half)), dma((D, M)),
                dma((D,)), dma((D,)),
                dma((M - 1,)), dma((M - 1,)),
                dma((D,)), dma((D,)),
                dma((D, M)), dma((POS * half,)),
                dma, dma,
            ],
            compiler_params=pltpu.CompilerParams(
                collective_id=0, has_side_effects=True, vmem_limit_bytes=48 * 1024 * 1024
            ),
        )(positions, probe, object_slices, propagator_phase, measured, *tables)

    placed = (
        P("mode", None, None, None),
        P("depth", None, ("dp", "mode"), None),
        P(),
        P("dp", None),
        P("dp", None, None),
    )
    return jax.shard_map(
        body,
        mesh=mesh,
        in_specs=placed,
        out_specs=P("depth", None, ("dp", "mode"), None),
        check_vma=False,
    )
```

```python
import functools
import math

import jax
import jax.numpy as jnp
import ml_dtypes
import numpy as np
from jax import lax
from jax.experimental import pallas as pl
from jax.experimental.pallas import tpu as pltpu
from jax.sharding import PartitionSpec as P

MESH = pl.DeviceIdType.MESH
LANES = 128
F32 = jnp.float32
BF16 = jnp.bfloat16


def dft_tables(width):
    mid = width // 2
    rows, columns = [], []
    for parity in (0, 1):
        angles = np.outer(2 * np.arange(mid) + parity, np.arange(mid)) % width
        turn = np.exp(-2j * math.pi * angles / width) / math.sqrt(width)
        real = np.block([[turn.real, -turn.imag], [turn.imag, turn.real]])
        wide = np.zeros((2 * LANES, 2 * LANES))
        for a in range(2):
            for b in range(2):
                wide[a * LANES : a * LANES + mid, b * LANES : b * LANES + mid] = real[
                    b * mid : (b + 1) * mid, a * mid : (a + 1) * mid
                ].T
        rows.append(real)
        columns.append(wide)
    stacks = []
    for pair in (rows, columns):
        listed = []
        for table in pair + [one.T for one in pair]:
            head = table.astype(np.float32).astype(ml_dtypes.bfloat16)
            rest = (table - head.astype(np.float64)).astype(np.float32)
            listed += [head, rest.astype(ml_dtypes.bfloat16)]
        stacks.append(np.stack(listed))
    return stacks


def split(value):
    head = value.astype(BF16)
    return head, (value - head.astype(F32)).astype(BF16)


def mm(a, b):
    return jnp.dot(a, b, preferred_element_type=F32)


def dot3(a_head, a_rest, b_head, b_rest):
    return mm(a_head, b_head) + (mm(a_head, b_rest) + mm(a_rest, b_head))


def kernel(
    M, N, D, POS, W, H, WIDE, CH,
    pos_ref, probe_ref, obj_ref, phase_ref, meas_ref,
    row_hbm, col_hbm,
    out_ref,
    tile, phase, meas, row_t, col_t,
    rim, probe_in, fr, win, psi, kr, ki, inten, far, up, gs, pg, og, rg_out, rg_in,
    load, rim_s, rim_r, prb_s, prb_r, fr_s, win_r, fwd_s, fwd_r, int_s, int_r,
    pg_s, pg_r, og_s, og_r, rg_s, rg_r,
):
    m = lax.axis_index("mode")
    g = lax.axis_index("dp")
    d = lax.axis_index("depth")
    c = d % 2
    half = M // 2
    u = (d // 2) * M + m
    p = u % D
    mu = 2 * (u // D) + c
    active = p < POS
    partner = (m, g, d + 1 - 2 * c)
    tail = W - LANES
    mid = W // 2
    HC = H // CH
    before = (m, (g + N - 1) % N, d)
    after = (m, (g + 1) % N, d)

    def handler(pos, mode):
        at = D * (mode // 2) + pos
        return at % M, 2 * (at // M) + mode % 2

    def remote(src, dst, s_sem, r_sem, device):
        return pltpu.make_async_remote_copy(
            src_ref=src, dst_ref=dst, send_sem=s_sem, recv_sem=r_sem,
            device_id=device, device_id_type=MESH,
        )

    def arrived(ref, sem):
        pltpu.make_async_copy(ref, ref, sem).wait()

    loads = [
        pltpu.make_async_copy(src, dst, load.at[at])
        for at, (src, dst) in enumerate(
            ((phase_ref, phase), (obj_ref.at[0], tile), (row_hbm, row_t), (col_hbm, col_t))
        )
    ]
    for one in loads:
        one.start()
    meas_load = pltpu.make_async_copy(meas_ref.at[jnp.minimum(p, POS - 1)], meas, load.at[4])
    meas_load.start()
    own_probe = pltpu.make_async_copy(probe_ref.at[0], probe_in, prb_r)

    @pl.when(active & (mu == m))
    def _():
        own_probe.start()

    barrier = pltpu.get_barrier_semaphore()
    me = d * M + m
    for step in range(1, M * D):
        other = (me + step) % (M * D)
        pl.semaphore_signal(
            barrier, inc=1, device_id=(other % M, g, other // M), device_id_type=MESH
        )
    for device in (before, after):
        pl.semaphore_signal(barrier, inc=1, device_id=device, device_id_type=MESH)
    pl.semaphore_wait(barrier, M * D + 1)

    def rim_copy(ch):
        rows = pl.ds(ch * HC, HC)
        return remote(
            obj_ref.at[0, :, rows, :], rim.at[:, rows, :], rim_s.at[ch], rim_r.at[ch], before
        )

    for ch in range(CH):
        rim_copy(ch).start()

    def probe_needed(mode_at):
        return 2 * (((d // 2) * M + mode_at) // D) + c

    def probe_copy(step):
        return remote(
            probe_ref.at[0], probe_in, prb_s.at[step - 1], prb_r, ((m + step) % M, g, d)
        )

    def probe_goes(step):
        target = (m + step) % M
        return (probe_needed(target) == m) & (((d // 2) * M + target) % D < POS)

    for step in range(1, M):
        @pl.when(probe_goes(step))
        def _():
            probe_copy(step).start()

    lane = lax.broadcasted_iota(jnp.int32, (1, LANES), 1)
    low = lane < tail

    def pack(re, im, put):
        put(0, re[:, :LANES])
        put(1, im[:, :LANES])
        put(2, jnp.where(low, re[:, LANES:], pltpu.roll(im[:, LANES:], tail, 1)))

    def unpack(a, b, t):
        re_tail = jnp.where(low, t, 0.0)
        im_tail = jnp.where(low, pltpu.roll(t, LANES - tail, 1), 0.0)
        return (
            jnp.concatenate([a, re_tail], axis=1),
            jnp.concatenate([b, im_tail], axis=1),
        )

    def thirds(x):
        first = x.astype(BF16)
        x = x - first.astype(F32)
        second = x.astype(BF16)
        return first, second, (x - second.astype(F32)).astype(BF16)

    def hot(mask):
        return jnp.where(mask, 1.0, 0.0).astype(BF16)

    def moved(x, rows_hot, cols_hot):
        a0, a1, a2 = thirds(x)
        x = mm(a0, cols_hot) + (mm(a1, cols_hot) + mm(a2, cols_hot))
        a0, a1, a2 = thirds(x)
        return mm(rows_hot, a0) + (mm(rows_hot, a1) + mm(rows_hot, a2))

    def wide_iota(axis):
        return lax.broadcasted_iota(jnp.int32, (W, WIDE), axis)

    def square_iota(axis):
        return lax.broadcasted_iota(jnp.int32, (W, W), axis)

    block_lane = wide_iota(1)
    in_second = block_lane >= LANES
    at_lane = jnp.where(in_second, block_lane - LANES, block_lane)
    filled = at_lane < mid

    loads[0].wait()
    meas_load.wait()

    @pl.when(active)
    def _():
        i = square_iota(0)
        rows_hot = hot(square_iota(1) == jnp.where(i < mid, 2 * i, 2 * (i - mid) + 1))
        wanted = jnp.where(in_second, 2 * at_lane + 1, 2 * at_lane)
        cols_hot = hot((wide_iota(0) == wanted) & filled)
        turned = moved(phase[...], rows_hot, cols_hot)
        kr[...] = jnp.cos(turned)
        ki[...] = jnp.sin(turned)
        up[:W, :] = moved(meas[...], rows_hot, cols_hot)

    loads[1].wait()
    row_id = lax.broadcasted_iota(jnp.int32, (H, 1), 0) + m * H
    col_id = lax.broadcasted_iota(jnp.int32, (1, WIDE), 1)

    def frame_copy(pos, k, start=0, rows=H):
        to_m, _ = handler(pos, 2 * k)
        to_d = 2 * ((D * k + pos) // M) + c
        source = fr.at[pos, :, pl.ds(start, rows), :]
        place = win.at[d, :, pl.ds(pl.multiple_of(m * H + start, 8), rows), :]
        own = (m == to_m) & (d == to_d)
        far_copy = remote(source, place, fr_s.at[pos, k], win_r.at[d, m], (to_m, g, to_d))
        near_copy = pltpu.make_async_copy(source, place, win_r.at[d, m])
        return own, far_copy, near_copy

    for ch in range(CH):
        rim_copy(ch).wait_recv()
        rows = slice(ch * HC, (ch + 1) * HC)
        for pos in range(POS):
            row_off = pos_ref[pos, 0] - g * W
            col_off = pos_ref[pos, 1]
            parts = []
            for part in range(2):
                chosen = jnp.where(row_id[rows] >= row_off, tile[part, rows], rim[part, rows])
                wrapped = pltpu.roll(chosen, WIDE - W, 1)
                parts.append(jnp.where(col_id >= col_off, chosen, wrapped))

            def put(at, value, pos=pos, rows=rows):
                fr[pos, at, rows] = value

            pack(parts[0], parts[1], put)
            for k in range(half):
                own, far_copy, near_copy = frame_copy(pos, k, ch * HC, HC)

                @pl.when(own)
                def _():
                    near_copy.start()

                @pl.when(jnp.logical_not(own))
                def _():
                    far_copy.start()

    loads[2].wait()
    loads[3].wait()

    def by_rows(at, x):
        head, rest = split(x)
        return dot3(row_t[2 * at], row_t[2 * at + 1], head, rest)

    def by_columns(at, x):
        head, rest = split(x)
        return dot3(head, rest, col_t[2 * at], col_t[2 * at + 1])

    def dft(re, im):
        z0 = jnp.concatenate([re[:mid], im[:mid]], axis=0)
        z1 = jnp.concatenate([re[mid:], im[mid:]], axis=0)
        even, odd = by_rows(0, z0 + z1), by_rows(1, z0 - z1)
        re = jnp.concatenate([even[:mid], odd[:mid]], axis=0)
        im = jnp.concatenate([even[mid:], odd[mid:]], axis=0)
        z0 = jnp.concatenate([re[:, :LANES], im[:, :LANES]], axis=1)
        z1 = jnp.concatenate([re[:, LANES:], im[:, LANES:]], axis=1)
        even, odd = by_columns(0, z0 + z1), by_columns(1, z0 - z1)
        re = jnp.concatenate([even[:, :LANES], odd[:, :LANES]], axis=1)
        im = jnp.concatenate([even[:, LANES:], odd[:, LANES:]], axis=1)
        return re, im

    def idft(re, im):
        even = by_columns(2, jnp.concatenate([re[:, :LANES], im[:, :LANES]], axis=1))
        odd = by_columns(3, jnp.concatenate([re[:, LANES:], im[:, LANES:]], axis=1))
        z0, z1 = even + odd, even - odd
        re = jnp.concatenate([z0[:, :LANES], z1[:, :LANES]], axis=1)
        im = jnp.concatenate([z0[:, LANES:], z1[:, LANES:]], axis=1)
        even = by_rows(2, jnp.concatenate([re[:mid], im[:mid]], axis=0))
        odd = by_rows(3, jnp.concatenate([re[mid:], im[mid:]], axis=0))
        z0, z1 = even + odd, even - odd
        re = jnp.concatenate([z0[:mid], z1[:mid]], axis=0)
        im = jnp.concatenate([z0[mid:], z1[mid:]], axis=0)
        return re, im

    def mul(ar, ai, br, bi):
        return ar * br - ai * bi, ar * bi + ai * br

    def cmul(ar, ai, br, bi):
        return ar * br + ai * bi, ar * bi - ai * br

    def window(s):
        both = unpack(win[s, 0], win[s, 1], win[s, 2])
        return [
            jnp.concatenate(
                [one[:, :LANES], pltpu.roll(one, LANES - mid, 1)[:, LANES:]], axis=1
            )
            for one in both
        ]

    def fwd_copy(s):
        return remote(win.at[s], win.at[s], fwd_s.at[s], fwd_r.at[s], partner)

    def int_copy(step):
        to_m, to_d = handler(p, (mu + step) % M)
        return remote(
            inten.at[0], inten.at[step], int_s.at[step - 1], int_r.at[step - 1], (to_m, g, to_d)
        )

    def pair_copy(s):
        return remote(gs.at[s], pg.at[s], pg_s.at[s], pg_r.at[s], partner)

    slot = p * half + mu // 2

    def owner_copy(s, to_m):
        place = gs.at[s, :, pl.ds(to_m * H, H), :]
        own = (m == to_m) & (d == s)
        far_copy = remote(place, og.at[slot], og_s.at[s, to_m], og_r.at[slot], (to_m, g, s))
        near_copy = pltpu.make_async_copy(place, og.at[slot], og_r.at[slot])
        return own, far_copy, near_copy

    def send_gradient(s, re, im):
        def put(at, value):
            gs[s, at] = value

        back = WIDE - (LANES - mid)
        re = jnp.where(col_id < mid, re, pltpu.roll(re, back, 1))
        im = jnp.where(col_id < mid, im, pltpu.roll(im, back, 1))
        pack(re, im, put)

        @pl.when(s % 2 != c)
        def _():
            pair_copy(s).start()

    def finish_gradient(s):
        @pl.when(s % 2 == c)
        def _():
            arrived(pg.at[s], pg_r.at[s])
            gs[s] = gs[s] + pg[s]
            for to_m in range(M):
                own, far_copy, near_copy = owner_copy(s, to_m)

                @pl.when(own)
                def _():
                    near_copy.start()

                @pl.when(jnp.logical_not(own))
                def _():
                    far_copy.start()

    @pl.when(active)
    def _():
        arrived(probe_in, prb_r)
        row_off = pos_ref[p, 0] - g * W
        col_off = pos_ref[p, 1]
        i = square_iota(0) - row_off
        j = square_iota(1)
        rows_hot = hot((i == j) | (i + W == j))
        b = jnp.where(in_second, at_lane + mid, at_lane) - col_off
        j = wide_iota(0)
        cols_hot = hot(((b == j) | (b + W == j)) & filled)
        for part in range(2):
            psi[0, part * W : (part + 1) * W, :] = moved(probe_in[part], rows_hot, cols_hot)

        def pass_on(at):
            s = 2 * at + c
            for from_m in range(M):
                arrived(win.at[s, :, pl.ds(from_m * H, H), :], win_r.at[s, from_m])
            fwd_copy(s).start()

        pass_on(0)

        def await_window(s):
            @pl.when(s % 2 != c)
            def _():
                arrived(win.at[s], fwd_r.at[s])

        def forward(s, carry):
            await_window(s)
            wr, wi = window(s)
            fr_, fi_ = dft(*mul(psi[s, :W, :], psi[s, W:, :], wr, wi))
            nr, ni = idft(*mul(kr[...], ki[...], fr_, fi_))
            psi[s + 1, :W, :] = nr
            psi[s + 1, W:, :] = ni

            @pl.when((s % 2 == 0) & (s + 2 < D))
            def _():
                pass_on(s // 2 + 1)

            return carry

        lax.fori_loop(0, D - 1, forward, 0)
        last = D - 1
        await_window(last)
        wr, wi = window(last)
        fr_, fi_ = dft(*mul(psi[last, :W, :], psi[last, W:, :], wr, wi))
        fr_, fi_ = mul(kr[...], ki[...], fr_, fi_)
        far[:W, :] = fr_
        far[W:, :] = fi_
        inten[0] = fr_ * fr_ + fi_ * fi_
        for step in range(1, M):
            int_copy(step).start()
        for step in range(1, M):
            arrived(inten.at[step], int_r.at[step - 1])
        total = inten[0]
        for step in range(1, M):
            total = total + inten[step]
        far_r, far_i = far[:W, :], far[W:, :]
        weight = 2.0 * (total - up[:W, :])
        inc_r, inc_i = idft(*cmul(kr[...], ki[...], weight * far_r, weight * far_i))
        send_gradient(last, *cmul(psi[last, :W, :], psi[last, W:, :], inc_r, inc_i))
        up_r, up_i = cmul(wr, wi, inc_r, inc_i)
        up[:W, :] = up_r
        up[W:, :] = up_i

        def backward(at, carry):
            s = D - 2 - at
            gr, gi = dft(up[:W, :], up[W:, :])
            inc_r, inc_i = idft(*cmul(kr[...], ki[...], gr, gi))
            send_gradient(s, *cmul(psi[s, :W, :], psi[s, W:, :], inc_r, inc_i))
            finish_gradient(s + 1)
            wr, wi = window(s)
            up_r, up_i = cmul(wr, wi, inc_r, inc_i)
            up[:W, :] = up_r
            up[W:, :] = up_i
            return carry

        lax.fori_loop(0, D - 1, backward, 0)
        finish_gradient(jnp.int32(0))

    for part in range(2):
        rg_out[part] = jnp.zeros((H, WIDE), F32)
        out_ref[0, part] = jnp.zeros((H, WIDE), F32)
    for pos in range(POS):
        row_off = pos_ref[pos, 0] - g * W
        col_off = pos_ref[pos, 1]
        for k in range(half):
            arrived(og.at[pos * half + k], og_r.at[pos * half + k])
        parts = [og[pos * half, at] for at in range(3)]
        for k in range(1, half):
            parts = [parts[at] + og[pos * half + k, at] for at in range(3)]
        both = unpack(*parts)
        for part in range(2):
            inside = jnp.where(col_id >= col_off, both[part], 0.0)
            outside = jnp.where(col_id < col_off, both[part], 0.0)
            placed = inside + pltpu.roll(outside, W, 1)
            out_ref[0, part] += jnp.where(row_id >= row_off, placed, 0.0)
            rg_out[part] += jnp.where(row_id >= row_off, 0.0, placed)
    rg_copy = remote(rg_out, rg_in, rg_s, rg_r, after)
    rg_copy.start()
    rg_copy.wait_recv()
    for part in range(2):
        out_ref[0, part] += rg_in[part]

    rg_copy.wait_send()
    for ch in range(CH):
        rim_copy(ch).wait_send()
    for step in range(1, M):
        @pl.when(probe_goes(step))
        def _():
            probe_copy(step).wait_send()
    for pos in range(POS):
        for k in range(half):
            own, far_copy, _ = frame_copy(pos, k)

            @pl.when(jnp.logical_not(own))
            def _():
                far_copy.wait_send()

    @pl.when(active)
    def _():
        for step in range(1, M):
            int_copy(step).wait_send()
        for s in range(D):
            @pl.when(s % 2 == c)
            def _():
                fwd_copy(s).wait_send()
                for to_m in range(M):
                    own, far_copy, _ = owner_copy(s, to_m)

                    @pl.when(jnp.logical_not(own))
                    def _():
                        far_copy.wait_send()

            @pl.when(s % 2 != c)
            def _():
                pair_copy(s).wait_send()


def solution(mesh):
    M, N, D = mesh.shape["mode"], mesh.shape["dp"], mesh.shape["depth"]

    def body(probe, object_slices, propagator_phase, positions, measured):
        W = probe.shape[-1]
        H, WIDE = object_slices.shape[2], object_slices.shape[3]
        POS = positions.shape[0]
        assert object_slices.shape[0] == 1 and probe.shape[0] == 1
        assert H * M == W and POS <= D and WIDE == 2 * LANES and WIDE - W <= W - LANES
        half = M // 2
        CH = 3 if H % 24 == 0 else 1
        tables = [jnp.asarray(table) for table in dft_tables(W)]
        vmem = pl.BlockSpec(memory_space=pltpu.VMEM)
        hbm = pl.BlockSpec(memory_space=pltpu.HBM)
        dma = pltpu.SemaphoreType.DMA
        return pl.pallas_call(
            functools.partial(kernel, M, N, D, POS, W, H, WIDE, CH),
            out_shape=jax.ShapeDtypeStruct(object_slices.shape, F32),
            in_specs=[pl.BlockSpec(memory_space=pltpu.SMEM)] + [hbm] * 6,
            out_specs=vmem,
            scratch_shapes=[
                pltpu.VMEM((2, H, WIDE), F32),
                pltpu.VMEM((W, W), F32),
                pltpu.VMEM((W, W), F32),
                pltpu.VMEM(tables[0].shape, BF16),
                pltpu.VMEM(tables[1].shape, BF16),
                pltpu.VMEM((2, H, WIDE), F32),
                pltpu.VMEM((2, W, W), F32),
                pltpu.VMEM((POS, 3, H, LANES), F32),
                pltpu.VMEM((D, 3, W, LANES), F32),
                pltpu.VMEM((D, 2 * W, WIDE), F32),
                pltpu.VMEM((W, WIDE), F32),
                pltpu.VMEM((W, WIDE), F32),
                pltpu.VMEM((M, W, WIDE), F32),
                pltpu.VMEM((2 * W, WIDE), F32),
                pltpu.VMEM((2 * W, WIDE), F32),
                pltpu.VMEM((D, 3, W, LANES), F32),
                pltpu.VMEM((D, 3, W, LANES), F32),
                pltpu.VMEM((POS * half, 3, H, LANES), F32),
                pltpu.VMEM((2, H, WIDE), F32),
                pltpu.VMEM((2, H, WIDE), F32),
                dma((5,)), dma((CH,)), dma((CH,)),
                dma((M - 1,)), dma,
                dma((POS, half)), dma((D, M)),
                dma((D,)), dma((D,)),
                dma((M - 1,)), dma((M - 1,)),
                dma((D,)), dma((D,)),
                dma((D, M)), dma((POS * half,)),
                dma, dma,
            ],
            compiler_params=pltpu.CompilerParams(
                collective_id=0, has_side_effects=True, vmem_limit_bytes=48 * 1024 * 1024
            ),
        )(positions, probe, object_slices, propagator_phase, measured, *tables)

    placed = (
        P("mode", None, None, None),
        P("depth", None, ("dp", "mode"), None),
        P(),
        P("dp", None),
        P("dp", None, None),
    )
    return jax.shard_map(
        body,
        mesh=mesh,
        in_specs=placed,
        out_specs=P("depth", None, ("dp", "mode"), None),
        check_vma=False,
    )
```

```python
import functools
import math

import jax
import jax.numpy as jnp
import ml_dtypes
import numpy as np
from jax import lax
from jax.experimental import pallas as pl
from jax.experimental.pallas import tpu as pltpu
from jax.sharding import PartitionSpec as P

MESH = pl.DeviceIdType.MESH
LANES = 128
F32 = jnp.float32
BF16 = jnp.bfloat16


def dft_tables(width):
    mid = width // 2
    rows, columns = [], []
    for parity in (0, 1):
        angles = np.outer(2 * np.arange(mid) + parity, np.arange(mid)) % width
        turn = np.exp(-2j * math.pi * angles / width) / math.sqrt(width)
        real = np.block([[turn.real, -turn.imag], [turn.imag, turn.real]])
        wide = np.zeros((2 * LANES, 2 * LANES))
        for a in range(2):
            for b in range(2):
                wide[a * LANES : a * LANES + mid, b * LANES : b * LANES + mid] = real[
                    b * mid : (b + 1) * mid, a * mid : (a + 1) * mid
                ].T
        rows.append(real)
        columns.append(wide)
    stacks = []
    for axis, pair in ((1, rows), (0, columns)):
        listed = []
        for table in pair + [one.T for one in pair]:
            head = table.astype(np.float32).astype(ml_dtypes.bfloat16)
            rest = (table - head.astype(np.float64)).astype(np.float32)
            rest = rest.astype(ml_dtypes.bfloat16)
            listed.append(np.concatenate([head, head, rest], axis=axis))
        stacks.append(np.stack(listed))
    return stacks


def split(value):
    head = value.astype(BF16)
    return head, (value - head.astype(F32)).astype(BF16)


def mm(a, b):
    return jnp.dot(a, b, preferred_element_type=F32)


def kernel(
    M, N, D, POS, W, H, WIDE, CH,
    pos_ref, probe_ref, obj_ref, phase_ref, meas_ref,
    row_hbm, col_hbm,
    out_ref,
    tile, phase, meas, row_t, col_t,
    rim, probe_in, fr, win, psi, kr, ki, inten, far, up, kept, gs, pg, og, rg_out, rg_in,
    load, rim_s, rim_r, prb_s, prb_r, fr_s, win_r, fwd_s, fwd_r, int_s, int_r,
    pg_s, pg_r, og_s, og_r, rg_s, rg_r,
):
    m = lax.axis_index("mode")
    g = lax.axis_index("dp")
    d = lax.axis_index("depth")
    c = d % 2
    half = M // 2
    u = (d // 2) * M + m
    p = u % D
    mu = 2 * (u // D) + c
    active = p < POS
    partner = (m, g, d + 1 - 2 * c)
    tail = W - LANES
    mid = W // 2
    HC = H // CH
    before = (m, (g + N - 1) % N, d)
    after = (m, (g + 1) % N, d)

    def handler(pos, mode):
        at = D * (mode // 2) + pos
        return at % M, 2 * (at // M) + mode % 2

    def remote(src, dst, s_sem, r_sem, device):
        return pltpu.make_async_remote_copy(
            src_ref=src, dst_ref=dst, send_sem=s_sem, recv_sem=r_sem,
            device_id=device, device_id_type=MESH,
        )

    def arrived(ref, sem):
        pltpu.make_async_copy(ref, ref, sem).wait()

    loads = [
        pltpu.make_async_copy(src, dst, load.at[at])
        for at, (src, dst) in enumerate(
            ((phase_ref, phase), (obj_ref.at[0], tile), (row_hbm, row_t), (col_hbm, col_t))
        )
    ]
    for one in loads:
        one.start()
    meas_load = pltpu.make_async_copy(meas_ref.at[jnp.minimum(p, POS - 1)], meas, load.at[4])
    meas_load.start()
    own_probe = pltpu.make_async_copy(probe_ref.at[0], probe_in, prb_r)

    @pl.when(active & (mu == m))
    def _():
        own_probe.start()

    barrier = pltpu.get_barrier_semaphore()
    me = d * M + m
    for step in range(1, M * D):
        other = (me + step) % (M * D)
        pl.semaphore_signal(
            barrier, inc=1, device_id=(other % M, g, other // M), device_id_type=MESH
        )
    for device in (before, after):
        pl.semaphore_signal(barrier, inc=1, device_id=device, device_id_type=MESH)
    pl.semaphore_wait(barrier, M * D + 1)

    def rim_copy(ch):
        rows = pl.ds(ch * HC, HC)
        return remote(
            obj_ref.at[0, :, rows, :], rim.at[:, rows, :], rim_s.at[ch], rim_r.at[ch], before
        )

    for ch in range(CH):
        rim_copy(ch).start()

    def probe_needed(mode_at):
        return 2 * (((d // 2) * M + mode_at) // D) + c

    def probe_copy(step):
        return remote(
            probe_ref.at[0], probe_in, prb_s.at[step - 1], prb_r, ((m + step) % M, g, d)
        )

    def probe_goes(step):
        target = (m + step) % M
        return (probe_needed(target) == m) & (((d // 2) * M + target) % D < POS)

    for step in range(1, M):
        @pl.when(probe_goes(step))
        def _():
            probe_copy(step).start()

    lane = lax.broadcasted_iota(jnp.int32, (1, LANES), 1)
    low = lane < tail

    def pack(re, im, put):
        put(0, re[:, :LANES])
        put(1, im[:, :LANES])
        put(2, jnp.where(low, re[:, LANES:], pltpu.roll(im[:, LANES:], tail, 1)))

    def unpack(a, b, t):
        re_tail = jnp.where(low, t, 0.0)
        im_tail = jnp.where(low, pltpu.roll(t, LANES - tail, 1), 0.0)
        return (
            jnp.concatenate([a, re_tail], axis=1),
            jnp.concatenate([b, im_tail], axis=1),
        )

    def thirds(x):
        first = x.astype(BF16)
        x = x - first.astype(F32)
        second = x.astype(BF16)
        return first, second, (x - second.astype(F32)).astype(BF16)

    def hot(mask):
        return jnp.where(mask, 1.0, 0.0).astype(BF16)

    def moved(x, rows_hot, cols_hot):
        a0, a1, a2 = thirds(x)
        x = mm(a0, cols_hot) + (mm(a1, cols_hot) + mm(a2, cols_hot))
        a0, a1, a2 = thirds(x)
        return mm(rows_hot, a0) + (mm(rows_hot, a1) + mm(rows_hot, a2))

    def wide_iota(axis):
        return lax.broadcasted_iota(jnp.int32, (W, WIDE), axis)

    def square_iota(axis):
        return lax.broadcasted_iota(jnp.int32, (W, W), axis)

    block_lane = wide_iota(1)
    in_second = block_lane >= LANES
    at_lane = jnp.where(in_second, block_lane - LANES, block_lane)
    filled = at_lane < mid

    loads[1].wait()
    row_id = lax.broadcasted_iota(jnp.int32, (H, 1), 0) + m * H
    col_id = lax.broadcasted_iota(jnp.int32, (1, WIDE), 1)

    def frame_copy(pos, k, start=0, rows=H):
        to_m, _ = handler(pos, 2 * k)
        to_d = 2 * ((D * k + pos) // M) + c
        source = fr.at[pos, :, pl.ds(start, rows), :]
        place = win.at[d, :, pl.ds(pl.multiple_of(m * H + start, 8), rows), :]
        own = (m == to_m) & (d == to_d)
        far_copy = remote(source, place, fr_s.at[pos, k], win_r.at[d, m], (to_m, g, to_d))
        near_copy = pltpu.make_async_copy(source, place, win_r.at[d, m])
        return own, far_copy, near_copy

    for ch in range(CH):
        rim_copy(ch).wait_recv()
        rows = slice(ch * HC, (ch + 1) * HC)
        for pos in range(POS):
            row_off = pos_ref[pos, 0] - g * W
            col_off = pos_ref[pos, 1]
            parts = []
            for part in range(2):
                chosen = jnp.where(row_id[rows] >= row_off, tile[part, rows], rim[part, rows])
                wrapped = pltpu.roll(chosen, WIDE - W, 1)
                parts.append(jnp.where(col_id >= col_off, chosen, wrapped))

            def put(at, value, pos=pos, rows=rows):
                fr[pos, at, rows] = value

            pack(parts[0], parts[1], put)
            for k in range(half):
                own, far_copy, near_copy = frame_copy(pos, k, ch * HC, HC)

                @pl.when(own)
                def _():
                    near_copy.start()

                @pl.when(jnp.logical_not(own))
                def _():
                    far_copy.start()

    loads[0].wait()
    loads[2].wait()
    loads[3].wait()
    meas_load.wait()

    @pl.when(active)
    def _():
        i = square_iota(0)
        rows_hot = hot(square_iota(1) == jnp.where(i < mid, 2 * i, 2 * (i - mid) + 1))
        wanted = jnp.where(in_second, 2 * at_lane + 1, 2 * at_lane)
        cols_hot = hot((wide_iota(0) == wanted) & filled)
        turned = moved(phase[...], rows_hot, cols_hot)
        kr[...] = jnp.cos(turned)
        ki[...] = jnp.sin(turned)
        up[:W, :] = moved(meas[...], rows_hot, cols_hot)

    def by_rows(at, x):
        head, rest = split(x)
        return mm(row_t[at], jnp.concatenate([head, rest, head], axis=0))

    def by_columns(at, x):
        head, rest = split(x)
        return mm(jnp.concatenate([head, rest, head], axis=1), col_t[at])

    def dft(re, im):
        z0 = jnp.concatenate([re[:mid], im[:mid]], axis=0)
        z1 = jnp.concatenate([re[mid:], im[mid:]], axis=0)
        even, odd = by_rows(0, z0 + z1), by_rows(1, z0 - z1)
        re = jnp.concatenate([even[:mid], odd[:mid]], axis=0)
        im = jnp.concatenate([even[mid:], odd[mid:]], axis=0)
        z0 = jnp.concatenate([re[:, :LANES], im[:, :LANES]], axis=1)
        z1 = jnp.concatenate([re[:, LANES:], im[:, LANES:]], axis=1)
        even, odd = by_columns(0, z0 + z1), by_columns(1, z0 - z1)
        re = jnp.concatenate([even[:, :LANES], odd[:, :LANES]], axis=1)
        im = jnp.concatenate([even[:, LANES:], odd[:, LANES:]], axis=1)
        return re, im

    def idft(re, im):
        even = by_columns(2, jnp.concatenate([re[:, :LANES], im[:, :LANES]], axis=1))
        odd = by_columns(3, jnp.concatenate([re[:, LANES:], im[:, LANES:]], axis=1))
        z0, z1 = even + odd, even - odd
        re = jnp.concatenate([z0[:, :LANES], z1[:, :LANES]], axis=1)
        im = jnp.concatenate([z0[:, LANES:], z1[:, LANES:]], axis=1)
        even = by_rows(2, jnp.concatenate([re[:mid], im[:mid]], axis=0))
        odd = by_rows(3, jnp.concatenate([re[mid:], im[mid:]], axis=0))
        z0, z1 = even + odd, even - odd
        re = jnp.concatenate([z0[:mid], z1[:mid]], axis=0)
        im = jnp.concatenate([z0[mid:], z1[mid:]], axis=0)
        return re, im

    def mul(ar, ai, br, bi):
        return ar * br - ai * bi, ar * bi + ai * br

    def cmul(ar, ai, br, bi):
        return ar * br + ai * bi, ar * bi - ai * br

    def unpack_window(s):
        both = unpack(win[s, 0], win[s, 1], win[s, 2])
        for part, one in enumerate(both):
            shifted = pltpu.roll(one, LANES - mid, 1)
            kept[s, part, :, :LANES] = one[:, :LANES]
            kept[s, part, :, LANES:] = shifted[:, LANES:]

    def window(s):
        return kept[s, 0], kept[s, 1]

    def fwd_copy(s):
        return remote(win.at[s], win.at[s], fwd_s.at[s], fwd_r.at[s], partner)

    def int_copy(step):
        to_m, to_d = handler(p, (mu + step) % M)
        return remote(
            inten.at[0], inten.at[step], int_s.at[step - 1], int_r.at[step - 1], (to_m, g, to_d)
        )

    def pair_copy(s, to_m, ch):
        rows = pl.ds(to_m * H + ch * HC, HC)
        return remote(
            gs.at[s, :, rows, :], pg.at[s, :, rows, :], pg_s.at[s], pg_r.at[s, to_m, ch], partner
        )

    slot = p * half + mu // 2

    def owner_copy(s, to_m, start=0, rows=H, ch=0):
        source = gs.at[s, :, pl.ds(to_m * H + start, rows), :]
        place = og.at[slot, :, pl.ds(start, rows), :]
        own = (m == to_m) & (d == s)
        far_copy = remote(source, place, og_s.at[s, to_m], og_r.at[slot, ch], (to_m, g, s))
        near_copy = pltpu.make_async_copy(source, place, og_r.at[slot, ch])
        return own, far_copy, near_copy

    def send_gradient(s, re, im):
        def put(at, value):
            gs[s, at] = value

        back = WIDE - (LANES - mid)
        re = jnp.where(col_id < mid, re, pltpu.roll(re, back, 1))
        im = jnp.where(col_id < mid, im, pltpu.roll(im, back, 1))
        pack(re, im, put)

        @pl.when(s % 2 != c)
        def _():
            for to_m in range(M):
                for ch in range(CH):
                    pair_copy(s, to_m, ch).start()

    def finish_gradient(s):
        @pl.when(s % 2 == c)
        def _():
            for to_m in range(M):
                for ch in range(CH):
                    rows = pl.ds(to_m * H + ch * HC, HC)
                    arrived(pg.at[s, :, rows, :], pg_r.at[s, to_m, ch])
                    gs[s, :, rows, :] = gs[s, :, rows, :] + pg[s, :, rows, :]
                    own, far_copy, near_copy = owner_copy(s, to_m, ch * HC, HC, ch)

                    @pl.when(own)
                    def _():
                        near_copy.start()

                    @pl.when(jnp.logical_not(own))
                    def _():
                        far_copy.start()

    @pl.when(active)
    def _():
        arrived(probe_in, prb_r)
        row_off = pos_ref[p, 0] - g * W
        col_off = pos_ref[p, 1]
        i = square_iota(0) - row_off
        j = square_iota(1)
        rows_hot = hot((i == j) | (i + W == j))
        b = jnp.where(in_second, at_lane + mid, at_lane) - col_off
        j = wide_iota(0)
        cols_hot = hot(((b == j) | (b + W == j)) & filled)
        for part in range(2):
            psi[0, part * W : (part + 1) * W, :] = moved(probe_in[part], rows_hot, cols_hot)

        def pass_on(at):
            s = 2 * at + c
            for from_m in range(M):
                arrived(win.at[s, :, pl.ds(from_m * H, H), :], win_r.at[s, from_m])
            fwd_copy(s).start()

        pass_on(0)

        def await_window(s):
            @pl.when(s % 2 != c)
            def _():
                arrived(win.at[s], fwd_r.at[s])

        def forward(s, carry):
            await_window(s)
            unpack_window(s)
            wr, wi = window(s)
            fr_, fi_ = dft(*mul(psi[s, :W, :], psi[s, W:, :], wr, wi))
            nr, ni = idft(*mul(kr[...], ki[...], fr_, fi_))
            psi[s + 1, :W, :] = nr
            psi[s + 1, W:, :] = ni

            @pl.when((s % 2 == 0) & (s + 2 < D))
            def _():
                pass_on(s // 2 + 1)

            return carry

        lax.fori_loop(0, D - 1, forward, 0)
        last = D - 1
        await_window(last)
        unpack_window(last)
        wr, wi = window(last)
        fr_, fi_ = dft(*mul(psi[last, :W, :], psi[last, W:, :], wr, wi))
        fr_, fi_ = mul(kr[...], ki[...], fr_, fi_)
        far[:W, :] = fr_
        far[W:, :] = fi_
        inten[0] = fr_ * fr_ + fi_ * fi_
        for step in range(1, M):
            int_copy(step).start()
        for step in range(1, M):
            arrived(inten.at[step], int_r.at[step - 1])
        total = inten[0]
        for step in range(1, M):
            total = total + inten[step]
        far_r, far_i = far[:W, :], far[W:, :]
        weight = 2.0 * (total - up[:W, :])
        inc_r, inc_i = idft(*cmul(kr[...], ki[...], weight * far_r, weight * far_i))
        send_gradient(last, *cmul(psi[last, :W, :], psi[last, W:, :], inc_r, inc_i))
        up_r, up_i = cmul(wr, wi, inc_r, inc_i)
        up[:W, :] = up_r
        up[W:, :] = up_i

        def backward(at, carry):
            s = D - 2 - at
            gr, gi = dft(up[:W, :], up[W:, :])
            inc_r, inc_i = idft(*cmul(kr[...], ki[...], gr, gi))
            send_gradient(s, *cmul(psi[s, :W, :], psi[s, W:, :], inc_r, inc_i))
            finish_gradient(s + 1)
            wr, wi = window(s)
            up_r, up_i = cmul(wr, wi, inc_r, inc_i)
            up[:W, :] = up_r
            up[W:, :] = up_i
            return carry

        lax.fori_loop(0, D - 1, backward, 0)
        finish_gradient(jnp.int32(0))

    def rg_copy(ch):
        rows = pl.ds(ch * HC, HC)
        return remote(
            rg_out.at[:, rows, :], rg_in.at[:, rows, :], rg_s.at[ch], rg_r.at[ch], after
        )

    for ch in range(CH):
        rows = slice(ch * HC, (ch + 1) * HC)
        kept_here = [jnp.zeros((HC, WIDE), F32) for _ in range(2)]
        passed = [jnp.zeros((HC, WIDE), F32) for _ in range(2)]
        for pos in range(POS):
            row_off = pos_ref[pos, 0] - g * W
            col_off = pos_ref[pos, 1]
            for k in range(half):
                at = pos * half + k
                arrived(og.at[at, :, pl.ds(ch * HC, HC), :], og_r.at[at, ch])
            parts = [og[pos * half, at, rows] for at in range(3)]
            for k in range(1, half):
                parts = [parts[at] + og[pos * half + k, at, rows] for at in range(3)]
            both = unpack(*parts)
            for part in range(2):
                inside = jnp.where(col_id >= col_off, both[part], 0.0)
                outside = jnp.where(col_id < col_off, both[part], 0.0)
                placed = inside + pltpu.roll(outside, W, 1)
                own_rows = row_id[rows] >= row_off
                kept_here[part] += jnp.where(own_rows, placed, 0.0)
                passed[part] += jnp.where(own_rows, 0.0, placed)
        for part in range(2):
            rg_out[part, rows] = passed[part]
        rg_copy(ch).start()
        for part in range(2):
            out_ref[0, part, rows] = kept_here[part]
    for ch in range(CH):
        rows = slice(ch * HC, (ch + 1) * HC)
        rg_copy(ch).wait_recv()
        for part in range(2):
            out_ref[0, part, rows] += rg_in[part, rows]

    for ch in range(CH):
        rg_copy(ch).wait_send()
        rim_copy(ch).wait_send()
    for step in range(1, M):
        @pl.when(probe_goes(step))
        def _():
            probe_copy(step).wait_send()
    for pos in range(POS):
        for k in range(half):
            own, far_copy, _ = frame_copy(pos, k)

            @pl.when(jnp.logical_not(own))
            def _():
                far_copy.wait_send()

    @pl.when(active)
    def _():
        for step in range(1, M):
            int_copy(step).wait_send()
        for s in range(D):
            @pl.when(s % 2 == c)
            def _():
                fwd_copy(s).wait_send()
                for to_m in range(M):
                    own, far_copy, _ = owner_copy(s, to_m)

                    @pl.when(jnp.logical_not(own))
                    def _():
                        far_copy.wait_send()

            @pl.when(s % 2 != c)
            def _():
                whole = remote(gs.at[s], pg.at[s], pg_s.at[s], pg_r.at[s, 0, 0], partner)
                whole.wait_send()


def solution(mesh):
    M, N, D = mesh.shape["mode"], mesh.shape["dp"], mesh.shape["depth"]

    def body(probe, object_slices, propagator_phase, positions, measured):
        W = probe.shape[-1]
        H, WIDE = object_slices.shape[2], object_slices.shape[3]
        POS = positions.shape[0]
        assert object_slices.shape[0] == 1 and probe.shape[0] == 1
        assert H * M == W and POS <= D and WIDE == 2 * LANES and WIDE - W <= W - LANES
        half = M // 2
        CH = 3 if H % 24 == 0 else 1
        tables = [jnp.asarray(table) for table in dft_tables(W)]
        vmem = pl.BlockSpec(memory_space=pltpu.VMEM)
        hbm = pl.BlockSpec(memory_space=pltpu.HBM)
        dma = pltpu.SemaphoreType.DMA
        return pl.pallas_call(
            functools.partial(kernel, M, N, D, POS, W, H, WIDE, CH),
            out_shape=jax.ShapeDtypeStruct(object_slices.shape, F32),
            in_specs=[pl.BlockSpec(memory_space=pltpu.SMEM)] + [hbm] * 6,
            out_specs=vmem,
            scratch_shapes=[
                pltpu.VMEM((2, H, WIDE), F32),
                pltpu.VMEM((W, W), F32),
                pltpu.VMEM((W, W), F32),
                pltpu.VMEM(tables[0].shape, BF16),
                pltpu.VMEM(tables[1].shape, BF16),
                pltpu.VMEM((2, H, WIDE), F32),
                pltpu.VMEM((2, W, W), F32),
                pltpu.VMEM((POS, 3, H, LANES), F32),
                pltpu.VMEM((D, 3, W, LANES), F32),
                pltpu.VMEM((D, 2 * W, WIDE), F32),
                pltpu.VMEM((W, WIDE), F32),
                pltpu.VMEM((W, WIDE), F32),
                pltpu.VMEM((M, W, WIDE), F32),
                pltpu.VMEM((2 * W, WIDE), F32),
                pltpu.VMEM((2 * W, WIDE), F32),
                pltpu.VMEM((D, 2, W, WIDE), F32),
                pltpu.VMEM((D, 3, W, LANES), F32),
                pltpu.VMEM((D, 3, W, LANES), F32),
                pltpu.VMEM((POS * half, 3, H, LANES), F32),
                pltpu.VMEM((2, H, WIDE), F32),
                pltpu.VMEM((2, H, WIDE), F32),
                dma((5,)), dma((CH,)), dma((CH,)),
                dma((M - 1,)), dma,
                dma((POS, half)), dma((D, M)),
                dma((D,)), dma((D,)),
                dma((M - 1,)), dma((M - 1,)),
                dma((D,)), dma((D, M, CH)),
                dma((D, M)), dma((POS * half, CH)),
                dma((CH,)), dma((CH,)),
            ],
            compiler_params=pltpu.CompilerParams(
                collective_id=0, has_side_effects=True, vmem_limit_bytes=63 * 1024 * 1024
            ),
        )(positions, probe, object_slices, propagator_phase, measured, *tables)

    placed = (
        P("mode", None, None, None),
        P("depth", None, ("dp", "mode"), None),
        P(),
        P("dp", None),
        P("dp", None, None),
    )
    return jax.shard_map(
        body,
        mesh=mesh,
        in_specs=placed,
        out_specs=P("depth", None, ("dp", "mode"), None),
        check_vma=False,
    )
```

```python
import functools
import math

import jax
import jax.numpy as jnp
import ml_dtypes
import numpy as np
from jax import lax
from jax.experimental import pallas as pl
from jax.experimental.pallas import tpu as pltpu
from jax.sharding import PartitionSpec as P

MESH = pl.DeviceIdType.MESH
LANES = 128
F32 = jnp.float32
BF16 = jnp.bfloat16


def dft_tables(width):
    mid = width // 2
    rows, columns = [], []
    for parity in (0, 1):
        angles = np.outer(2 * np.arange(mid) + parity, np.arange(mid)) % width
        turn = np.exp(-2j * math.pi * angles / width) / math.sqrt(width)
        real = np.block([[turn.real, -turn.imag], [turn.imag, turn.real]])
        wide = np.zeros((2 * LANES, 2 * LANES))
        for a in range(2):
            for b in range(2):
                wide[a * LANES : a * LANES + mid, b * LANES : b * LANES + mid] = real[
                    b * mid : (b + 1) * mid, a * mid : (a + 1) * mid
                ].T
        rows.append(real)
        columns.append(wide)
    stacks = []
    for axis, pair in ((1, rows), (0, columns)):
        listed = []
        for table in pair + [one.T for one in pair]:
            head = table.astype(np.float32).astype(ml_dtypes.bfloat16)
            rest = (table - head.astype(np.float64)).astype(np.float32)
            rest = rest.astype(ml_dtypes.bfloat16)
            listed.append(np.concatenate([head, head, rest], axis=axis))
        stacks.append(np.stack(listed))
    return stacks


def split(value):
    head = value.astype(BF16)
    return head, (value - head.astype(F32)).astype(BF16)


def mm(a, b):
    return jnp.dot(a, b, preferred_element_type=F32)


def kernel(
    M, N, D, POS, W, H, WIDE, CH,
    pos_ref, probe_ref, obj_ref, phase_ref, meas_ref,
    row_hbm, col_hbm,
    out_ref,
    tile, phase, meas, row_t, col_t,
    rim, probe_in, fr, win, psi, kr, ki, inten, far, up, kept, gs, pg, og, rg_out, rg_in,
    load, rim_s, rim_r, prb_s, prb_r, fr_s, win_r, fwd_s, fwd_r, int_s, int_r,
    pg_s, pg_r, og_s, og_r, rg_s, rg_r,
):
    m = lax.axis_index("mode")
    g = lax.axis_index("dp")
    d = lax.axis_index("depth")
    c = d % 2
    half = M // 2
    u = (d // 2) * M + m
    p = u % D
    mu = 2 * (u // D) + c
    active = p < POS
    partner = (m, g, d + 1 - 2 * c)
    tail = W - LANES
    mid = W // 2
    HC = H // CH
    before = (m, (g + N - 1) % N, d)
    after = (m, (g + 1) % N, d)

    def handler(pos, mode):
        at = D * (mode // 2) + pos
        return at % M, 2 * (at // M) + mode % 2

    def remote(src, dst, s_sem, r_sem, device):
        return pltpu.make_async_remote_copy(
            src_ref=src, dst_ref=dst, send_sem=s_sem, recv_sem=r_sem,
            device_id=device, device_id_type=MESH,
        )

    def arrived(ref, sem):
        pltpu.make_async_copy(ref, ref, sem).wait()

    loads = [
        pltpu.make_async_copy(src, dst, load.at[at])
        for at, (src, dst) in enumerate(
            ((phase_ref, phase), (obj_ref.at[0], tile), (row_hbm, row_t), (col_hbm, col_t))
        )
    ]
    for one in loads:
        one.start()
    meas_load = pltpu.make_async_copy(meas_ref.at[jnp.minimum(p, POS - 1)], meas, load.at[4])
    meas_load.start()
    own_probe = pltpu.make_async_copy(probe_ref.at[0], probe_in, prb_r)

    @pl.when(active & (mu == m))
    def _():
        own_probe.start()

    barrier = pltpu.get_barrier_semaphore()
    me = d * M + m
    for step in range(1, M * D):
        other = (me + step) % (M * D)
        pl.semaphore_signal(
            barrier, inc=1, device_id=(other % M, g, other // M), device_id_type=MESH
        )
    for device in (before, after):
        pl.semaphore_signal(barrier, inc=1, device_id=device, device_id_type=MESH)
    pl.semaphore_wait(barrier, M * D + 1)

    def rim_copy(ch):
        rows = pl.ds(ch * HC, HC)
        return remote(
            obj_ref.at[0, :, rows, :], rim.at[:, rows, :], rim_s.at[ch], rim_r.at[ch], before
        )

    for ch in range(CH):
        rim_copy(ch).start()

    def probe_needed(mode_at):
        return 2 * (((d // 2) * M + mode_at) // D) + c

    def probe_copy(step):
        return remote(
            probe_ref.at[0], probe_in, prb_s.at[step - 1], prb_r, ((m + step) % M, g, d)
        )

    def probe_goes(step):
        target = (m + step) % M
        return (probe_needed(target) == m) & (((d // 2) * M + target) % D < POS)

    for step in range(1, M):
        @pl.when(probe_goes(step))
        def _():
            probe_copy(step).start()

    lane = lax.broadcasted_iota(jnp.int32, (1, LANES), 1)
    low = lane < tail

    def pack(re, im, put):
        put(0, re[:, :LANES])
        put(1, im[:, :LANES])
        put(2, jnp.where(low, re[:, LANES:], pltpu.roll(im[:, LANES:], tail, 1)))

    def unpack(a, b, t):
        re_tail = jnp.where(low, t, 0.0)
        im_tail = jnp.where(low, pltpu.roll(t, LANES - tail, 1), 0.0)
        return (
            jnp.concatenate([a, re_tail], axis=1),
            jnp.concatenate([b, im_tail], axis=1),
        )

    def thirds(x):
        first = x.astype(BF16)
        x = x - first.astype(F32)
        second = x.astype(BF16)
        return first, second, (x - second.astype(F32)).astype(BF16)

    def hot(mask):
        return jnp.where(mask, 1.0, 0.0).astype(BF16)

    def moved(x, rows_hot, cols_hot):
        a0, a1, a2 = thirds(x)
        x = mm(a0, cols_hot) + (mm(a1, cols_hot) + mm(a2, cols_hot))
        a0, a1, a2 = thirds(x)
        return mm(rows_hot, a0) + (mm(rows_hot, a1) + mm(rows_hot, a2))

    def wide_iota(axis):
        return lax.broadcasted_iota(jnp.int32, (W, WIDE), axis)

    def square_iota(axis):
        return lax.broadcasted_iota(jnp.int32, (W, W), axis)

    block_lane = wide_iota(1)
    in_second = block_lane >= LANES
    at_lane = jnp.where(in_second, block_lane - LANES, block_lane)
    filled = at_lane < mid

    loads[1].wait()
    late = d >= D // 2
    row_id = lax.broadcasted_iota(jnp.int32, (H, 1), 0) + m * H
    col_id = lax.broadcasted_iota(jnp.int32, (1, WIDE), 1)

    def frame_copy(pos, k, start=0, rows=H):
        to_m, _ = handler(pos, 2 * k)
        to_d = 2 * ((D * k + pos) // M) + c
        source = fr.at[pos, :, pl.ds(start, rows), :]
        place = win.at[d, :, pl.ds(pl.multiple_of(m * H + start, 8), rows), :]
        own = (m == to_m) & (d == to_d)
        far_copy = remote(source, place, fr_s.at[pos, k], win_r.at[d, m], (to_m, g, to_d))
        near_copy = pltpu.make_async_copy(source, place, win_r.at[d, m])
        return own, far_copy, near_copy

    for ch in range(CH):
        rim_copy(ch).wait_recv()
        rows = slice(ch * HC, (ch + 1) * HC)
        for pos in range(POS):
            row_off = pos_ref[pos, 0] - g * W
            col_off = pos_ref[pos, 1]
            parts = []
            for part in range(2):
                chosen = jnp.where(row_id[rows] >= row_off, tile[part, rows], rim[part, rows])
                wrapped = pltpu.roll(chosen, WIDE - W, 1)
                parts.append(jnp.where(col_id >= col_off, chosen, wrapped))

            def put(at, value, pos=pos, rows=rows):
                fr[pos, at, rows] = value

            pack(parts[0], parts[1], put)
            for k in range(half):
                own, far_copy, near_copy = frame_copy(pos, k, ch * HC, HC)

                @pl.when(own)
                def _():
                    near_copy.start()

                @pl.when(jnp.logical_not(own | late))
                def _():
                    far_copy.start()

    loads[0].wait()
    loads[2].wait()
    loads[3].wait()
    meas_load.wait()

    i = square_iota(0)
    rows_hot = hot(square_iota(1) == jnp.where(i < mid, 2 * i, 2 * (i - mid) + 1))
    wanted = jnp.where(in_second, 2 * at_lane + 1, 2 * at_lane)
    cols_hot = hot((wide_iota(0) == wanted) & filled)
    turned = moved(phase[...], rows_hot, cols_hot)
    kr[...] = jnp.cos(turned)
    ki[...] = jnp.sin(turned)
    up[:W, :] = moved(meas[...], rows_hot, cols_hot)

    for pos in range(POS):
        for k in range(half):
            own, far_copy, _ = frame_copy(pos, k)

            @pl.when(late & jnp.logical_not(own))
            def _():
                far_copy.start()

    def by_rows(at, x):
        head, rest = split(x)
        return mm(row_t[at], jnp.concatenate([head, rest, head], axis=0))

    def by_columns(at, x):
        head, rest = split(x)
        return mm(jnp.concatenate([head, rest, head], axis=1), col_t[at])

    def dft(re, im):
        z0 = jnp.concatenate([re[:mid], im[:mid]], axis=0)
        z1 = jnp.concatenate([re[mid:], im[mid:]], axis=0)
        even, odd = by_rows(0, z0 + z1), by_rows(1, z0 - z1)
        re = jnp.concatenate([even[:mid], odd[:mid]], axis=0)
        im = jnp.concatenate([even[mid:], odd[mid:]], axis=0)
        z0 = jnp.concatenate([re[:, :LANES], im[:, :LANES]], axis=1)
        z1 = jnp.concatenate([re[:, LANES:], im[:, LANES:]], axis=1)
        even, odd = by_columns(0, z0 + z1), by_columns(1, z0 - z1)
        re = jnp.concatenate([even[:, :LANES], odd[:, :LANES]], axis=1)
        im = jnp.concatenate([even[:, LANES:], odd[:, LANES:]], axis=1)
        return re, im

    def idft(re, im):
        even = by_columns(2, jnp.concatenate([re[:, :LANES], im[:, :LANES]], axis=1))
        odd = by_columns(3, jnp.concatenate([re[:, LANES:], im[:, LANES:]], axis=1))
        z0, z1 = even + odd, even - odd
        re = jnp.concatenate([z0[:, :LANES], z1[:, :LANES]], axis=1)
        im = jnp.concatenate([z0[:, LANES:], z1[:, LANES:]], axis=1)
        even = by_rows(2, jnp.concatenate([re[:mid], im[:mid]], axis=0))
        odd = by_rows(3, jnp.concatenate([re[mid:], im[mid:]], axis=0))
        z0, z1 = even + odd, even - odd
        re = jnp.concatenate([z0[:mid], z1[:mid]], axis=0)
        im = jnp.concatenate([z0[mid:], z1[mid:]], axis=0)
        return re, im

    def mul(ar, ai, br, bi):
        return ar * br - ai * bi, ar * bi + ai * br

    def cmul(ar, ai, br, bi):
        return ar * br + ai * bi, ar * bi - ai * br

    def unpack_window(s):
        both = unpack(win[s, 0], win[s, 1], win[s, 2])
        for part, one in enumerate(both):
            shifted = pltpu.roll(one, LANES - mid, 1)
            kept[s, part, :, :LANES] = one[:, :LANES]
            kept[s, part, :, LANES:] = shifted[:, LANES:]

    def window(s):
        return kept[s, 0], kept[s, 1]

    def fwd_copy(s):
        return remote(win.at[s], win.at[s], fwd_s.at[s], fwd_r.at[s], partner)

    def int_copy(step):
        to_m, to_d = handler(p, (mu + step) % M)
        return remote(
            inten.at[0], inten.at[step], int_s.at[step - 1], int_r.at[step - 1], (to_m, g, to_d)
        )

    def pair_copy(s, to_m, ch):
        rows = pl.ds(to_m * H + ch * HC, HC)
        return remote(
            gs.at[s, :, rows, :], pg.at[s, :, rows, :], pg_s.at[s], pg_r.at[s, to_m, ch], partner
        )

    slot = p * half + mu // 2

    def owner_copy(s, to_m, start=0, rows=H, ch=0):
        source = gs.at[s, :, pl.ds(to_m * H + start, rows), :]
        place = og.at[slot, :, pl.ds(start, rows), :]
        own = (m == to_m) & (d == s)
        far_copy = remote(source, place, og_s.at[s, to_m], og_r.at[slot, ch], (to_m, g, s))
        near_copy = pltpu.make_async_copy(source, place, og_r.at[slot, ch])
        return own, far_copy, near_copy

    def send_gradient(s, re, im):
        def put(at, value):
            gs[s, at] = value

        back = WIDE - (LANES - mid)
        re = jnp.where(col_id < mid, re, pltpu.roll(re, back, 1))
        im = jnp.where(col_id < mid, im, pltpu.roll(im, back, 1))
        pack(re, im, put)

        @pl.when(s % 2 != c)
        def _():
            for to_m in range(M):
                for ch in range(CH):
                    pair_copy(s, to_m, ch).start()

    def finish_gradient(s):
        @pl.when(s % 2 == c)
        def _():
            for to_m in range(M):
                for ch in range(CH):
                    rows = pl.ds(to_m * H + ch * HC, HC)
                    arrived(pg.at[s, :, rows, :], pg_r.at[s, to_m, ch])
                    gs[s, :, rows, :] = gs[s, :, rows, :] + pg[s, :, rows, :]
                    own, far_copy, near_copy = owner_copy(s, to_m, ch * HC, HC, ch)

                    @pl.when(own)
                    def _():
                        near_copy.start()

                    @pl.when(jnp.logical_not(own))
                    def _():
                        far_copy.start()

    @pl.when(active)
    def _():
        arrived(probe_in, prb_r)
        row_off = pos_ref[p, 0] - g * W
        col_off = pos_ref[p, 1]
        i = square_iota(0) - row_off
        j = square_iota(1)
        rows_hot = hot((i == j) | (i + W == j))
        b = jnp.where(in_second, at_lane + mid, at_lane) - col_off
        j = wide_iota(0)
        cols_hot = hot(((b == j) | (b + W == j)) & filled)
        for part in range(2):
            psi[0, part * W : (part + 1) * W, :] = moved(probe_in[part], rows_hot, cols_hot)

        def pass_on(at):
            s = 2 * at + c
            for from_m in range(M):
                arrived(win.at[s, :, pl.ds(from_m * H, H), :], win_r.at[s, from_m])
            fwd_copy(s).start()

        pass_on(0)

        def await_window(s):
            @pl.when(s % 2 != c)
            def _():
                arrived(win.at[s], fwd_r.at[s])

        def forward(s, carry):
            await_window(s)
            unpack_window(s)
            wr, wi = window(s)
            fr_, fi_ = dft(*mul(psi[s, :W, :], psi[s, W:, :], wr, wi))
            nr, ni = idft(*mul(kr[...], ki[...], fr_, fi_))
            psi[s + 1, :W, :] = nr
            psi[s + 1, W:, :] = ni

            @pl.when((s % 2 == 0) & (s + 2 < D))
            def _():
                pass_on(s // 2 + 1)

            return carry

        lax.fori_loop(0, D - 1, forward, 0)
        last = D - 1
        await_window(last)
        unpack_window(last)
        wr, wi = window(last)
        fr_, fi_ = dft(*mul(psi[last, :W, :], psi[last, W:, :], wr, wi))
        fr_, fi_ = mul(kr[...], ki[...], fr_, fi_)
        far[:W, :] = fr_
        far[W:, :] = fi_
        inten[0] = fr_ * fr_ + fi_ * fi_
        for step in range(1, M):
            int_copy(step).start()
        for step in range(1, M):
            arrived(inten.at[step], int_r.at[step - 1])
        total = inten[0]
        for step in range(1, M):
            total = total + inten[step]
        far_r, far_i = far[:W, :], far[W:, :]
        weight = 2.0 * (total - up[:W, :])
        inc_r, inc_i = idft(*cmul(kr[...], ki[...], weight * far_r, weight * far_i))
        send_gradient(last, *cmul(psi[last, :W, :], psi[last, W:, :], inc_r, inc_i))
        up_r, up_i = cmul(wr, wi, inc_r, inc_i)
        up[:W, :] = up_r
        up[W:, :] = up_i

        def backward(at, carry):
            s = D - 2 - at
            gr, gi = dft(up[:W, :], up[W:, :])
            inc_r, inc_i = idft(*cmul(kr[...], ki[...], gr, gi))
            send_gradient(s, *cmul(psi[s, :W, :], psi[s, W:, :], inc_r, inc_i))
            finish_gradient(s + 1)
            wr, wi = window(s)
            up_r, up_i = cmul(wr, wi, inc_r, inc_i)
            up[:W, :] = up_r
            up[W:, :] = up_i
            return carry

        lax.fori_loop(0, D - 1, backward, 0)
        finish_gradient(jnp.int32(0))

    def rg_copy(ch):
        rows = pl.ds(ch * HC, HC)
        return remote(
            rg_out.at[:, rows, :], rg_in.at[:, rows, :], rg_s.at[ch], rg_r.at[ch], after
        )

    for ch in range(CH):
        rows = slice(ch * HC, (ch + 1) * HC)
        kept_here = [jnp.zeros((HC, WIDE), F32) for _ in range(2)]
        passed = [jnp.zeros((HC, WIDE), F32) for _ in range(2)]
        for pos in range(POS):
            row_off = pos_ref[pos, 0] - g * W
            col_off = pos_ref[pos, 1]
            for k in range(half):
                at = pos * half + k
                arrived(og.at[at, :, pl.ds(ch * HC, HC), :], og_r.at[at, ch])
            parts = [og[pos * half, at, rows] for at in range(3)]
            for k in range(1, half):
                parts = [parts[at] + og[pos * half + k, at, rows] for at in range(3)]
            both = unpack(*parts)
            for part in range(2):
                inside = jnp.where(col_id >= col_off, both[part], 0.0)
                outside = jnp.where(col_id < col_off, both[part], 0.0)
                placed = inside + pltpu.roll(outside, W, 1)
                own_rows = row_id[rows] >= row_off
                kept_here[part] += jnp.where(own_rows, placed, 0.0)
                passed[part] += jnp.where(own_rows, 0.0, placed)
        for part in range(2):
            rg_out[part, rows] = passed[part]
        rg_copy(ch).start()
        for part in range(2):
            out_ref[0, part, rows] = kept_here[part]
    for ch in range(CH):
        rows = slice(ch * HC, (ch + 1) * HC)
        rg_copy(ch).wait_recv()
        for part in range(2):
            out_ref[0, part, rows] += rg_in[part, rows]

    for ch in range(CH):
        rg_copy(ch).wait_send()
        rim_copy(ch).wait_send()
    for step in range(1, M):
        @pl.when(probe_goes(step))
        def _():
            probe_copy(step).wait_send()
    for pos in range(POS):
        for k in range(half):
            own, far_copy, _ = frame_copy(pos, k)

            @pl.when(jnp.logical_not(own))
            def _():
                far_copy.wait_send()

    @pl.when(active)
    def _():
        for step in range(1, M):
            int_copy(step).wait_send()
        for s in range(D):
            @pl.when(s % 2 == c)
            def _():
                fwd_copy(s).wait_send()
                for to_m in range(M):
                    own, far_copy, _ = owner_copy(s, to_m)

                    @pl.when(jnp.logical_not(own))
                    def _():
                        far_copy.wait_send()

            @pl.when(s % 2 != c)
            def _():
                whole = remote(gs.at[s], pg.at[s], pg_s.at[s], pg_r.at[s, 0, 0], partner)
                whole.wait_send()


def solution(mesh):
    M, N, D = mesh.shape["mode"], mesh.shape["dp"], mesh.shape["depth"]

    def body(probe, object_slices, propagator_phase, positions, measured):
        W = probe.shape[-1]
        H, WIDE = object_slices.shape[2], object_slices.shape[3]
        POS = positions.shape[0]
        assert object_slices.shape[0] == 1 and probe.shape[0] == 1
        assert H * M == W and POS <= D and WIDE == 2 * LANES and WIDE - W <= W - LANES
        half = M // 2
        CH = 3 if H % 24 == 0 else 1
        tables = [jnp.asarray(table) for table in dft_tables(W)]
        vmem = pl.BlockSpec(memory_space=pltpu.VMEM)
        hbm = pl.BlockSpec(memory_space=pltpu.HBM)
        dma = pltpu.SemaphoreType.DMA
        return pl.pallas_call(
            functools.partial(kernel, M, N, D, POS, W, H, WIDE, CH),
            out_shape=jax.ShapeDtypeStruct(object_slices.shape, F32),
            in_specs=[pl.BlockSpec(memory_space=pltpu.SMEM)] + [hbm] * 6,
            out_specs=vmem,
            scratch_shapes=[
                pltpu.VMEM((2, H, WIDE), F32),
                pltpu.VMEM((W, W), F32),
                pltpu.VMEM((W, W), F32),
                pltpu.VMEM(tables[0].shape, BF16),
                pltpu.VMEM(tables[1].shape, BF16),
                pltpu.VMEM((2, H, WIDE), F32),
                pltpu.VMEM((2, W, W), F32),
                pltpu.VMEM((POS, 3, H, LANES), F32),
                pltpu.VMEM((D, 3, W, LANES), F32),
                pltpu.VMEM((D, 2 * W, WIDE), F32),
                pltpu.VMEM((W, WIDE), F32),
                pltpu.VMEM((W, WIDE), F32),
                pltpu.VMEM((M, W, WIDE), F32),
                pltpu.VMEM((2 * W, WIDE), F32),
                pltpu.VMEM((2 * W, WIDE), F32),
                pltpu.VMEM((D, 2, W, WIDE), F32),
                pltpu.VMEM((D, 3, W, LANES), F32),
                pltpu.VMEM((D, 3, W, LANES), F32),
                pltpu.VMEM((POS * half, 3, H, LANES), F32),
                pltpu.VMEM((2, H, WIDE), F32),
                pltpu.VMEM((2, H, WIDE), F32),
                dma((5,)), dma((CH,)), dma((CH,)),
                dma((M - 1,)), dma,
                dma((POS, half)), dma((D, M)),
                dma((D,)), dma((D,)),
                dma((M - 1,)), dma((M - 1,)),
                dma((D,)), dma((D, M, CH)),
                dma((D, M)), dma((POS * half, CH)),
                dma((CH,)), dma((CH,)),
            ],
            compiler_params=pltpu.CompilerParams(
                collective_id=0, has_side_effects=True, vmem_limit_bytes=63 * 1024 * 1024
            ),
        )(positions, probe, object_slices, propagator_phase, measured, *tables)

    placed = (
        P("mode", None, None, None),
        P("depth", None, ("dp", "mode"), None),
        P(),
        P("dp", None),
        P("dp", None, None),
    )
    return jax.shard_map(
        body,
        mesh=mesh,
        in_specs=placed,
        out_specs=P("depth", None, ("dp", "mode"), None),
        check_vma=False,
    )
```

```python
import functools
import math

import jax
import jax.numpy as jnp
import ml_dtypes
import numpy as np
from jax import lax
from jax.experimental import pallas as pl
from jax.experimental.pallas import tpu as pltpu
from jax.sharding import PartitionSpec as P

MESH = pl.DeviceIdType.MESH
LANES = 128
F32 = jnp.float32
BF16 = jnp.bfloat16


def dft_tables(width):
    third = width // 3
    rows, columns = [], []
    turns = []
    for q in range(3):
        angles = np.outer(3 * np.arange(third) + q, np.arange(third)) % width
        turns.append(np.exp(-2j * math.pi * angles / width) / math.sqrt(width))
    for turn in turns + [one.conj().T for one in turns]:
        left = np.concatenate([turn.real, turn.imag], 1)
        right = np.block([[turn.real.T, turn.imag.T], [-turn.imag.T, turn.real.T]])
        parts = []
        for table in (left, right):
            head = table.astype(np.float32).astype(ml_dtypes.bfloat16)
            rest = (table - head.astype(np.float64)).astype(np.float32)
            parts += [head, rest.astype(ml_dtypes.bfloat16)]
        rows.append(np.block([[parts[0], parts[0]], [parts[1], 0 * parts[1]]]))
        columns.append(np.block([[parts[2], parts[3]], [parts[2], 0 * parts[3]]]))
    return [np.stack(one).astype(ml_dtypes.bfloat16) for one in (rows, columns)]


def split(value):
    head = value.astype(BF16)
    return head, (value - head.astype(F32)).astype(BF16)


def mm(a, b):
    return jnp.dot(a, b, preferred_element_type=F32)


def kernel(
    M, N, D, POS, W, H, WIDE, CH,
    pos_ref, probe_ref, obj_ref, phase_ref, meas_ref,
    row_hbm, col_hbm,
    out_ref,
    tile, phase, meas, row_t, col_t,
    rim, probe_in, fr, win, psi, kern, inten, far, up, kept, gs, pg, og, rg_out, rg_in,
    load, rim_s, rim_r, prb_s, prb_r, fr_s, win_r, fwd_s, fwd_r, int_s, int_r,
    pg_s, pg_r, og_s, og_r, rg_s, rg_r,
):
    m = lax.axis_index("mode")
    g = lax.axis_index("dp")
    d = lax.axis_index("depth")
    c = d % 2
    half = M // 2
    u = (d // 2) * M + m
    p = u % D
    mu = 2 * (u // D) + c
    active = p < POS
    partner = (m, g, d + 1 - 2 * c)
    third = W // 3
    HC = H // CH
    before = (m, (g + N - 1) % N, d)
    after = (m, (g + 1) % N, d)

    def handler(pos, mode):
        at = D * (mode // 2) + pos
        return at % M, 2 * (at // M) + mode % 2

    def remote(src, dst, s_sem, r_sem, device):
        return pltpu.make_async_remote_copy(
            src_ref=src, dst_ref=dst, send_sem=s_sem, recv_sem=r_sem,
            device_id=device, device_id_type=MESH,
        )

    def arrived(ref, sem):
        pltpu.make_async_copy(ref, ref, sem).wait()

    loads = [
        pltpu.make_async_copy(src, dst, load.at[at])
        for at, (src, dst) in enumerate(
            ((phase_ref, phase), (obj_ref.at[0], tile), (row_hbm, row_t), (col_hbm, col_t))
        )
    ]
    for one in loads:
        one.start()
    meas_load = pltpu.make_async_copy(meas_ref.at[jnp.minimum(p, POS - 1)], meas, load.at[4])
    meas_load.start()
    own_probe = pltpu.make_async_copy(probe_ref.at[0], probe_in, prb_r)

    @pl.when(active & (mu == m))
    def _():
        own_probe.start()

    barrier = pltpu.get_barrier_semaphore()
    me = d * M + m
    for step in range(1, M * D):
        other = (me + step) % (M * D)
        pl.semaphore_signal(
            barrier, inc=1, device_id=(other % M, g, other // M), device_id_type=MESH
        )
    for device in (before, after):
        pl.semaphore_signal(barrier, inc=1, device_id=device, device_id_type=MESH)
    pl.semaphore_wait(barrier, M * D + 1)

    def rim_copy(ch):
        rows = pl.ds(ch * HC, HC)
        return remote(
            obj_ref.at[0, :, rows, :], rim.at[:, rows, :], rim_s.at[ch], rim_r.at[ch], before
        )

    for ch in range(CH):
        rim_copy(ch).start()

    def probe_needed(mode_at):
        return 2 * (((d // 2) * M + mode_at) // D) + c

    def probe_copy(step):
        return remote(
            probe_ref.at[0], probe_in, prb_s.at[step - 1], prb_r, ((m + step) % M, g, d)
        )

    def probe_goes(step):
        target = (m + step) % M
        return (probe_needed(target) == m) & (((d // 2) * M + target) % D < POS)

    for step in range(1, M):
        @pl.when(probe_goes(step))
        def _():
            probe_copy(step).start()

    lane = lax.broadcasted_iota(jnp.int32, (1, LANES), 1)
    low = lane < third

    sign = jnp.where(low, -1.0, 1.0)

    def swap(x):
        return pltpu.roll(x, third, 1)

    def pack(re, im):
        return [
            jnp.where(low, re[:, :LANES], swap(im[:, :LANES])),
            jnp.where(low, swap(re[:, :LANES]), im[:, :LANES]),
            jnp.where(low, re[:, LANES:], swap(im[:, LANES:])),
        ]

    def unpack(a, b, t):
        re = [jnp.where(low, a, swap(b)), jnp.where(low, t, 0.0)]
        im = [jnp.where(low, swap(a), b), jnp.where(low, swap(t), 0.0)]
        return jnp.concatenate(re, axis=1), jnp.concatenate(im, axis=1)

    def thirds(x):
        first = x.astype(BF16)
        x = x - first.astype(F32)
        second = x.astype(BF16)
        return first, second, (x - second.astype(F32)).astype(BF16)

    def hot(mask):
        return jnp.where(mask, 1.0, 0.0).astype(BF16)

    def hot_columns(x, cols_hot):
        a0, a1, a2 = thirds(x)
        return mm(a0, cols_hot) + (mm(a1, cols_hot) + mm(a2, cols_hot))

    def hot_rows(x, rows_hot):
        a0, a1, a2 = thirds(x)
        return mm(rows_hot, a0) + (mm(rows_hot, a1) + mm(rows_hot, a2))

    def wide_iota(axis):
        return lax.broadcasted_iota(jnp.int32, (W, 3 * LANES), axis)

    def square_iota(axis):
        return lax.broadcasted_iota(jnp.int32, (W, W), axis)

    block = wide_iota(1) // LANES
    at_lane = wide_iota(1) % third
    imag = (wide_iota(1) // third) % 2 == 1

    loads[1].wait()
    row_id = lax.broadcasted_iota(jnp.int32, (H, 1), 0) + m * H
    col_id = lax.broadcasted_iota(jnp.int32, (1, WIDE), 1)

    def frame_copy(pos, k, start=0, rows=H):
        to_m, _ = handler(pos, 2 * k)
        to_d = 2 * ((D * k + pos) // M) + c
        source = fr.at[pos, :, pl.ds(start, rows), :]
        place = win.at[d, :, pl.ds(pl.multiple_of(m * H + start, 8), rows), :]
        own = (m == to_m) & (d == to_d)
        far_copy = remote(source, place, fr_s.at[pos, k], win_r.at[d, m], (to_m, g, to_d))
        near_copy = pltpu.make_async_copy(source, place, win_r.at[d, m])
        return own, far_copy, near_copy

    for ch in range(CH):
        rim_copy(ch).wait_recv()
        rows = slice(ch * HC, (ch + 1) * HC)
        for pos in range(POS):
            row_off = pos_ref[pos, 0] - g * W
            col_off = pos_ref[pos, 1]
            parts = []
            for part in range(2):
                chosen = jnp.where(row_id[rows] >= row_off, tile[part, rows], rim[part, rows])
                wrapped = pltpu.roll(chosen, WIDE - W, 1)
                parts.append(jnp.where(col_id >= col_off, chosen, wrapped))

            for at, value in enumerate(pack(parts[0], parts[1])):
                fr[pos, at, rows] = value
            for k in range(half):
                own, far_copy, near_copy = frame_copy(pos, k, ch * HC, HC)

                @pl.when(own)
                def _():
                    near_copy.start()

                @pl.when(jnp.logical_not(own))
                def _():
                    far_copy.start()

    loads[0].wait()
    loads[2].wait()
    loads[3].wait()
    meas_load.wait()

    @pl.when(active)
    def _():
        i = square_iota(0)
        rows_hot = hot(square_iota(1) == 3 * (i % third) + i // third)
        cols_hot = hot(wide_iota(0) == 3 * at_lane + block)
        turned = hot_rows(hot_columns(phase[...], cols_hot), rows_hot)
        wanted = hot_rows(hot_columns(meas[...], cols_hot), rows_hot)
        for at in range(3):
            lanes = slice(at * LANES, (at + 1) * LANES)
            kern[0, at] = jnp.cos(turned[:, lanes])
            kern[1, at] = sign * jnp.sin(turned[:, lanes])
            up[at] = wanted[:, lanes]

    sign_root = sign * (0.5 * math.sqrt(3.0))
    sign_wide = jnp.concatenate([sign] * 3, axis=1).astype(BF16)

    def combine(a, b, c):
        both = b + c
        turned = swap(b - c) * sign_root
        base = a - 0.5 * both
        return a + both, base - turned, base + turned

    def join(values, axis):
        return jnp.concatenate(values, axis=axis)

    def times_i(x):
        parts = [swap(x[:, at * LANES : (at + 1) * LANES]) for at in range(3)]
        return join(parts, 1) * sign_wide

    def by_rows(at, x):
        head, rest = split(x)
        out = mm(row_t[at], join([head, times_i(head), rest, times_i(rest)], 0))
        return out[:third] + out[third:]

    def by_columns(at, x):
        head, rest = split(x)
        out = mm(join([head, rest], 1), col_t[at])
        return out[:, :LANES] + out[:, LANES:]

    def row_parts(x, q):
        return x[q * third : (q + 1) * third]

    def lane_parts(x, q):
        return x[:, q * LANES : (q + 1) * LANES]

    def dft(x):
        mixed = [combine(*[row_parts(one, q) for q in range(3)]) for one in x]
        out = [by_rows(q, join([one[q] for one in mixed], 1)) for q in range(3)]
        x = [join([lane_parts(one, at) for one in out], 0) for at in range(3)]
        mixed = combine(*x)
        return [by_columns(q, mixed[q]) for q in range(3)]

    def idft(x):
        out = [by_columns(3 + q, x[q]) for q in range(3)]
        first, second, last_ = combine(*out)
        x = [first, last_, second]
        out = [by_rows(3 + q, join([row_parts(one, q) for one in x], 1)) for q in range(3)]
        mixed = [combine(*[lane_parts(one, at) for one in out]) for at in range(3)]
        return [join([one[0], one[2], one[1]], 0) for one in mixed]

    def factor(x):
        turned = swap(x)
        return jnp.where(low, x, turned), jnp.where(low, -turned, x)

    def mul(x, pair):
        return [one * a + swap(one) * b for one, (a, b) in zip(x, pair)]

    def cmul(x, pair):
        return [one * a - swap(one) * b for one, (a, b) in zip(x, pair)]

    def kernel_pair():
        return [(kern[0, at], kern[1, at]) for at in range(3)]

    def field(ref, *at):
        return [ref[(*at, one)] for one in range(3)]

    def put(ref, x, *at):
        for one in range(3):
            ref[(*at, one)] = x[one]

    def unpack_window(s):
        for at in range(3):
            kept[s, 0, at], kept[s, 1, at] = factor(win[s, at])

    def window(s):
        return [(kept[s, 0, at], kept[s, 1, at]) for at in range(3)]

    def fwd_copy(s):
        return remote(win.at[s], win.at[s], fwd_s.at[s], fwd_r.at[s], partner)

    def int_copy(step):
        to_m, to_d = handler(p, (mu + step) % M)
        return remote(
            inten.at[0], inten.at[step], int_s.at[step - 1], int_r.at[step - 1], (to_m, g, to_d)
        )

    def pair_copy(s, to_m, ch):
        rows = pl.ds(to_m * H + ch * HC, HC)
        return remote(
            gs.at[s, :, rows, :], pg.at[s, :, rows, :], pg_s.at[s], pg_r.at[s, to_m, ch], partner
        )

    slot = p * half + mu // 2

    def owner_copy(s, to_m, start=0, rows=H, ch=0):
        source = gs.at[s, :, pl.ds(to_m * H + start, rows), :]
        place = og.at[slot, :, pl.ds(start, rows), :]
        own = (m == to_m) & (d == s)
        far_copy = remote(source, place, og_s.at[s, to_m], og_r.at[slot, ch], (to_m, g, s))
        near_copy = pltpu.make_async_copy(source, place, og_r.at[slot, ch])
        return own, far_copy, near_copy

    def send_gradient(s, incident):
        put(gs, cmul(incident, [factor(one) for one in field(psi, s)]), s)

        @pl.when(s % 2 != c)
        def _():
            for to_m in range(M):
                for ch in range(CH):
                    pair_copy(s, to_m, ch).start()

    def finish_gradient(s):
        @pl.when(s % 2 == c)
        def _():
            for to_m in range(M):
                for ch in range(CH):
                    rows = pl.ds(to_m * H + ch * HC, HC)
                    arrived(pg.at[s, :, rows, :], pg_r.at[s, to_m, ch])
                    gs[s, :, rows, :] = gs[s, :, rows, :] + pg[s, :, rows, :]
                    own, far_copy, near_copy = owner_copy(s, to_m, ch * HC, HC, ch)

                    @pl.when(own)
                    def _():
                        near_copy.start()

                    @pl.when(jnp.logical_not(own))
                    def _():
                        far_copy.start()

    @pl.when(active)
    def _():
        arrived(probe_in, prb_r)
        row_off = pos_ref[p, 0] - g * W
        col_off = pos_ref[p, 1]
        i = square_iota(0) - row_off
        j = square_iota(1)
        rows_hot = hot((i == j) | (i + W == j))
        b = block * third + at_lane - col_off
        j = wide_iota(0)
        hit = (b == j) | (b + W == j)
        start = hot_columns(probe_in[0], hot(hit & jnp.logical_not(imag)))
        start = start + hot_columns(probe_in[1], hot(hit & imag))
        start = hot_rows(start, rows_hot)
        put(psi, [lane_parts(start, at) for at in range(3)], 0)

        def pass_on(at):
            s = 2 * at + c
            for from_m in range(M):
                arrived(win.at[s, :, pl.ds(from_m * H, H), :], win_r.at[s, from_m])
            fwd_copy(s).start()

        pass_on(0)

        def await_window(s):
            @pl.when(s % 2 != c)
            def _():
                arrived(win.at[s], fwd_r.at[s])

        def forward(s, carry):
            await_window(s)
            unpack_window(s)
            spectrum = dft(mul(field(psi, s), window(s)))
            put(psi, idft(mul(spectrum, kernel_pair())), s + 1)

            @pl.when((s % 2 == 0) & (s + 2 < D))
            def _():
                pass_on(s // 2 + 1)

            return carry

        lax.fori_loop(0, D - 1, forward, 0)
        last = D - 1
        await_window(last)
        unpack_window(last)
        spectrum = mul(dft(mul(field(psi, last), window(last))), kernel_pair())
        put(far, spectrum)
        power = [one * one for one in spectrum]
        power = [one + swap(one) for one in power]
        inten[0, :, :LANES] = jnp.where(low, power[0], power[1])
        inten[0, :, LANES:] = power[2]
        for step in range(1, M):
            int_copy(step).start()
        for step in range(1, M):
            arrived(inten.at[step], int_r.at[step - 1])
        total = inten[0]
        for step in range(1, M):
            total = total + inten[step]
        front, rear = total[:, :LANES], total[:, LANES:]
        turned = swap(front)
        total = [jnp.where(low, front, turned), jnp.where(low, turned, front), rear]
        weighted = [
            2.0 * (total[at] - up[at]) * far[at] for at in range(3)
        ]
        incident = idft(cmul(weighted, kernel_pair()))
        send_gradient(last, incident)
        put(up, cmul(incident, window(last)))

        def backward(at, carry):
            s = D - 2 - at
            incident = idft(cmul(dft(field(up)), kernel_pair()))
            send_gradient(s, incident)
            finish_gradient(s + 1)
            put(up, cmul(incident, window(s)))
            return carry

        lax.fori_loop(0, D - 1, backward, 0)
        finish_gradient(jnp.int32(0))

    def rg_copy(ch):
        rows = pl.ds(ch * HC, HC)
        return remote(
            rg_out.at[:, rows, :], rg_in.at[:, rows, :], rg_s.at[ch], rg_r.at[ch], after
        )

    for ch in range(CH):
        rows = slice(ch * HC, (ch + 1) * HC)
        kept_here = [jnp.zeros((HC, WIDE), F32) for _ in range(2)]
        passed = [jnp.zeros((HC, WIDE), F32) for _ in range(2)]
        for pos in range(POS):
            row_off = pos_ref[pos, 0] - g * W
            col_off = pos_ref[pos, 1]
            for k in range(half):
                at = pos * half + k
                arrived(og.at[at, :, pl.ds(ch * HC, HC), :], og_r.at[at, ch])
            parts = [og[pos * half, at, rows] for at in range(3)]
            for k in range(1, half):
                parts = [parts[at] + og[pos * half + k, at, rows] for at in range(3)]
            both = unpack(*parts)
            for part in range(2):
                inside = jnp.where(col_id >= col_off, both[part], 0.0)
                outside = jnp.where(col_id < col_off, both[part], 0.0)
                placed = inside + pltpu.roll(outside, W, 1)
                own_rows = row_id[rows] >= row_off
                kept_here[part] += jnp.where(own_rows, placed, 0.0)
                passed[part] += jnp.where(own_rows, 0.0, placed)
        for part in range(2):
            rg_out[part, rows] = passed[part]
        rg_copy(ch).start()
        for part in range(2):
            out_ref[0, part, rows] = kept_here[part]
    for ch in range(CH):
        rows = slice(ch * HC, (ch + 1) * HC)
        rg_copy(ch).wait_recv()
        for part in range(2):
            out_ref[0, part, rows] += rg_in[part, rows]

    for ch in range(CH):
        rg_copy(ch).wait_send()
        rim_copy(ch).wait_send()
    for step in range(1, M):
        @pl.when(probe_goes(step))
        def _():
            probe_copy(step).wait_send()
    for pos in range(POS):
        for k in range(half):
            own, far_copy, _ = frame_copy(pos, k)

            @pl.when(jnp.logical_not(own))
            def _():
                far_copy.wait_send()

    @pl.when(active)
    def _():
        for step in range(1, M):
            int_copy(step).wait_send()
        for s in range(D):
            @pl.when(s % 2 == c)
            def _():
                fwd_copy(s).wait_send()
                for to_m in range(M):
                    own, far_copy, _ = owner_copy(s, to_m)

                    @pl.when(jnp.logical_not(own))
                    def _():
                        far_copy.wait_send()

            @pl.when(s % 2 != c)
            def _():
                whole = remote(gs.at[s], pg.at[s], pg_s.at[s], pg_r.at[s, 0, 0], partner)
                whole.wait_send()


def solution(mesh):
    M, N, D = mesh.shape["mode"], mesh.shape["dp"], mesh.shape["depth"]

    def body(probe, object_slices, propagator_phase, positions, measured):
        W = probe.shape[-1]
        H, WIDE = object_slices.shape[2], object_slices.shape[3]
        POS = positions.shape[0]
        assert object_slices.shape[0] == 1 and probe.shape[0] == 1
        assert H * M == W and POS <= D and WIDE == 2 * LANES and 2 * W == 3 * LANES
        half = M // 2
        CH = 3 if H % 24 == 0 else 1
        tables = [jnp.asarray(table) for table in dft_tables(W)]
        vmem = pl.BlockSpec(memory_space=pltpu.VMEM)
        hbm = pl.BlockSpec(memory_space=pltpu.HBM)
        dma = pltpu.SemaphoreType.DMA
        return pl.pallas_call(
            functools.partial(kernel, M, N, D, POS, W, H, WIDE, CH),
            out_shape=jax.ShapeDtypeStruct(object_slices.shape, F32),
            in_specs=[pl.BlockSpec(memory_space=pltpu.SMEM)] + [hbm] * 6,
            out_specs=vmem,
            scratch_shapes=[
                pltpu.VMEM((2, H, WIDE), F32),
                pltpu.VMEM((W, W), F32),
                pltpu.VMEM((W, W), F32),
                pltpu.VMEM(tables[0].shape, BF16),
                pltpu.VMEM(tables[1].shape, BF16),
                pltpu.VMEM((2, H, WIDE), F32),
                pltpu.VMEM((2, W, W), F32),
                pltpu.VMEM((POS, 3, H, LANES), F32),
                pltpu.VMEM((D, 3, W, LANES), F32),
                pltpu.VMEM((D, 3, W, LANES), F32),
                pltpu.VMEM((2, 3, W, LANES), F32),
                pltpu.VMEM((M, W, WIDE), F32),
                pltpu.VMEM((3, W, LANES), F32),
                pltpu.VMEM((3, W, LANES), F32),
                pltpu.VMEM((D, 2, 3, W, LANES), F32),
                pltpu.VMEM((D, 3, W, LANES), F32),
                pltpu.VMEM((D, 3, W, LANES), F32),
                pltpu.VMEM((POS * half, 3, H, LANES), F32),
                pltpu.VMEM((2, H, WIDE), F32),
                pltpu.VMEM((2, H, WIDE), F32),
                dma((5,)), dma((CH,)), dma((CH,)),
                dma((M - 1,)), dma,
                dma((POS, half)), dma((D, M)),
                dma((D,)), dma((D,)),
                dma((M - 1,)), dma((M - 1,)),
                dma((D,)), dma((D, M, CH)),
                dma((D, M)), dma((POS * half, CH)),
                dma((CH,)), dma((CH,)),
            ],
            compiler_params=pltpu.CompilerParams(
                collective_id=0, has_side_effects=True, vmem_limit_bytes=63 * 1024 * 1024
            ),
        )(positions, probe, object_slices, propagator_phase, measured, *tables)

    placed = (
        P("mode", None, None, None),
        P("depth", None, ("dp", "mode"), None),
        P(),
        P("dp", None),
        P("dp", None, None),
    )
    return jax.shard_map(
        body,
        mesh=mesh,
        in_specs=placed,
        out_specs=P("depth", None, ("dp", "mode"), None),
        check_vma=False,
    )
```

```python
import functools
import math

import jax
import jax.numpy as jnp
import ml_dtypes
import numpy as np
from jax import lax
from jax.experimental import pallas as pl
from jax.experimental.pallas import tpu as pltpu
from jax.sharding import PartitionSpec as P

MESH = pl.DeviceIdType.MESH
LANES = 128
F32 = jnp.float32
BF16 = jnp.bfloat16


def dft_tables(width):
    third = width // 3
    rows, columns = [], []
    turns = []
    for q in range(3):
        angles = np.outer(3 * np.arange(third) + q, np.arange(third)) % width
        turns.append(np.exp(-2j * math.pi * angles / width) / math.sqrt(width))
    for turn in turns + [one.conj().T for one in turns]:
        left = np.concatenate([turn.real, turn.imag], 1)
        right = np.block([[turn.real.T, turn.imag.T], [-turn.imag.T, turn.real.T]])
        parts = []
        for table in (left, right):
            head = table.astype(np.float32).astype(ml_dtypes.bfloat16)
            rest = (table - head.astype(np.float64)).astype(np.float32)
            parts += [head, rest.astype(ml_dtypes.bfloat16)]
        rows.append(np.block([[parts[0], parts[0]], [parts[1], 0 * parts[1]]]))
        columns.append(np.block([[parts[2], parts[3]], [parts[2], 0 * parts[3]]]))
    return [np.stack(one).astype(ml_dtypes.bfloat16) for one in (rows, columns)]


def split(value):
    head = value.astype(BF16)
    return head, (value - head.astype(F32)).astype(BF16)


def mm(a, b):
    return jnp.dot(a, b, preferred_element_type=F32)


def kernel(
    M, N, D, POS, W, H, WIDE, CH,
    pos_ref, probe_ref, obj_ref, phase_ref, meas_ref,
    row_hbm, col_hbm,
    own_ref, rim_ref,
    tile, phase, meas, row_t, col_t,
    rim, probe_in, fr, win, psi, kern, inten, far, up, kept, gs, pg, og, rg_out, own_out, rl,
    load, rim_s, rim_r, prb_s, prb_r, fr_s, win_r, fwd_s, fwd_r, int_s, int_r,
    pg_s, pg_r, og_s, og_r, rg_s, rg_r, rl_s, rl_r,
):
    m = lax.axis_index("mode")
    g = lax.axis_index("dp")
    d = lax.axis_index("depth")
    c = d % 2
    half = M // 2
    u = (d // 2) * M + m
    p = u % D
    mu = 2 * (u // D) + c
    active = p < POS
    partner = (m, g, d + 1 - 2 * c)
    third = W // 3
    HC = H // CH
    before = (m, (g + N - 1) % N, d)
    after = (m, (g + 1) % N, d)

    def handler(pos, mode):
        at = D * (mode // 2) + pos
        return at % M, 2 * (at // M) + mode % 2

    def remote(src, dst, s_sem, r_sem, device):
        return pltpu.make_async_remote_copy(
            src_ref=src, dst_ref=dst, send_sem=s_sem, recv_sem=r_sem,
            device_id=device, device_id_type=MESH,
        )

    def arrived(ref, sem):
        pltpu.make_async_copy(ref, ref, sem).wait()

    loads = [
        pltpu.make_async_copy(src, dst, load.at[at])
        for at, (src, dst) in enumerate(
            ((phase_ref, phase), (obj_ref.at[0], tile), (row_hbm, row_t), (col_hbm, col_t))
        )
    ]
    for one in loads:
        one.start()
    meas_load = pltpu.make_async_copy(meas_ref.at[jnp.minimum(p, POS - 1)], meas, load.at[4])
    meas_load.start()
    own_probe = pltpu.make_async_copy(probe_ref.at[0], probe_in, prb_r)

    @pl.when(active & (mu == m))
    def _():
        own_probe.start()

    barrier = pltpu.get_barrier_semaphore()
    me = d * M + m
    for step in range(1, M * D):
        other = (me + step) % (M * D)
        pl.semaphore_signal(
            barrier, inc=1, device_id=(other % M, g, other // M), device_id_type=MESH
        )
    for device in (before, after):
        pl.semaphore_signal(barrier, inc=1, device_id=device, device_id_type=MESH)
    pl.semaphore_wait(barrier, M * D + 1)

    def rim_copy(ch):
        rows = pl.ds(ch * HC, HC)
        return remote(
            obj_ref.at[0, :, rows, :], rim.at[:, rows, :], rim_s.at[ch], rim_r.at[ch], before
        )

    for ch in range(CH):
        rim_copy(ch).start()

    def probe_needed(mode_at):
        return 2 * (((d // 2) * M + mode_at) // D) + c

    def probe_copy(step):
        return remote(
            probe_ref.at[0], probe_in, prb_s.at[step - 1], prb_r, ((m + step) % M, g, d)
        )

    def probe_goes(step):
        target = (m + step) % M
        return (probe_needed(target) == m) & (((d // 2) * M + target) % D < POS)

    for step in range(1, M):
        @pl.when(probe_goes(step))
        def _():
            probe_copy(step).start()

    lane = lax.broadcasted_iota(jnp.int32, (1, LANES), 1)
    low = lane < third

    sign = jnp.where(low, -1.0, 1.0)

    def swap(x):
        return pltpu.roll(x, third, 1)

    def pack(re, im):
        return [
            jnp.where(low, re[:, :LANES], swap(im[:, :LANES])),
            jnp.where(low, swap(re[:, :LANES]), im[:, :LANES]),
            jnp.where(low, re[:, LANES:], swap(im[:, LANES:])),
        ]

    def unpack(a, b, t):
        re = [jnp.where(low, a, swap(b)), jnp.where(low, t, 0.0)]
        im = [jnp.where(low, swap(a), b), jnp.where(low, swap(t), 0.0)]
        return jnp.concatenate(re, axis=1), jnp.concatenate(im, axis=1)

    def thirds(x):
        first = x.astype(BF16)
        x = x - first.astype(F32)
        second = x.astype(BF16)
        return first, second, (x - second.astype(F32)).astype(BF16)

    def hot(mask):
        return jnp.where(mask, 1.0, 0.0).astype(BF16)

    def hot_columns(x, cols_hot):
        a0, a1, a2 = thirds(x)
        return mm(a0, cols_hot) + (mm(a1, cols_hot) + mm(a2, cols_hot))

    def hot_rows(x, rows_hot):
        a0, a1, a2 = thirds(x)
        return mm(rows_hot, a0) + (mm(rows_hot, a1) + mm(rows_hot, a2))

    def wide_iota(axis):
        return lax.broadcasted_iota(jnp.int32, (W, 3 * LANES), axis)

    def square_iota(axis):
        return lax.broadcasted_iota(jnp.int32, (W, W), axis)

    block = wide_iota(1) // LANES
    at_lane = wide_iota(1) % third
    imag = (wide_iota(1) // third) % 2 == 1

    loads[1].wait()
    row_id = lax.broadcasted_iota(jnp.int32, (H, 1), 0) + m * H
    col_id = lax.broadcasted_iota(jnp.int32, (1, WIDE), 1)

    def frame_copy(pos, k, start=0, rows=H):
        to_m, _ = handler(pos, 2 * k)
        to_d = 2 * ((D * k + pos) // M) + c
        source = fr.at[pos, :, pl.ds(start, rows), :]
        place = win.at[d, :, pl.ds(pl.multiple_of(m * H + start, 8), rows), :]
        own = (m == to_m) & (d == to_d)
        far_copy = remote(source, place, fr_s.at[pos, k], win_r.at[d, m], (to_m, g, to_d))
        near_copy = pltpu.make_async_copy(source, place, win_r.at[d, m])
        return own, far_copy, near_copy

    for ch in range(CH):
        rim_copy(ch).wait_recv()
        rows = slice(ch * HC, (ch + 1) * HC)
        for pos in range(POS):
            row_off = pos_ref[0, pos] - g * W
            col_off = pos_ref[1, pos]
            parts = []
            for part in range(2):
                chosen = jnp.where(row_id[rows] >= row_off, tile[part, rows], rim[part, rows])
                wrapped = pltpu.roll(chosen, WIDE - W, 1)
                parts.append(jnp.where(col_id >= col_off, chosen, wrapped))

            for at, value in enumerate(pack(parts[0], parts[1])):
                fr[pos, at, rows] = value
            for k in range(half):
                own, far_copy, near_copy = frame_copy(pos, k, ch * HC, HC)

                @pl.when(own)
                def _():
                    near_copy.start()

                @pl.when(jnp.logical_not(own))
                def _():
                    far_copy.start()

    loads[0].wait()
    loads[2].wait()
    loads[3].wait()
    meas_load.wait()

    @pl.when(active)
    def _():
        i = square_iota(0)
        rows_hot = hot(square_iota(1) == 3 * (i % third) + i // third)
        cols_hot = hot(wide_iota(0) == 3 * at_lane + block)
        turned = hot_rows(hot_columns(phase[...], cols_hot), rows_hot)
        wanted = hot_rows(hot_columns(meas[...], cols_hot), rows_hot)
        for at in range(3):
            lanes = slice(at * LANES, (at + 1) * LANES)
            kern[0, at] = jnp.cos(turned[:, lanes])
            kern[1, at] = sign * jnp.sin(turned[:, lanes])
            up[at] = wanted[:, lanes]

    sign_root = sign * (0.5 * math.sqrt(3.0))
    sign_wide = jnp.concatenate([sign] * 3, axis=1).astype(BF16)

    def combine(a, b, c):
        both = b + c
        turned = swap(b - c) * sign_root
        base = a - 0.5 * both
        return a + both, base - turned, base + turned

    def join(values, axis):
        return jnp.concatenate(values, axis=axis)

    def times_i(x):
        parts = [swap(x[:, at * LANES : (at + 1) * LANES]) for at in range(3)]
        return join(parts, 1) * sign_wide

    def by_rows(at, x):
        head, rest = split(x)
        out = mm(row_t[at], join([head, times_i(head), rest, times_i(rest)], 0))
        return out[:third] + out[third:]

    def by_columns(at, x):
        head, rest = split(x)
        out = mm(join([head, rest], 1), col_t[at])
        return out[:, :LANES] + out[:, LANES:]

    def row_parts(x, q):
        return x[q * third : (q + 1) * third]

    def lane_parts(x, q):
        return x[:, q * LANES : (q + 1) * LANES]

    def dft(x):
        mixed = [combine(*[row_parts(one, q) for q in range(3)]) for one in x]
        out = [by_rows(q, join([one[q] for one in mixed], 1)) for q in range(3)]
        x = [join([lane_parts(one, at) for one in out], 0) for at in range(3)]
        mixed = combine(*x)
        return [by_columns(q, mixed[q]) for q in range(3)]

    def idft(x):
        out = [by_columns(3 + q, x[q]) for q in range(3)]
        first, second, last_ = combine(*out)
        x = [first, last_, second]
        out = [by_rows(3 + q, join([row_parts(one, q) for one in x], 1)) for q in range(3)]
        mixed = [combine(*[lane_parts(one, at) for one in out]) for at in range(3)]
        return [join([one[0], one[2], one[1]], 0) for one in mixed]

    def factor(x):
        turned = swap(x)
        return jnp.where(low, x, turned), jnp.where(low, -turned, x)

    def mul(x, pair):
        return [one * a + swap(one) * b for one, (a, b) in zip(x, pair)]

    def cmul(x, pair):
        return [one * a - swap(one) * b for one, (a, b) in zip(x, pair)]

    def kernel_pair():
        return [(kern[0, at], kern[1, at]) for at in range(3)]

    def field(ref, *at):
        return [ref[(*at, one)] for one in range(3)]

    def put(ref, x, *at):
        for one in range(3):
            ref[(*at, one)] = x[one]

    def unpack_window(s):
        for at in range(3):
            kept[s, 0, at], kept[s, 1, at] = factor(win[s, at])

    def window(s):
        return [(kept[s, 0, at], kept[s, 1, at]) for at in range(3)]

    def fwd_copy(s, from_m):
        place = win.at[s, :, pl.ds(from_m * H, H), :]
        return remote(place, place, fwd_s.at[s], fwd_r.at[s, from_m], partner)

    def int_copy(step):
        to_m, to_d = handler(p, (mu + step) % M)
        return remote(
            inten.at[0], inten.at[step], int_s.at[step - 1], int_r.at[step - 1], (to_m, g, to_d)
        )

    def pair_copy(s, to_m, ch):
        rows = pl.ds(to_m * H + ch * HC, HC)
        return remote(
            gs.at[s, :, rows, :], pg.at[s, :, rows, :], pg_s.at[s], pg_r.at[s, to_m, ch], partner
        )

    slot = p * half + mu // 2

    def owner_copy(s, to_m, start=0, rows=H, ch=0):
        source = gs.at[s, :, pl.ds(to_m * H + start, rows), :]
        place = og.at[slot, :, pl.ds(start, rows), :]
        own = (m == to_m) & (d == s)
        far_copy = remote(source, place, og_s.at[s, to_m], og_r.at[slot, ch], (to_m, g, s))
        near_copy = pltpu.make_async_copy(source, place, og_r.at[slot, ch])
        hop_copy = remote(
            source, rl.at[:, pl.ds(start, rows), :], og_s.at[s, to_m], rl_r.at[ch], (to_m, g, d)
        )
        return own, far_copy, near_copy, hop_copy

    relays = M == 2 and POS == 3 and D == 4

    def hops(s, to_m):
        return (p == 2) & (s < 2) & (to_m != m) if relays else False

    def relay_copy(ch):
        rows = pl.ds(ch * HC, HC)
        return remote(
            rl.at[:, rows, :], og.at[2, :, rows, :], rl_s.at[ch], og_r.at[2, ch], (m, g, c)
        )

    def send_gradient(s, incident):
        put(gs, cmul(incident, [factor(one) for one in field(psi, s)]), s)

        @pl.when(s % 2 != c)
        def _():
            for to_m in range(M):
                for ch in range(CH):
                    pair_copy(s, to_m, ch).start()

    def finish_gradient(s):
        @pl.when(s % 2 == c)
        def _():
            for to_m in range(M):
                for ch in range(CH):
                    rows = pl.ds(to_m * H + ch * HC, HC)
                    arrived(pg.at[s, :, rows, :], pg_r.at[s, to_m, ch])
                    gs[s, :, rows, :] = gs[s, :, rows, :] + pg[s, :, rows, :]
                    own, far_copy, near_copy, hop_copy = owner_copy(s, to_m, ch * HC, HC, ch)
                    hop = hops(s, to_m)

                    @pl.when(own)
                    def _():
                        near_copy.start()

                    @pl.when(jnp.logical_not(own | hop))
                    def _():
                        far_copy.start()

                    if relays:
                        @pl.when(hop)
                        def _():
                            hop_copy.start()

    @pl.when(active)
    def _():
        arrived(probe_in, prb_r)
        row_off = pos_ref[0, p] - g * W
        col_off = pos_ref[1, p]
        i = square_iota(0) - row_off
        j = square_iota(1)
        rows_hot = hot((i == j) | (i + W == j))
        b = block * third + at_lane - col_off
        j = wide_iota(0)
        hit = (b == j) | (b + W == j)
        start = hot_columns(probe_in[0], hot(hit & jnp.logical_not(imag)))
        start = start + hot_columns(probe_in[1], hot(hit & imag))
        start = hot_rows(start, rows_hot)
        put(psi, [lane_parts(start, at) for at in range(3)], 0)

        def pass_on(at):
            s = 2 * at + c
            for from_m in range(M):
                arrived(win.at[s, :, pl.ds(from_m * H, H), :], win_r.at[s, from_m])
                fwd_copy(s, from_m).start()

        pass_on(0)

        def await_window(s):
            @pl.when(s % 2 != c)
            def _():
                for from_m in range(M):
                    arrived(win.at[s, :, pl.ds(from_m * H, H), :], fwd_r.at[s, from_m])

        def forward(s, carry):
            await_window(s)
            unpack_window(s)
            spectrum = dft(mul(field(psi, s), window(s)))
            put(psi, idft(mul(spectrum, kernel_pair())), s + 1)

            @pl.when((s % 2 == 0) & (s + 2 < D))
            def _():
                pass_on(s // 2 + 1)

            return carry

        lax.fori_loop(0, D - 1, forward, 0)
        last = D - 1
        await_window(last)
        unpack_window(last)
        spectrum = mul(dft(mul(field(psi, last), window(last))), kernel_pair())
        put(far, spectrum)
        power = [one * one for one in spectrum]
        power = [one + swap(one) for one in power]
        inten[0, :, :LANES] = jnp.where(low, power[0], power[1])
        inten[0, :, LANES:] = power[2]
        for step in range(1, M):
            int_copy(step).start()
        for step in range(1, M):
            arrived(inten.at[step], int_r.at[step - 1])
        total = inten[0]
        for step in range(1, M):
            total = total + inten[step]
        front, rear = total[:, :LANES], total[:, LANES:]
        turned = swap(front)
        total = [jnp.where(low, front, turned), jnp.where(low, turned, front), rear]
        weighted = [
            2.0 * (total[at] - up[at]) * far[at] for at in range(3)
        ]
        incident = idft(cmul(weighted, kernel_pair()))
        send_gradient(last, incident)
        put(up, cmul(incident, window(last)))

        def backward(at, carry):
            s = D - 2 - at
            put(up, cmul(dft(field(up)), kernel_pair()))
            finish_gradient(s + 1)
            incident = idft(field(up))
            send_gradient(s, incident)
            put(up, cmul(incident, window(s)))
            return carry

        lax.fori_loop(0, D - 1, backward, 0)
        finish_gradient(jnp.int32(0))

    def rg_copy(ch):
        rows = pl.ds(ch * HC, HC)
        return remote(
            rg_out.at[:, rows, :], rim_ref.at[0, :, rows, :], rg_s.at[ch], rg_r.at[ch], after
        )

    for ch in range(CH):
        rows = slice(ch * HC, (ch + 1) * HC)
        kept_here = [jnp.zeros((HC, WIDE), F32) for _ in range(2)]
        passed = [jnp.zeros((HC, WIDE), F32) for _ in range(2)]
        for pos in range(POS):
            row_off = pos_ref[0, pos] - g * W
            col_off = pos_ref[1, pos]
            for k in range(half):
                at = pos * half + k
                arrived(og.at[at, :, pl.ds(ch * HC, HC), :], og_r.at[at, ch])
            parts = [og[pos * half, at, rows] for at in range(3)]
            for k in range(1, half):
                parts = [parts[at] + og[pos * half + k, at, rows] for at in range(3)]
            both = unpack(*parts)
            for part in range(2):
                inside = jnp.where(col_id >= col_off, both[part], 0.0)
                outside = jnp.where(col_id < col_off, both[part], 0.0)
                placed = inside + pltpu.roll(outside, W, 1)
                own_rows = row_id[rows] >= row_off
                kept_here[part] += jnp.where(own_rows, placed, 0.0)
                passed[part] += jnp.where(own_rows, 0.0, placed)
        for part in range(2):
            rg_out[part, rows] = passed[part]
        rg_copy(ch).start()
        for part in range(2):
            own_out[part, rows] = kept_here[part]
    stored = pltpu.make_async_copy(own_out, own_ref.at[0], load.at[0])
    stored.start()
    if relays:
        @pl.when(p == 3)
        def _():
            for ch in range(CH):
                arrived(rl.at[:, pl.ds(ch * HC, HC), :], rl_r.at[ch])
                relay_copy(ch).start()

    for ch in range(CH):
        rg_copy(ch).wait_recv()
    stored.wait()

    for ch in range(CH):
        rg_copy(ch).wait_send()
        rim_copy(ch).wait_send()
    for step in range(1, M):
        @pl.when(probe_goes(step))
        def _():
            probe_copy(step).wait_send()
    for pos in range(POS):
        for k in range(half):
            own, far_copy, _ = frame_copy(pos, k)

            @pl.when(jnp.logical_not(own))
            def _():
                far_copy.wait_send()

    if relays:
        @pl.when(p == 3)
        def _():
            for ch in range(CH):
                relay_copy(ch).wait_send()

    @pl.when(active)
    def _():
        for step in range(1, M):
            int_copy(step).wait_send()
        for s in range(D):
            @pl.when(s % 2 == c)
            def _():
                whole = remote(win.at[s], win.at[s], fwd_s.at[s], fwd_r.at[s, 0], partner)
                whole.wait_send()
                for to_m in range(M):
                    own, far_copy, _, _ = owner_copy(s, to_m)

                    @pl.when(jnp.logical_not(own))
                    def _():
                        far_copy.wait_send()

            @pl.when(s % 2 != c)
            def _():
                whole = remote(gs.at[s], pg.at[s], pg_s.at[s], pg_r.at[s, 0, 0], partner)
                whole.wait_send()


def solution(mesh):
    M, N, D = mesh.shape["mode"], mesh.shape["dp"], mesh.shape["depth"]

    def body(probe, object_slices, propagator_phase, positions, measured):
        W = probe.shape[-1]
        H, WIDE = object_slices.shape[2], object_slices.shape[3]
        POS = positions.shape[0]
        assert object_slices.shape[0] == 1 and probe.shape[0] == 1
        assert H * M == W and POS <= D and WIDE == 2 * LANES and 2 * W == 3 * LANES
        half = M // 2
        CH = 3 if H % 24 == 0 else 1
        tables = [jnp.asarray(table) for table in dft_tables(W)]
        hbm = pl.BlockSpec(memory_space=pltpu.HBM)
        dma = pltpu.SemaphoreType.DMA
        own, below = pl.pallas_call(
            functools.partial(kernel, M, N, D, POS, W, H, WIDE, CH),
            out_shape=[jax.ShapeDtypeStruct(object_slices.shape, F32)] * 2,
            in_specs=[pl.BlockSpec(memory_space=pltpu.SMEM)] + [hbm] * 6,
            out_specs=[hbm, hbm],
            scratch_shapes=[
                pltpu.VMEM((2, H, WIDE), F32),
                pltpu.VMEM((W, W), F32),
                pltpu.VMEM((W, W), F32),
                pltpu.VMEM(tables[0].shape, BF16),
                pltpu.VMEM(tables[1].shape, BF16),
                pltpu.VMEM((2, H, WIDE), F32),
                pltpu.VMEM((2, W, W), F32),
                pltpu.VMEM((POS, 3, H, LANES), F32),
                pltpu.VMEM((D, 3, W, LANES), F32),
                pltpu.VMEM((D, 3, W, LANES), F32),
                pltpu.VMEM((2, 3, W, LANES), F32),
                pltpu.VMEM((M, W, WIDE), F32),
                pltpu.VMEM((3, W, LANES), F32),
                pltpu.VMEM((3, W, LANES), F32),
                pltpu.VMEM((D, 2, 3, W, LANES), F32),
                pltpu.VMEM((D, 3, W, LANES), F32),
                pltpu.VMEM((D, 3, W, LANES), F32),
                pltpu.VMEM((POS * half, 3, H, LANES), F32),
                pltpu.VMEM((2, H, WIDE), F32),
                pltpu.VMEM((2, H, WIDE), F32),
                pltpu.VMEM((3, H, LANES), F32),
                dma((5,)), dma((CH,)), dma((CH,)),
                dma((M - 1,)), dma,
                dma((POS, half)), dma((D, M)),
                dma((D,)), dma((D, M)),
                dma((M - 1,)), dma((M - 1,)),
                dma((D,)), dma((D, M, CH)),
                dma((D, M)), dma((POS * half, CH)),
                dma((CH,)), dma((CH,)),
                dma((CH,)), dma((CH,)),
            ],
            compiler_params=pltpu.CompilerParams(
                collective_id=0, has_side_effects=True, vmem_limit_bytes=63 * 1024 * 1024
            ),
        )(positions.T, probe, object_slices, propagator_phase, measured, *tables)
        return own + below

    placed = (
        P("mode", None, None, None),
        P("depth", None, ("dp", "mode"), None),
        P(),
        P("dp", None),
        P("dp", None, None),
    )
    return jax.shard_map(
        body,
        mesh=mesh,
        in_specs=placed,
        out_specs=P("depth", None, ("dp", "mode"), None),
        check_vma=False,
    )
```

```python
import functools
import math

import jax
import jax.numpy as jnp
import ml_dtypes
import numpy as np
from jax import lax
from jax.experimental import pallas as pl
from jax.experimental.pallas import tpu as pltpu
from jax.sharding import PartitionSpec as P

MESH = pl.DeviceIdType.MESH
LANES = 128
F32 = jnp.float32
BF16 = jnp.bfloat16


def dft_tables(width):
    third = width // 3
    rows, columns = [], []
    turns = []
    for q in range(3):
        angles = np.outer(3 * np.arange(third) + q, np.arange(third)) % width
        turns.append(np.exp(-2j * math.pi * angles / width) / math.sqrt(width))
    for turn in turns + [one.conj().T for one in turns]:
        left = np.concatenate([turn.real, turn.imag], 1)
        right = np.block([[turn.real.T, turn.imag.T], [-turn.imag.T, turn.real.T]])
        parts = []
        for table in (left, right):
            head = table.astype(np.float32).astype(ml_dtypes.bfloat16)
            rest = (table - head.astype(np.float64)).astype(np.float32)
            parts += [head, rest.astype(ml_dtypes.bfloat16)]
        rows.append(np.block([[parts[0], parts[0]], [parts[1], 0 * parts[1]]]))
        columns.append(np.block([[parts[2], parts[3]], [parts[2], 0 * parts[3]]]))
    return [np.stack(one).astype(ml_dtypes.bfloat16) for one in (rows, columns)]


def split(value):
    head = value.astype(BF16)
    return head, (value - head.astype(F32)).astype(BF16)


def mm(a, b):
    return jnp.dot(a, b, preferred_element_type=F32)


def kernel(
    M, N, D, POS, W, H, WIDE, CH,
    pos_ref, probe_ref, obj_ref, phase_ref, meas_ref,
    row_hbm, col_hbm,
    out_ref,
    tile, phase, meas, row_t, col_t,
    rim, probe_in, fr, win, psi, kern, wanted, inten, far, up, kept, gs, pg, og, rg_out, rg_in,
    load, rim_s, rim_r, prb_s, prb_r, fr_s, win_r, fwd_s, fwd_r, int_s, int_r,
    pg_s, pg_r, og_s, og_r, rg_s, rg_r,
):
    m = lax.axis_index("mode")
    g = lax.axis_index("dp")
    d = lax.axis_index("depth")
    c = d % 2
    half = M // 2
    u = (d // 2) * M + m
    p = u % D
    mu = 2 * (u // D) + c
    active = p < POS
    partner = (m, g, d + 1 - 2 * c)
    third = W // 3
    HC = H // CH
    before = (m, (g + N - 1) % N, d)
    after = (m, (g + 1) % N, d)

    def handler(pos, mode):
        at = D * (mode // 2) + pos
        return at % M, 2 * (at // M) + mode % 2

    def remote(src, dst, s_sem, r_sem, device):
        return pltpu.make_async_remote_copy(
            src_ref=src, dst_ref=dst, send_sem=s_sem, recv_sem=r_sem,
            device_id=device, device_id_type=MESH,
        )

    def arrived(ref, sem):
        pltpu.make_async_copy(ref, ref, sem).wait()

    loads = [
        pltpu.make_async_copy(src, dst, load.at[at])
        for at, (src, dst) in enumerate(
            ((phase_ref, phase), (obj_ref.at[0], tile), (row_hbm, row_t), (col_hbm, col_t))
        )
    ]
    for one in loads:
        one.start()
    meas_load = pltpu.make_async_copy(meas_ref.at[jnp.minimum(p, POS - 1)], meas, load.at[4])
    meas_load.start()
    own_probe = pltpu.make_async_copy(probe_ref.at[0], probe_in, prb_r)

    @pl.when(active & (mu == m))
    def _():
        own_probe.start()

    barrier = pltpu.get_barrier_semaphore()
    me = d * M + m
    for step in range(1, M * D):
        other = (me + step) % (M * D)
        pl.semaphore_signal(
            barrier, inc=1, device_id=(other % M, g, other // M), device_id_type=MESH
        )
    for device in (before, after):
        pl.semaphore_signal(barrier, inc=1, device_id=device, device_id_type=MESH)
    pl.semaphore_wait(barrier, M * D + 1)

    def rim_copy(ch):
        rows = pl.ds(ch * HC, HC)
        return remote(
            obj_ref.at[0, :, rows, :], rim.at[:, rows, :], rim_s.at[ch], rim_r.at[ch], before
        )

    for ch in range(CH):
        rim_copy(ch).start()

    def probe_needed(mode_at):
        return 2 * (((d // 2) * M + mode_at) // D) + c

    def probe_copy(step):
        return remote(
            probe_ref.at[0], probe_in, prb_s.at[step - 1], prb_r, ((m + step) % M, g, d)
        )

    def probe_goes(step):
        target = (m + step) % M
        return (probe_needed(target) == m) & (((d // 2) * M + target) % D < POS)

    for step in range(1, M):
        @pl.when(probe_goes(step))
        def _():
            probe_copy(step).start()

    lane = lax.broadcasted_iota(jnp.int32, (1, LANES), 1)
    low = lane < third

    sign = jnp.where(low, -1.0, 1.0)

    def swap(x):
        return pltpu.roll(x, third, 1)

    def pack(re, im):
        return [
            jnp.where(low, re[:, :LANES], swap(im[:, :LANES])),
            jnp.where(low, swap(re[:, :LANES]), im[:, :LANES]),
            jnp.where(low, re[:, LANES:], swap(im[:, LANES:])),
        ]

    def unpack(a, b, t):
        re = [jnp.where(low, a, swap(b)), jnp.where(low, t, 0.0)]
        im = [jnp.where(low, swap(a), b), jnp.where(low, swap(t), 0.0)]
        return jnp.concatenate(re, axis=1), jnp.concatenate(im, axis=1)

    def hot(mask):
        return jnp.where(mask, 1.0, 0.0).astype(BF16)

    def pieces(x, count):
        out = []
        for _ in range(count):
            out.append(x.astype(BF16))
            x = x - out[-1].astype(F32)
        return out

    def moved(x, rows_hot, cols_hot, count):
        x = sum(mm(rows_hot, one) for one in reversed(pieces(x, count)))
        return sum(mm(one, cols_hot) for one in reversed(pieces(x, count)))

    def expand(x):
        front, rear = x[:, :LANES], x[:, LANES:]
        turned = swap(front)
        return [
            jnp.where(low, front, turned),
            jnp.where(low, turned, front),
            jnp.where(low, rear, swap(rear)),
        ]

    def turn(angle):
        y = 0.5 * angle
        z = y * y
        sine = z * (1.0 / 6227020800.0) - 1.0 / 39916800.0
        for top in (362880.0, -5040.0, 120.0, -6.0, 1.0):
            sine = sine * z + 1.0 / top
        sine = sine * y
        cosine = z * (-1.0 / 87178291200.0) + 1.0 / 479001600.0
        for top in (-3628800.0, 40320.0, -720.0, 24.0, -2.0, 1.0):
            cosine = cosine * z + 1.0 / top
        return 1.0 - 2.0 * sine * sine, 2.0 * sine * cosine

    down = lax.broadcasted_iota(jnp.int32, (W, 1), 0)
    across = lax.broadcasted_iota(jnp.int32, (1, W), 1)
    col_id = lax.broadcasted_iota(jnp.int32, (1, WIDE), 1)

    loads[0].wait()
    meas_load.wait()

    @pl.when(active)
    def _():
        rows_hot = hot(across == 3 * (down % third) + down // third)
        cols_hot = hot((down == 3 * (col_id % third) + col_id // third) & (col_id < W))
        wanted[...] = moved(meas[...], rows_hot, cols_hot, 2)
        cosine, sine = turn(moved(phase[...], rows_hot, cols_hot, 3))
        for at, value in enumerate(expand(cosine)):
            kern[0, at] = value
        for at, value in enumerate(expand(sine)):
            kern[1, at] = sign * value

    loads[1].wait()
    row_id = lax.broadcasted_iota(jnp.int32, (H, 1), 0) + m * H

    def frame_copy(pos, k, start=0, rows=H):
        to_m, _ = handler(pos, 2 * k)
        to_d = 2 * ((D * k + pos) // M) + c
        source = fr.at[pos, :, pl.ds(start, rows), :]
        place = win.at[d, :, pl.ds(pl.multiple_of(m * H + start, 8), rows), :]
        own = (m == to_m) & (d == to_d)
        far_copy = remote(source, place, fr_s.at[pos, k], win_r.at[d, m], (to_m, g, to_d))
        near_copy = pltpu.make_async_copy(source, place, win_r.at[d, m])
        return own, far_copy, near_copy

    for ch in range(CH):
        rim_copy(ch).wait_recv()
        rows = slice(ch * HC, (ch + 1) * HC)
        for pos in range(POS):
            row_off = pos_ref[0, pos] - g * W
            col_off = pos_ref[1, pos]
            parts = []
            for part in range(2):
                chosen = jnp.where(row_id[rows] >= row_off, tile[part, rows], rim[part, rows])
                wrapped = pltpu.roll(chosen, WIDE - W, 1)
                parts.append(jnp.where(col_id >= col_off, chosen, wrapped))

            for at, value in enumerate(pack(parts[0], parts[1])):
                fr[pos, at, rows] = value
            for k in range(half):
                own, far_copy, near_copy = frame_copy(pos, k, ch * HC, HC)

                @pl.when(own)
                def _():
                    near_copy.start()

                @pl.when(jnp.logical_not(own))
                def _():
                    far_copy.start()

    loads[2].wait()
    loads[3].wait()

    sign_root = sign * (0.5 * math.sqrt(3.0))
    sign_wide = jnp.concatenate([sign] * 3, axis=1).astype(BF16)

    def combine(a, b, c):
        both = b + c
        turned = swap(b - c) * sign_root
        base = a - 0.5 * both
        return a + both, base - turned, base + turned

    def join(values, axis):
        return jnp.concatenate(values, axis=axis)

    def times_i(x):
        parts = [swap(x[:, at * LANES : (at + 1) * LANES]) for at in range(3)]
        return join(parts, 1) * sign_wide

    def by_rows(at, x):
        head, rest = split(x)
        out = mm(row_t[at], join([head, times_i(head), rest, times_i(rest)], 0))
        return out[:third] + out[third:]

    def by_columns(at, x):
        head, rest = split(x)
        out = mm(join([head, rest], 1), col_t[at])
        return out[:, :LANES] + out[:, LANES:]

    def row_parts(x, q):
        return x[q * third : (q + 1) * third]

    def lane_parts(x, q):
        return x[:, q * LANES : (q + 1) * LANES]

    def dft(x):
        mixed = [combine(*[row_parts(one, q) for q in range(3)]) for one in x]
        out = [by_rows(q, join([one[q] for one in mixed], 1)) for q in range(3)]
        x = [join([lane_parts(one, at) for one in out], 0) for at in range(3)]
        mixed = combine(*x)
        return [by_columns(q, mixed[q]) for q in range(3)]

    def idft(x):
        out = [by_columns(3 + q, x[q]) for q in range(3)]
        first, second, last_ = combine(*out)
        x = [first, last_, second]
        out = [by_rows(3 + q, join([row_parts(one, q) for one in x], 1)) for q in range(3)]
        mixed = [combine(*[lane_parts(one, at) for one in out]) for at in range(3)]
        return [join([one[0], one[2], one[1]], 0) for one in mixed]

    def factor(x):
        turned = swap(x)
        return jnp.where(low, x, turned), jnp.where(low, -turned, x)

    def mul(x, pair):
        return [one * a + swap(one) * b for one, (a, b) in zip(x, pair)]

    def cmul(x, pair):
        return [one * a - swap(one) * b for one, (a, b) in zip(x, pair)]

    def kernel_pair():
        return [(kern[0, at], kern[1, at]) for at in range(3)]

    def field(ref, *at):
        return [ref[(*at, one)] for one in range(3)]

    def put(ref, x, *at):
        for one in range(3):
            ref[(*at, one)] = x[one]

    def unpack_window(s):
        for at in range(3):
            kept[s, 0, at], kept[s, 1, at] = factor(win[s, at])

    def window(s):
        return [(kept[s, 0, at], kept[s, 1, at]) for at in range(3)]

    def fwd_copy(s):
        return remote(win.at[s], win.at[s], fwd_s.at[s], fwd_r.at[s], partner)

    def int_copy(step):
        to_m, to_d = handler(p, (mu + step) % M)
        return remote(
            inten.at[0], inten.at[step], int_s.at[step - 1], int_r.at[step - 1], (to_m, g, to_d)
        )

    def pair_copy(s, to_m, ch):
        rows = pl.ds(to_m * H + ch * HC, HC)
        return remote(
            gs.at[s, :, rows, :], pg.at[s, :, rows, :], pg_s.at[s], pg_r.at[s, to_m, ch], partner
        )

    slot = p * half + mu // 2

    def owner_copy(s, to_m, start=0, rows=H, ch=0):
        source = gs.at[s, :, pl.ds(to_m * H + start, rows), :]
        place = og.at[slot, :, pl.ds(start, rows), :]
        own = (m == to_m) & (d == s)
        far_copy = remote(source, place, og_s.at[s, to_m], og_r.at[slot, ch], (to_m, g, s))
        near_copy = pltpu.make_async_copy(source, place, og_r.at[slot, ch])
        return own, far_copy, near_copy

    def send_gradient(s, incident):
        put(gs, cmul(incident, [factor(one) for one in field(psi, s)]), s)

        @pl.when(s % 2 != c)
        def _():
            for to_m in range(M):
                for ch in range(CH):
                    pair_copy(s, to_m, ch).start()

    def finish_gradient(s):
        @pl.when(s % 2 == c)
        def _():
            for to_m in range(M):
                for ch in range(CH):
                    rows = pl.ds(to_m * H + ch * HC, HC)
                    arrived(pg.at[s, :, rows, :], pg_r.at[s, to_m, ch])
                    gs[s, :, rows, :] = gs[s, :, rows, :] + pg[s, :, rows, :]
                    own, far_copy, near_copy = owner_copy(s, to_m, ch * HC, HC, ch)

                    @pl.when(own)
                    def _():
                        near_copy.start()

                    @pl.when(jnp.logical_not(own))
                    def _():
                        far_copy.start()

    @pl.when(active)
    def _():
        arrived(probe_in, prb_r)
        row_off = pos_ref[0, p] - g * W
        col_off = pos_ref[1, p]
        i = down - row_off
        rows_hot = hot((i == across) | (i + W == across))
        b = col_id - col_off
        cols_hot = hot(((b == down) | (b + W == down)) & (col_id < W))
        start = [moved(probe_in[part], rows_hot, cols_hot, 2) for part in range(2)]
        put(psi, pack(*start), 0)

        def pass_on(at):
            s = 2 * at + c
            for from_m in range(M):
                arrived(win.at[s, :, pl.ds(from_m * H, H), :], win_r.at[s, from_m])
            fwd_copy(s).start()

        pass_on(0)

        def await_window(s):
            @pl.when(s % 2 != c)
            def _():
                arrived(win.at[s], fwd_r.at[s])

        def forward(s, carry):
            await_window(s)
            unpack_window(s)
            spectrum = dft(mul(field(psi, s), window(s)))
            put(psi, idft(mul(spectrum, kernel_pair())), s + 1)

            @pl.when((s % 2 == 0) & (s + 2 < D))
            def _():
                pass_on(s // 2 + 1)

            return carry

        lax.fori_loop(0, D - 1, forward, 0)
        last = D - 1
        await_window(last)
        unpack_window(last)
        spectrum = mul(dft(mul(field(psi, last), window(last))), kernel_pair())
        put(far, spectrum)
        power = [one * one for one in spectrum]
        power = [one + swap(one) for one in power]
        inten[0, :, :LANES] = jnp.where(low, power[0], power[1])
        inten[0, :, LANES:] = power[2]
        for step in range(1, M):
            int_copy(step).start()
        for step in range(1, M):
            arrived(inten.at[step], int_r.at[step - 1])
        total = inten[0]
        for step in range(1, M):
            total = total + inten[step]
        misfit = expand(2.0 * (total - wanted[...]))
        weighted = [misfit[at] * far[at] for at in range(3)]
        incident = idft(cmul(weighted, kernel_pair()))
        send_gradient(last, incident)
        put(up, cmul(incident, window(last)))

        def backward(at, carry):
            s = D - 2 - at
            incident = idft(cmul(dft(field(up)), kernel_pair()))
            send_gradient(s, incident)
            finish_gradient(s + 1)
            put(up, cmul(incident, window(s)))
            return carry

        lax.fori_loop(0, D - 1, backward, 0)
        finish_gradient(jnp.int32(0))

    def rg_copy(ch):
        rows = pl.ds(ch * HC, HC)
        return remote(
            rg_out.at[:, rows, :], rg_in.at[:, rows, :], rg_s.at[ch], rg_r.at[ch], after
        )

    for ch in range(CH):
        rows = slice(ch * HC, (ch + 1) * HC)
        kept_here = [jnp.zeros((HC, WIDE), F32) for _ in range(2)]
        passed = [jnp.zeros((HC, WIDE), F32) for _ in range(2)]
        for pos in range(POS):
            row_off = pos_ref[0, pos] - g * W
            col_off = pos_ref[1, pos]
            for k in range(half):
                at = pos * half + k
                arrived(og.at[at, :, pl.ds(ch * HC, HC), :], og_r.at[at, ch])
            parts = [og[pos * half, at, rows] for at in range(3)]
            for k in range(1, half):
                parts = [parts[at] + og[pos * half + k, at, rows] for at in range(3)]
            both = unpack(*parts)
            for part in range(2):
                inside = jnp.where(col_id >= col_off, both[part], 0.0)
                outside = jnp.where(col_id < col_off, both[part], 0.0)
                placed = inside + pltpu.roll(outside, W, 1)
                own_rows = row_id[rows] >= row_off
                kept_here[part] += jnp.where(own_rows, placed, 0.0)
                passed[part] += jnp.where(own_rows, 0.0, placed)
        for part in range(2):
            rg_out[part, rows] = passed[part]
        rg_copy(ch).start()
        for part in range(2):
            out_ref[0, part, rows] = kept_here[part]
    for ch in range(CH):
        rows = slice(ch * HC, (ch + 1) * HC)
        rg_copy(ch).wait_recv()
        for part in range(2):
            out_ref[0, part, rows] += rg_in[part, rows]

    for ch in range(CH):
        rg_copy(ch).wait_send()
        rim_copy(ch).wait_send()
    for step in range(1, M):
        @pl.when(probe_goes(step))
        def _():
            probe_copy(step).wait_send()
    for pos in range(POS):
        for k in range(half):
            own, far_copy, _ = frame_copy(pos, k)

            @pl.when(jnp.logical_not(own))
            def _():
                far_copy.wait_send()

    @pl.when(active)
    def _():
        for step in range(1, M):
            int_copy(step).wait_send()
        for s in range(D):
            @pl.when(s % 2 == c)
            def _():
                fwd_copy(s).wait_send()
                for to_m in range(M):
                    own, far_copy, _ = owner_copy(s, to_m)

                    @pl.when(jnp.logical_not(own))
                    def _():
                        far_copy.wait_send()

            @pl.when(s % 2 != c)
            def _():
                whole = remote(gs.at[s], pg.at[s], pg_s.at[s], pg_r.at[s, 0, 0], partner)
                whole.wait_send()


def solution(mesh):
    M, N, D = mesh.shape["mode"], mesh.shape["dp"], mesh.shape["depth"]

    def body(probe, object_slices, propagator_phase, positions, measured):
        W = probe.shape[-1]
        H, WIDE = object_slices.shape[2], object_slices.shape[3]
        POS = positions.shape[0]
        assert object_slices.shape[0] == 1 and probe.shape[0] == 1
        assert H * M == W and POS <= D and WIDE == 2 * LANES and 2 * W == 3 * LANES
        half = M // 2
        CH = 3 if H % 24 == 0 else 1
        tables = [jnp.asarray(table) for table in dft_tables(W)]
        vmem = pl.BlockSpec(memory_space=pltpu.VMEM)
        hbm = pl.BlockSpec(memory_space=pltpu.HBM)
        dma = pltpu.SemaphoreType.DMA
        return pl.pallas_call(
            functools.partial(kernel, M, N, D, POS, W, H, WIDE, CH),
            out_shape=jax.ShapeDtypeStruct(object_slices.shape, F32),
            in_specs=[pl.BlockSpec(memory_space=pltpu.SMEM)] + [hbm] * 6,
            out_specs=vmem,
            scratch_shapes=[
                pltpu.VMEM((2, H, WIDE), F32),
                pltpu.VMEM((W, W), F32),
                pltpu.VMEM((W, W), F32),
                pltpu.VMEM(tables[0].shape, BF16),
                pltpu.VMEM(tables[1].shape, BF16),
                pltpu.VMEM((2, H, WIDE), F32),
                pltpu.VMEM((2, W, W), F32),
                pltpu.VMEM((POS, 3, H, LANES), F32),
                pltpu.VMEM((D, 3, W, LANES), F32),
                pltpu.VMEM((D, 3, W, LANES), F32),
                pltpu.VMEM((2, 3, W, LANES), F32),
                pltpu.VMEM((W, WIDE), F32),
                pltpu.VMEM((M, W, WIDE), F32),
                pltpu.VMEM((3, W, LANES), F32),
                pltpu.VMEM((3, W, LANES), F32),
                pltpu.VMEM((D, 2, 3, W, LANES), F32),
                pltpu.VMEM((D, 3, W, LANES), F32),
                pltpu.VMEM((D, 3, W, LANES), F32),
                pltpu.VMEM((POS * half, 3, H, LANES), F32),
                pltpu.VMEM((2, H, WIDE), F32),
                pltpu.VMEM((2, H, WIDE), F32),
                dma((5,)), dma((CH,)), dma((CH,)),
                dma((M - 1,)), dma,
                dma((POS, half)), dma((D, M)),
                dma((D,)), dma((D,)),
                dma((M - 1,)), dma((M - 1,)),
                dma((D,)), dma((D, M, CH)),
                dma((D, M)), dma((POS * half, CH)),
                dma((CH,)), dma((CH,)),
            ],
            compiler_params=pltpu.CompilerParams(
                collective_id=0, has_side_effects=True, vmem_limit_bytes=63 * 1024 * 1024
            ),
        )(positions.T, probe, object_slices, propagator_phase, measured, *tables)

    placed = (
        P("mode", None, None, None),
        P("depth", None, ("dp", "mode"), None),
        P(),
        P("dp", None),
        P("dp", None, None),
    )
    return jax.shard_map(
        body,
        mesh=mesh,
        in_specs=placed,
        out_specs=P("depth", None, ("dp", "mode"), None),
        check_vma=False,
    )
```

```python
import functools
import math

import jax
import jax.numpy as jnp
import ml_dtypes
import numpy as np
from jax import lax
from jax.experimental import pallas as pl
from jax.experimental.pallas import tpu as pltpu
from jax.sharding import PartitionSpec as P

MESH = pl.DeviceIdType.MESH
LANES = 128
F32 = jnp.float32
BF16 = jnp.bfloat16


def dft_tables(width):
    third = width // 3
    rows, columns = [], []
    turns = []
    for q in range(3):
        angles = np.outer(3 * np.arange(third) + q, np.arange(third)) % width
        turns.append(np.exp(-2j * math.pi * angles / width) / math.sqrt(width))
    for turn in turns + [one.conj().T for one in turns]:
        left = np.concatenate([turn.real, turn.imag], 1)
        right = np.block([[turn.real.T, turn.imag.T], [-turn.imag.T, turn.real.T]])
        parts = []
        for table in (left, right):
            head = table.astype(np.float32).astype(ml_dtypes.bfloat16)
            rest = (table - head.astype(np.float64)).astype(np.float32)
            parts += [head, rest.astype(ml_dtypes.bfloat16)]
        rows.append(np.block([[parts[0], parts[0]], [parts[1], 0 * parts[1]]]))
        columns.append(np.block([[parts[2], parts[3]], [parts[2], 0 * parts[3]]]))
    return [np.stack(one).astype(ml_dtypes.bfloat16) for one in (rows, columns)]


def split(value):
    head = value.astype(BF16)
    return head, (value - head.astype(F32)).astype(BF16)


def mm(a, b):
    return jnp.dot(a, b, preferred_element_type=F32)


def kernel(
    M, N, D, POS, W, H, WIDE, CH, CG,
    pos_ref, probe_ref, obj_ref, phase_ref, meas_ref,
    row_hbm, col_hbm,
    out_ref,
    tile, phase, meas, row_t, col_t,
    rim, probe_in, fr, win, psi, kern, wanted, inten, far, up, kept, gs, pg, og, rg_out, rg_in,
    load, rim_s, rim_r, prb_s, prb_r, fr_s, win_r, fwd_s, fwd_r, int_s, int_r,
    pg_s, pg_r, og_s, og_r, rg_s, rg_r,
):
    m = lax.axis_index("mode")
    g = lax.axis_index("dp")
    d = lax.axis_index("depth")
    c = d % 2
    half = M // 2
    u = (d // 2) * M + m
    p = u % D
    mu = 2 * (u // D) + c
    active = p < POS
    partner = (m, g, d + 1 - 2 * c)
    third = W // 3
    HC = H // CH
    HG = H // CG
    before = (m, (g + N - 1) % N, d)
    after = (m, (g + 1) % N, d)

    def handler(pos, mode):
        at = D * (mode // 2) + pos
        return at % M, 2 * (at // M) + mode % 2

    def remote(src, dst, s_sem, r_sem, device):
        return pltpu.make_async_remote_copy(
            src_ref=src, dst_ref=dst, send_sem=s_sem, recv_sem=r_sem,
            device_id=device, device_id_type=MESH,
        )

    def arrived(ref, sem):
        pltpu.make_async_copy(ref, ref, sem).wait()

    loads = [
        pltpu.make_async_copy(src, dst, load.at[at])
        for at, (src, dst) in enumerate(
            ((phase_ref, phase), (obj_ref.at[0], tile), (row_hbm, row_t), (col_hbm, col_t))
        )
    ]
    for one in loads:
        one.start()
    meas_load = pltpu.make_async_copy(meas_ref.at[jnp.minimum(p, POS - 1)], meas, load.at[4])
    meas_load.start()
    own_probe = pltpu.make_async_copy(probe_ref.at[0], probe_in, prb_r)

    @pl.when(active & (mu == m))
    def _():
        own_probe.start()

    barrier = pltpu.get_barrier_semaphore()
    me = d * M + m
    for step in range(1, M * D):
        other = (me + step) % (M * D)
        pl.semaphore_signal(
            barrier, inc=1, device_id=(other % M, g, other // M), device_id_type=MESH
        )
    for device in (before, after):
        pl.semaphore_signal(barrier, inc=1, device_id=device, device_id_type=MESH)
    pl.semaphore_wait(barrier, M * D + 1)

    def rim_copy(ch):
        rows = pl.ds(ch * HC, HC)
        return remote(
            obj_ref.at[0, :, rows, :], rim.at[:, rows, :], rim_s.at[ch], rim_r.at[ch], before
        )

    for ch in range(CH):
        rim_copy(ch).start()

    def probe_needed(mode_at):
        return 2 * (((d // 2) * M + mode_at) // D) + c

    def probe_copy(step):
        return remote(
            probe_ref.at[0], probe_in, prb_s.at[step - 1], prb_r, ((m + step) % M, g, d)
        )

    def probe_goes(step):
        target = (m + step) % M
        return (probe_needed(target) == m) & (((d // 2) * M + target) % D < POS)

    for step in range(1, M):
        @pl.when(probe_goes(step))
        def _():
            probe_copy(step).start()

    lane = lax.broadcasted_iota(jnp.int32, (1, LANES), 1)
    low = lane < third

    sign = jnp.where(low, -1.0, 1.0)

    def swap(x):
        return pltpu.roll(x, third, 1)

    def pack(re, im):
        return [
            jnp.where(low, re[:, :LANES], swap(im[:, :LANES])),
            jnp.where(low, swap(re[:, :LANES]), im[:, :LANES]),
            jnp.where(low, re[:, LANES:], swap(im[:, LANES:])),
        ]

    def unpack(a, b, t):
        re = [jnp.where(low, a, swap(b)), jnp.where(low, t, 0.0)]
        im = [jnp.where(low, swap(a), b), jnp.where(low, swap(t), 0.0)]
        return jnp.concatenate(re, axis=1), jnp.concatenate(im, axis=1)

    def hot(mask):
        return jnp.where(mask, 1.0, 0.0).astype(BF16)

    def pieces(x, count):
        out = []
        for _ in range(count):
            out.append(x.astype(BF16))
            x = x - out[-1].astype(F32)
        return out

    def moved(x, rows_hot, cols_hot, count):
        x = sum(mm(rows_hot, one) for one in reversed(pieces(x, count)))
        return sum(mm(one, cols_hot) for one in reversed(pieces(x, count)))

    def expand(x):
        front, rear = x[:, :LANES], x[:, LANES:]
        turned = swap(front)
        return [
            jnp.where(low, front, turned),
            jnp.where(low, turned, front),
            jnp.where(low, rear, swap(rear)),
        ]

    def turn(angle):
        y = 0.5 * angle
        z = y * y
        sine = z * (1.0 / 6227020800.0) - 1.0 / 39916800.0
        for top in (362880.0, -5040.0, 120.0, -6.0, 1.0):
            sine = sine * z + 1.0 / top
        sine = sine * y
        cosine = z * (-1.0 / 87178291200.0) + 1.0 / 479001600.0
        for top in (-3628800.0, 40320.0, -720.0, 24.0, -2.0, 1.0):
            cosine = cosine * z + 1.0 / top
        return 1.0 - 2.0 * sine * sine, 2.0 * sine * cosine

    down = lax.broadcasted_iota(jnp.int32, (W, 1), 0)
    across = lax.broadcasted_iota(jnp.int32, (1, W), 1)
    col_id = lax.broadcasted_iota(jnp.int32, (1, WIDE), 1)

    loads[0].wait()
    meas_load.wait()

    @pl.when(active)
    def _():
        rows_hot = hot(across == 3 * (down % third) + down // third)
        cols_hot = hot((down == 3 * (col_id % third) + col_id // third) & (col_id < W))
        wanted[...] = moved(meas[...], rows_hot, cols_hot, 2)
        cosine, sine = turn(moved(phase[...], rows_hot, cols_hot, 3))
        for at, value in enumerate(expand(cosine)):
            kern[0, at] = value
        for at, value in enumerate(expand(sine)):
            kern[1, at] = sign * value

    loads[1].wait()
    row_id = lax.broadcasted_iota(jnp.int32, (H, 1), 0) + m * H

    def frame_copy(pos, k, start=0, rows=H):
        to_m, _ = handler(pos, 2 * k)
        to_d = 2 * ((D * k + pos) // M) + c
        source = fr.at[pos, :, pl.ds(start, rows), :]
        place = win.at[d, :, pl.ds(pl.multiple_of(m * H + start, 8), rows), :]
        own = (m == to_m) & (d == to_d)
        far_copy = remote(source, place, fr_s.at[pos, k], win_r.at[d, m], (to_m, g, to_d))
        near_copy = pltpu.make_async_copy(source, place, win_r.at[d, m])
        return own, far_copy, near_copy

    for ch in range(CH):
        rim_copy(ch).wait_recv()
        rows = slice(ch * HC, (ch + 1) * HC)
        for pos in range(POS):
            row_off = pos_ref[0, pos] - g * W
            col_off = pos_ref[1, pos]
            parts = []
            for part in range(2):
                chosen = jnp.where(row_id[rows] >= row_off, tile[part, rows], rim[part, rows])
                wrapped = pltpu.roll(chosen, WIDE - W, 1)
                parts.append(jnp.where(col_id >= col_off, chosen, wrapped))

            for at, value in enumerate(pack(parts[0], parts[1])):
                fr[pos, at, rows] = value
            for k in range(half):
                own, far_copy, near_copy = frame_copy(pos, k, ch * HC, HC)

                @pl.when(own)
                def _():
                    near_copy.start()

                @pl.when(jnp.logical_not(own))
                def _():
                    far_copy.start()

    loads[2].wait()
    loads[3].wait()

    sign_root = sign * (0.5 * math.sqrt(3.0))
    sign_wide = jnp.concatenate([sign] * 3, axis=1).astype(BF16)

    def combine(a, b, c):
        both = b + c
        turned = swap(b - c) * sign_root
        base = a - 0.5 * both
        return a + both, base - turned, base + turned

    def join(values, axis):
        return jnp.concatenate(values, axis=axis)

    def times_i(x):
        parts = [swap(x[:, at * LANES : (at + 1) * LANES]) for at in range(3)]
        return join(parts, 1) * sign_wide

    def by_rows(at, x):
        head, rest = split(x)
        out = mm(row_t[at], join([head, times_i(head), rest, times_i(rest)], 0))
        return out[:third] + out[third:]

    def by_columns(at, x):
        head, rest = split(x)
        out = mm(join([head, rest], 1), col_t[at])
        return out[:, :LANES] + out[:, LANES:]

    def row_parts(x, q):
        return x[q * third : (q + 1) * third]

    def lane_parts(x, q):
        return x[:, q * LANES : (q + 1) * LANES]

    def dft(x):
        mixed = [combine(*[row_parts(one, q) for q in range(3)]) for one in x]
        out = [by_rows(q, join([one[q] for one in mixed], 1)) for q in range(3)]
        x = [join([lane_parts(one, at) for one in out], 0) for at in range(3)]
        mixed = combine(*x)
        return [by_columns(q, mixed[q]) for q in range(3)]

    def idft(x):
        out = [by_columns(3 + q, x[q]) for q in range(3)]
        first, second, last_ = combine(*out)
        x = [first, last_, second]
        out = [by_rows(3 + q, join([row_parts(one, q) for one in x], 1)) for q in range(3)]
        mixed = [combine(*[lane_parts(one, at) for one in out]) for at in range(3)]
        return [join([one[0], one[2], one[1]], 0) for one in mixed]

    def factor(x):
        turned = swap(x)
        return jnp.where(low, x, turned), jnp.where(low, -turned, x)

    def mul(x, pair):
        return [one * a + swap(one) * b for one, (a, b) in zip(x, pair)]

    def cmul(x, pair):
        return [one * a - swap(one) * b for one, (a, b) in zip(x, pair)]

    def kernel_pair():
        return [(kern[0, at], kern[1, at]) for at in range(3)]

    def field(ref, *at):
        return [ref[(*at, one)] for one in range(3)]

    def put(ref, x, *at):
        for one in range(3):
            ref[(*at, one)] = x[one]

    def unpack_window(s):
        for at in range(3):
            kept[s, 0, at], kept[s, 1, at] = factor(win[s, at])

    def window(s):
        return [(kept[s, 0, at], kept[s, 1, at]) for at in range(3)]

    def fwd_copy(s):
        return remote(win.at[s], win.at[s], fwd_s.at[s], fwd_r.at[s], partner)

    def int_copy(step):
        to_m, to_d = handler(p, (mu + step) % M)
        return remote(
            inten.at[0], inten.at[step], int_s.at[step - 1], int_r.at[step - 1], (to_m, g, to_d)
        )

    def pair_copy(s, to_m, ch):
        rows = pl.ds(to_m * H + ch * HG, HG)
        return remote(
            gs.at[s, :, rows, :], pg.at[s, :, rows, :], pg_s.at[s], pg_r.at[s, to_m, ch], partner
        )

    slot = p * half + mu // 2

    def owner_copy(s, to_m, start=0, rows=H, ch=0):
        source = gs.at[s, :, pl.ds(to_m * H + start, rows), :]
        place = og.at[slot, :, pl.ds(start, rows), :]
        own = (m == to_m) & (d == s)
        far_copy = remote(source, place, og_s.at[s, to_m], og_r.at[slot, ch], (to_m, g, s))
        near_copy = pltpu.make_async_copy(source, place, og_r.at[slot, ch])
        return own, far_copy, near_copy

    def send_gradient(s, incident):
        put(gs, cmul(incident, [factor(one) for one in field(psi, s)]), s)

        @pl.when(s % 2 != c)
        def _():
            for to_m in range(M):
                for ch in range(CG):
                    pair_copy(s, to_m, ch).start()

    def finish_gradient(s):
        @pl.when(s % 2 == c)
        def _():
            for to_m in range(M):
                for ch in range(CG):
                    rows = pl.ds(to_m * H + ch * HG, HG)
                    arrived(pg.at[s, :, rows, :], pg_r.at[s, to_m, ch])
                    gs[s, :, rows, :] = gs[s, :, rows, :] + pg[s, :, rows, :]
                    own, far_copy, near_copy = owner_copy(s, to_m, ch * HG, HG, ch)

                    @pl.when(own)
                    def _():
                        near_copy.start()

                    @pl.when(jnp.logical_not(own))
                    def _():
                        far_copy.start()

    @pl.when(active)
    def _():
        arrived(probe_in, prb_r)
        row_off = pos_ref[0, p] - g * W
        col_off = pos_ref[1, p]
        i = down - row_off
        rows_hot = hot((i == across) | (i + W == across))
        b = col_id - col_off
        cols_hot = hot(((b == down) | (b + W == down)) & (col_id < W))
        start = [moved(probe_in[part], rows_hot, cols_hot, 2) for part in range(2)]
        put(psi, pack(*start), 0)

        def pass_on(at):
            s = 2 * at + c
            for from_m in range(M):
                arrived(win.at[s, :, pl.ds(from_m * H, H), :], win_r.at[s, from_m])
            fwd_copy(s).start()

        pass_on(0)

        def await_window(s):
            @pl.when(s % 2 != c)
            def _():
                arrived(win.at[s], fwd_r.at[s])

        def forward(s, carry):
            await_window(s)
            unpack_window(s)
            spectrum = dft(mul(field(psi, s), window(s)))
            put(psi, idft(mul(spectrum, kernel_pair())), s + 1)

            @pl.when((s % 2 == 0) & (s + 2 < D))
            def _():
                pass_on(s // 2 + 1)

            return carry

        lax.fori_loop(0, D - 1, forward, 0)
        last = D - 1
        await_window(last)
        unpack_window(last)
        spectrum = mul(dft(mul(field(psi, last), window(last))), kernel_pair())
        put(far, spectrum)
        power = [one * one for one in spectrum]
        power = [one + swap(one) for one in power]
        inten[0, :, :LANES] = jnp.where(low, power[0], power[1])
        inten[0, :, LANES:] = power[2]
        for step in range(1, M):
            int_copy(step).start()
        for step in range(1, M):
            arrived(inten.at[step], int_r.at[step - 1])
        total = inten[0]
        for step in range(1, M):
            total = total + inten[step]
        misfit = expand(2.0 * (total - wanted[...]))
        weighted = [misfit[at] * far[at] for at in range(3)]
        incident = idft(cmul(weighted, kernel_pair()))
        send_gradient(last, incident)
        put(up, cmul(incident, window(last)))

        def backward(at, carry):
            s = D - 2 - at
            incident = idft(cmul(dft(field(up)), kernel_pair()))
            send_gradient(s, incident)
            finish_gradient(s + 1)
            put(up, cmul(incident, window(s)))
            return carry

        lax.fori_loop(0, D - 1, backward, 0)
        finish_gradient(jnp.int32(0))

    def rg_copy(ch):
        rows = pl.ds(ch * HG, HG)
        return remote(
            rg_out.at[:, rows, :], rg_in.at[:, rows, :], rg_s.at[ch], rg_r.at[ch], after
        )

    for ch in range(CG):
        rows = slice(ch * HG, (ch + 1) * HG)
        kept_here = [jnp.zeros((HG, WIDE), F32) for _ in range(2)]
        passed = [jnp.zeros((HG, WIDE), F32) for _ in range(2)]
        for pos in range(POS):
            row_off = pos_ref[0, pos] - g * W
            col_off = pos_ref[1, pos]
            for k in range(half):
                at = pos * half + k
                arrived(og.at[at, :, pl.ds(ch * HG, HG), :], og_r.at[at, ch])
            parts = [og[pos * half, at, rows] for at in range(3)]
            for k in range(1, half):
                parts = [parts[at] + og[pos * half + k, at, rows] for at in range(3)]
            both = unpack(*parts)
            for part in range(2):
                inside = jnp.where(col_id >= col_off, both[part], 0.0)
                outside = jnp.where(col_id < col_off, both[part], 0.0)
                placed = inside + pltpu.roll(outside, W, 1)
                own_rows = row_id[rows] >= row_off
                kept_here[part] += jnp.where(own_rows, placed, 0.0)
                passed[part] += jnp.where(own_rows, 0.0, placed)
        for part in range(2):
            rg_out[part, rows] = passed[part]
        rg_copy(ch).start()
        for part in range(2):
            out_ref[0, part, rows] = kept_here[part]
    for ch in range(CG):
        rows = slice(ch * HG, (ch + 1) * HG)
        rg_copy(ch).wait_recv()
        for part in range(2):
            out_ref[0, part, rows] += rg_in[part, rows]

    for ch in range(CG):
        rg_copy(ch).wait_send()
    for ch in range(CH):
        rim_copy(ch).wait_send()
    for step in range(1, M):
        @pl.when(probe_goes(step))
        def _():
            probe_copy(step).wait_send()
    for pos in range(POS):
        for k in range(half):
            own, far_copy, _ = frame_copy(pos, k)

            @pl.when(jnp.logical_not(own))
            def _():
                far_copy.wait_send()

    @pl.when(active)
    def _():
        for step in range(1, M):
            int_copy(step).wait_send()
        for s in range(D):
            @pl.when(s % 2 == c)
            def _():
                fwd_copy(s).wait_send()
                for to_m in range(M):
                    own, far_copy, _ = owner_copy(s, to_m)

                    @pl.when(jnp.logical_not(own))
                    def _():
                        far_copy.wait_send()

            @pl.when(s % 2 != c)
            def _():
                whole = remote(gs.at[s], pg.at[s], pg_s.at[s], pg_r.at[s, 0, 0], partner)
                whole.wait_send()


def solution(mesh):
    M, N, D = mesh.shape["mode"], mesh.shape["dp"], mesh.shape["depth"]

    def body(probe, object_slices, propagator_phase, positions, measured):
        W = probe.shape[-1]
        H, WIDE = object_slices.shape[2], object_slices.shape[3]
        POS = positions.shape[0]
        assert object_slices.shape[0] == 1 and probe.shape[0] == 1
        assert H * M == W and POS <= D and WIDE == 2 * LANES and 2 * W == 3 * LANES
        half = M // 2
        CH = 3 if H % 24 == 0 else 1
        CG = 1
        tables = [jnp.asarray(table) for table in dft_tables(W)]
        vmem = pl.BlockSpec(memory_space=pltpu.VMEM)
        hbm = pl.BlockSpec(memory_space=pltpu.HBM)
        dma = pltpu.SemaphoreType.DMA
        return pl.pallas_call(
            functools.partial(kernel, M, N, D, POS, W, H, WIDE, CH, CG),
            out_shape=jax.ShapeDtypeStruct(object_slices.shape, F32),
            in_specs=[pl.BlockSpec(memory_space=pltpu.SMEM)] + [hbm] * 6,
            out_specs=vmem,
            scratch_shapes=[
                pltpu.VMEM((2, H, WIDE), F32),
                pltpu.VMEM((W, W), F32),
                pltpu.VMEM((W, W), F32),
                pltpu.VMEM(tables[0].shape, BF16),
                pltpu.VMEM(tables[1].shape, BF16),
                pltpu.VMEM((2, H, WIDE), F32),
                pltpu.VMEM((2, W, W), F32),
                pltpu.VMEM((POS, 3, H, LANES), F32),
                pltpu.VMEM((D, 3, W, LANES), F32),
                pltpu.VMEM((D, 3, W, LANES), F32),
                pltpu.VMEM((2, 3, W, LANES), F32),
                pltpu.VMEM((W, WIDE), F32),
                pltpu.VMEM((M, W, WIDE), F32),
                pltpu.VMEM((3, W, LANES), F32),
                pltpu.VMEM((3, W, LANES), F32),
                pltpu.VMEM((D, 2, 3, W, LANES), F32),
                pltpu.VMEM((D, 3, W, LANES), F32),
                pltpu.VMEM((D, 3, W, LANES), F32),
                pltpu.VMEM((POS * half, 3, H, LANES), F32),
                pltpu.VMEM((2, H, WIDE), F32),
                pltpu.VMEM((2, H, WIDE), F32),
                dma((5,)), dma((CH,)), dma((CH,)),
                dma((M - 1,)), dma,
                dma((POS, half)), dma((D, M)),
                dma((D,)), dma((D,)),
                dma((M - 1,)), dma((M - 1,)),
                dma((D,)), dma((D, M, CG)),
                dma((D, M)), dma((POS * half, CG)),
                dma((CG,)), dma((CG,)),
            ],
            compiler_params=pltpu.CompilerParams(
                collective_id=0, has_side_effects=True, vmem_limit_bytes=63 * 1024 * 1024
            ),
        )(positions.T, probe, object_slices, propagator_phase, measured, *tables)

    placed = (
        P("mode", None, None, None),
        P("depth", None, ("dp", "mode"), None),
        P(),
        P("dp", None),
        P("dp", None, None),
    )
    return jax.shard_map(
        body,
        mesh=mesh,
        in_specs=placed,
        out_specs=P("depth", None, ("dp", "mode"), None),
        check_vma=False,
    )
```

```python
import functools
import math

import jax
import jax.numpy as jnp
import ml_dtypes
import numpy as np
from jax import lax
from jax.experimental import pallas as pl
from jax.experimental.pallas import tpu as pltpu
from jax.sharding import PartitionSpec as P

MESH = pl.DeviceIdType.MESH
LANES = 128
F32 = jnp.float32
BF16 = jnp.bfloat16


def dft_tables(width):
    third = width // 3
    rows, columns = [], []
    turns = []
    for q in range(3):
        angles = np.outer(3 * np.arange(third) + q, np.arange(third)) % width
        turns.append(np.exp(-2j * math.pi * angles / width) / math.sqrt(width))
    for turn in turns + [one.conj().T for one in turns]:
        left = np.concatenate([turn.real, turn.imag], 1)
        right = np.block([[turn.real.T, turn.imag.T], [-turn.imag.T, turn.real.T]])
        parts = []
        for table in (left, right):
            head = table.astype(np.float32).astype(ml_dtypes.bfloat16)
            rest = (table - head.astype(np.float64)).astype(np.float32)
            parts += [head, rest.astype(ml_dtypes.bfloat16)]
        rows.append(np.block([[parts[0], parts[0]], [parts[1], 0 * parts[1]]]))
        columns.append(np.block([[parts[2], parts[3]], [parts[2], 0 * parts[3]]]))
    return [np.stack(one).astype(ml_dtypes.bfloat16) for one in (rows, columns)]


def split(value):
    head = value.astype(BF16)
    return head, (value - head.astype(F32)).astype(BF16)


def mm(a, b):
    return jnp.dot(a, b, preferred_element_type=F32)


def kernel(
    M, N, D, POS, W, H, WIDE, CH,
    pos_ref, probe_ref, obj_ref, phase_ref, meas_ref,
    row_hbm, col_hbm,
    out_ref,
    tile, phase, meas, row_t, col_t,
    rim, probe_in, fr, win, psi, kern, wanted, inten, far, up, kept, gs, pg, og, rg_out, rg_in,
    load, rim_s, rim_r, prb_s, prb_r, fr_s, win_r, fwd_s, fwd_r, int_s, int_r,
    pg_s, pg_r, og_s, og_r, rg_s, rg_r,
):
    m = lax.axis_index("mode")
    g = lax.axis_index("dp")
    d = lax.axis_index("depth")
    c = d % 2
    half = M // 2
    u = (d // 2) * M + m
    p = u % D
    mu = 2 * (u // D) + c
    active = p < POS
    partner = (m, g, d + 1 - 2 * c)
    third = W // 3
    HC = H // CH
    before = (m, (g + N - 1) % N, d)
    after = (m, (g + 1) % N, d)

    def handler(pos, mode):
        at = D * (mode // 2) + pos
        return at % M, 2 * (at // M) + mode % 2

    def remote(src, dst, s_sem, r_sem, device):
        return pltpu.make_async_remote_copy(
            src_ref=src, dst_ref=dst, send_sem=s_sem, recv_sem=r_sem,
            device_id=device, device_id_type=MESH,
        )

    def arrived(ref, sem):
        pltpu.make_async_copy(ref, ref, sem).wait()

    loads = [
        pltpu.make_async_copy(src, dst, load.at[at])
        for at, (src, dst) in enumerate(
            ((phase_ref, phase), (obj_ref.at[0], tile), (row_hbm, row_t), (col_hbm, col_t))
        )
    ]
    for one in loads:
        one.start()
    meas_load = pltpu.make_async_copy(meas_ref.at[jnp.minimum(p, POS - 1)], meas, load.at[4])
    meas_load.start()
    own_probe = pltpu.make_async_copy(probe_ref.at[0], probe_in, prb_r)

    @pl.when(active & (mu == m))
    def _():
        own_probe.start()

    barrier = pltpu.get_barrier_semaphore()
    me = d * M + m
    for step in range(1, M * D):
        other = (me + step) % (M * D)
        pl.semaphore_signal(
            barrier, inc=1, device_id=(other % M, g, other // M), device_id_type=MESH
        )
    for device in (before, after):
        pl.semaphore_signal(barrier, inc=1, device_id=device, device_id_type=MESH)
    pl.semaphore_wait(barrier, M * D + 1)

    def rim_copy(ch):
        rows = pl.ds(ch * HC, HC)
        return remote(
            obj_ref.at[0, :, rows, :], rim.at[:, rows, :], rim_s.at[ch], rim_r.at[ch], before
        )

    for ch in range(CH):
        rim_copy(ch).start()

    def probe_needed(mode_at):
        return 2 * (((d // 2) * M + mode_at) // D) + c

    def probe_copy(step):
        return remote(
            probe_ref.at[0], probe_in, prb_s.at[step - 1], prb_r, ((m + step) % M, g, d)
        )

    def probe_goes(step):
        target = (m + step) % M
        return (probe_needed(target) == m) & (((d // 2) * M + target) % D < POS)

    for step in range(1, M):
        @pl.when(probe_goes(step))
        def _():
            probe_copy(step).start()

    lane = lax.broadcasted_iota(jnp.int32, (1, LANES), 1)
    low = lane < third

    sign = jnp.where(low, -1.0, 1.0)

    def swap(x):
        return pltpu.roll(x, third, 1)

    def pack(re, im):
        return [
            jnp.where(low, re[:, :LANES], swap(im[:, :LANES])),
            jnp.where(low, swap(re[:, :LANES]), im[:, :LANES]),
            jnp.where(low, re[:, LANES:], swap(im[:, LANES:])),
        ]

    def unpack(a, b, t):
        re = [jnp.where(low, a, swap(b)), jnp.where(low, t, 0.0)]
        im = [jnp.where(low, swap(a), b), jnp.where(low, swap(t), 0.0)]
        return jnp.concatenate(re, axis=1), jnp.concatenate(im, axis=1)

    def hot(mask):
        return jnp.where(mask, 1.0, 0.0).astype(BF16)

    def pieces(x, count):
        out = []
        for _ in range(count):
            out.append(x.astype(BF16))
            x = x - out[-1].astype(F32)
        return out

    def moved(x, rows_hot, cols_hot, count):
        x = sum(mm(rows_hot, one) for one in reversed(pieces(x, count)))
        return sum(mm(one, cols_hot) for one in reversed(pieces(x, count)))

    def expand(x):
        front, rear = x[:, :LANES], x[:, LANES:]
        turned = swap(front)
        return [
            jnp.where(low, front, turned),
            jnp.where(low, turned, front),
            jnp.where(low, rear, swap(rear)),
        ]

    def turn(angle):
        y = 0.5 * angle
        z = y * y
        sine = z * (1.0 / 6227020800.0) - 1.0 / 39916800.0
        for top in (362880.0, -5040.0, 120.0, -6.0, 1.0):
            sine = sine * z + 1.0 / top
        sine = sine * y
        cosine = z * (-1.0 / 87178291200.0) + 1.0 / 479001600.0
        for top in (-3628800.0, 40320.0, -720.0, 24.0, -2.0, 1.0):
            cosine = cosine * z + 1.0 / top
        return 1.0 - 2.0 * sine * sine, 2.0 * sine * cosine

    down = lax.broadcasted_iota(jnp.int32, (W, 1), 0)
    across = lax.broadcasted_iota(jnp.int32, (1, W), 1)
    col_id = lax.broadcasted_iota(jnp.int32, (1, WIDE), 1)

    loads[0].wait()
    meas_load.wait()

    @pl.when(active)
    def _():
        rows_hot = hot(across == 3 * (down % third) + down // third)
        cols_hot = hot((down == 3 * (col_id % third) + col_id // third) & (col_id < W))
        wanted[...] = moved(meas[...], rows_hot, cols_hot, 2)
        cosine, sine = turn(moved(phase[...], rows_hot, cols_hot, 3))
        for at, value in enumerate(expand(cosine)):
            kern[0, at] = value
        for at, value in enumerate(expand(sine)):
            kern[1, at] = sign * value

    loads[1].wait()
    row_id = lax.broadcasted_iota(jnp.int32, (H, 1), 0) + m * H

    def frame_copy(pos, k, start=0, rows=H):
        to_m, _ = handler(pos, 2 * k)
        to_d = 2 * ((D * k + pos) // M) + c
        source = fr.at[pos, :, pl.ds(start, rows), :]
        place = win.at[d, :, pl.ds(pl.multiple_of(m * H + start, 8), rows), :]
        own = (m == to_m) & (d == to_d)
        far_copy = remote(source, place, fr_s.at[pos, k], win_r.at[d, m], (to_m, g, to_d))
        near_copy = pltpu.make_async_copy(source, place, win_r.at[d, m])
        return own, far_copy, near_copy

    for ch in range(CH):
        rim_copy(ch).wait_recv()
        rows = slice(ch * HC, (ch + 1) * HC)
        for pos in range(POS):
            row_off = pos_ref[0, pos] - g * W
            col_off = pos_ref[1, pos]
            parts = []
            for part in range(2):
                chosen = jnp.where(row_id[rows] >= row_off, tile[part, rows], rim[part, rows])
                wrapped = pltpu.roll(chosen, WIDE - W, 1)
                parts.append(jnp.where(col_id >= col_off, chosen, wrapped))

            for at, value in enumerate(pack(parts[0], parts[1])):
                fr[pos, at, rows] = value
            for k in range(half):
                own, far_copy, near_copy = frame_copy(pos, k, ch * HC, HC)

                @pl.when(own)
                def _():
                    near_copy.start()

                @pl.when(jnp.logical_not(own))
                def _():
                    far_copy.start()

    loads[2].wait()
    loads[3].wait()

    sign_root = sign * (0.5 * math.sqrt(3.0))
    sign_wide = jnp.concatenate([sign] * 3, axis=1).astype(BF16)

    def combine(a, b, c):
        both = b + c
        turned = swap(b - c) * sign_root
        base = a - 0.5 * both
        return a + both, base - turned, base + turned

    def join(values, axis):
        return jnp.concatenate(values, axis=axis)

    def times_i(x):
        parts = [swap(x[:, at * LANES : (at + 1) * LANES]) for at in range(3)]
        return join(parts, 1) * sign_wide

    def by_rows(at, x):
        head, rest = split(x)
        out = mm(row_t[at], join([head, times_i(head), rest, times_i(rest)], 0))
        return out[:third] + out[third:]

    def by_columns(at, x):
        head, rest = split(x)
        out = mm(join([head, rest], 1), col_t[at])
        return out[:, :LANES] + out[:, LANES:]

    def row_parts(x, q):
        return x[q * third : (q + 1) * third]

    def lane_parts(x, q):
        return x[:, q * LANES : (q + 1) * LANES]

    def dft(x):
        mixed = [combine(*[row_parts(one, q) for q in range(3)]) for one in x]
        out = [by_rows(q, join([one[q] for one in mixed], 1)) for q in range(3)]
        x = [join([lane_parts(one, at) for one in out], 0) for at in range(3)]
        mixed = combine(*x)
        return [by_columns(q, mixed[q]) for q in range(3)]

    def idft(x):
        out = [by_columns(3 + q, x[q]) for q in range(3)]
        first, second, last_ = combine(*out)
        x = [first, last_, second]
        out = [by_rows(3 + q, join([row_parts(one, q) for one in x], 1)) for q in range(3)]
        mixed = [combine(*[lane_parts(one, at) for one in out]) for at in range(3)]
        return [join([one[0], one[2], one[1]], 0) for one in mixed]

    def factor(x):
        turned = swap(x)
        return jnp.where(low, x, turned), jnp.where(low, -turned, x)

    def mul(x, pair):
        return [one * a + swap(one) * b for one, (a, b) in zip(x, pair)]

    def cmul(x, pair):
        return [one * a - swap(one) * b for one, (a, b) in zip(x, pair)]

    def kernel_pair():
        return [(kern[0, at], kern[1, at]) for at in range(3)]

    def field(ref, *at):
        return [ref[(*at, one)] for one in range(3)]

    def put(ref, x, *at):
        for one in range(3):
            ref[(*at, one)] = x[one]

    def unpack_window(s):
        for at in range(3):
            kept[s, 0, at], kept[s, 1, at] = factor(win[s, at])

    def window(s):
        return [(kept[s, 0, at], kept[s, 1, at]) for at in range(3)]

    def fwd_copy(s):
        return remote(win.at[s], win.at[s], fwd_s.at[s], fwd_r.at[s], partner)

    def int_copy(step):
        to_m, to_d = handler(p, (mu + step) % M)
        return remote(
            inten.at[0], inten.at[step], int_s.at[step - 1], int_r.at[step - 1], (to_m, g, to_d)
        )

    def pair_copy(s, to_m, ch):
        rows = pl.ds(to_m * H + ch * HC, HC)
        return remote(
            gs.at[s, :, rows, :], pg.at[s, :, rows, :], pg_s.at[s], pg_r.at[s, to_m, ch], partner
        )

    slot = p * half + mu // 2

    def owner_copy(s, to_m, start=0, rows=H, ch=0):
        source = gs.at[s, :, pl.ds(to_m * H + start, rows), :]
        place = og.at[slot, :, pl.ds(start, rows), :]
        own = (m == to_m) & (d == s)
        far_copy = remote(source, place, og_s.at[s, to_m], og_r.at[slot, ch], (to_m, g, s))
        near_copy = pltpu.make_async_copy(source, place, og_r.at[slot, ch])
        return own, far_copy, near_copy

    def send_gradient(s, incident):
        put(gs, cmul(incident, [factor(one) for one in field(psi, s)]), s)

        @pl.when(s % 2 != c)
        def _():
            for to_m in range(M):
                for ch in range(CH):
                    pair_copy(s, to_m, ch).start()

    def finish_gradient(s):
        @pl.when(s % 2 == c)
        def _():
            for to_m in range(M):
                for ch in range(CH):
                    rows = pl.ds(to_m * H + ch * HC, HC)
                    arrived(pg.at[s, :, rows, :], pg_r.at[s, to_m, ch])
                    gs[s, :, rows, :] = gs[s, :, rows, :] + pg[s, :, rows, :]
                    own, far_copy, near_copy = owner_copy(s, to_m, ch * HC, HC, ch)

                    @pl.when(own)
                    def _():
                        near_copy.start()

                    @pl.when(jnp.logical_not(own))
                    def _():
                        far_copy.start()

    @pl.when(active)
    def _():
        arrived(probe_in, prb_r)
        row_off = pos_ref[0, p] - g * W
        col_off = pos_ref[1, p]
        i = down - row_off
        rows_hot = hot((i == across) | (i + W == across))
        b = col_id - col_off
        cols_hot = hot(((b == down) | (b + W == down)) & (col_id < W))
        start = [moved(probe_in[part], rows_hot, cols_hot, 2) for part in range(2)]
        put(psi, pack(*start), 0)

        def pass_on(at):
            s = 2 * at + c
            for from_m in range(M):
                arrived(win.at[s, :, pl.ds(from_m * H, H), :], win_r.at[s, from_m])
            fwd_copy(s).start()

        pass_on(0)

        def await_window(s):
            @pl.when(s % 2 != c)
            def _():
                arrived(win.at[s], fwd_r.at[s])

        def forward(s, carry):
            await_window(s)
            unpack_window(s)
            spectrum = dft(mul(field(psi, s), window(s)))
            put(psi, idft(mul(spectrum, kernel_pair())), s + 1)

            @pl.when((s % 2 == 0) & (s + 2 < D))
            def _():
                pass_on(s // 2 + 1)

            return carry

        lax.fori_loop(0, D - 1, forward, 0)
        last = D - 1
        await_window(last)
        unpack_window(last)
        spectrum = mul(dft(mul(field(psi, last), window(last))), kernel_pair())
        put(far, spectrum)
        power = [one * one for one in spectrum]
        power = [one + swap(one) for one in power]
        inten[0, :, :LANES] = jnp.where(low, power[0], power[1])
        inten[0, :, LANES:] = power[2]
        for step in range(1, M):
            int_copy(step).start()
        for step in range(1, M):
            arrived(inten.at[step], int_r.at[step - 1])
        total = inten[0]
        for step in range(1, M):
            total = total + inten[step]
        misfit = expand(2.0 * (total - wanted[...]))
        weighted = [misfit[at] * far[at] for at in range(3)]
        incident = idft(cmul(weighted, kernel_pair()))
        send_gradient(last, incident)
        put(up, cmul(incident, window(last)))

        def backward(at, carry):
            s = D - 2 - at
            incident = idft(cmul(dft(field(up)), kernel_pair()))
            send_gradient(s, incident)
            finish_gradient(s + 1)
            put(up, cmul(incident, window(s)))
            return carry

        lax.fori_loop(0, D - 1, backward, 0)
        finish_gradient(jnp.int32(0))

    def rg_copy(ch):
        rows = pl.ds(ch * HC, HC)
        return remote(
            rg_out.at[:, rows, :], rg_in.at[:, rows, :], rg_s.at[ch], rg_r.at[ch], after
        )

    for ch in range(CH):
        rows = slice(ch * HC, (ch + 1) * HC)
        kept_here = [jnp.zeros((HC, WIDE), F32) for _ in range(2)]
        passed = [jnp.zeros((HC, WIDE), F32) for _ in range(2)]
        for pos in range(POS):
            row_off = pos_ref[0, pos] - g * W
            col_off = pos_ref[1, pos]
            for k in range(half):
                at = pos * half + k
                arrived(og.at[at, :, pl.ds(ch * HC, HC), :], og_r.at[at, ch])
            parts = [og[pos * half, at, rows] for at in range(3)]
            for k in range(1, half):
                parts = [parts[at] + og[pos * half + k, at, rows] for at in range(3)]
            both = unpack(*parts)
            for part in range(2):
                inside = jnp.where(col_id >= col_off, both[part], 0.0)
                outside = jnp.where(col_id < col_off, both[part], 0.0)
                placed = inside + pltpu.roll(outside, W, 1)
                own_rows = row_id[rows] >= row_off
                kept_here[part] += jnp.where(own_rows, placed, 0.0)
                passed[part] += jnp.where(own_rows, 0.0, placed)
        for part in range(2):
            rg_out[part, rows] = passed[part]
        rg_copy(ch).start()
        for part in range(2):
            out_ref[0, part, rows] = kept_here[part]
    for ch in range(CH):
        rows = slice(ch * HC, (ch + 1) * HC)
        rg_copy(ch).wait_recv()
        for part in range(2):
            out_ref[0, part, rows] += rg_in[part, rows]

    for ch in range(CH):
        rg_copy(ch).wait_send()
        rim_copy(ch).wait_send()
    for step in range(1, M):
        @pl.when(probe_goes(step))
        def _():
            probe_copy(step).wait_send()
    for pos in range(POS):
        for k in range(half):
            own, far_copy, _ = frame_copy(pos, k)

            @pl.when(jnp.logical_not(own))
            def _():
                far_copy.wait_send()

    @pl.when(active)
    def _():
        for step in range(1, M):
            int_copy(step).wait_send()
        for s in range(D):
            @pl.when(s % 2 == c)
            def _():
                fwd_copy(s).wait_send()
                for to_m in range(M):
                    own, far_copy, _ = owner_copy(s, to_m)

                    @pl.when(jnp.logical_not(own))
                    def _():
                        far_copy.wait_send()

            @pl.when(s % 2 != c)
            def _():
                whole = remote(gs.at[s], pg.at[s], pg_s.at[s], pg_r.at[s, 0, 0], partner)
                whole.wait_send()


def solution(mesh):
    M, N, D = mesh.shape["mode"], mesh.shape["dp"], mesh.shape["depth"]

    def body(probe, object_slices, propagator_phase, positions, measured):
        W = probe.shape[-1]
        H, WIDE = object_slices.shape[2], object_slices.shape[3]
        POS = positions.shape[0]
        assert object_slices.shape[0] == 1 and probe.shape[0] == 1
        assert H * M == W and POS <= D and WIDE == 2 * LANES and 2 * W == 3 * LANES
        half = M // 2
        CH = 6 if H % 48 == 0 else 3 if H % 24 == 0 else 1
        tables = [jnp.asarray(table) for table in dft_tables(W)]
        vmem = pl.BlockSpec(memory_space=pltpu.VMEM)
        hbm = pl.BlockSpec(memory_space=pltpu.HBM)
        dma = pltpu.SemaphoreType.DMA
        return pl.pallas_call(
            functools.partial(kernel, M, N, D, POS, W, H, WIDE, CH),
            out_shape=jax.ShapeDtypeStruct(object_slices.shape, F32),
            in_specs=[pl.BlockSpec(memory_space=pltpu.SMEM)] + [hbm] * 6,
            out_specs=vmem,
            scratch_shapes=[
                pltpu.VMEM((2, H, WIDE), F32),
                pltpu.VMEM((W, W), F32),
                pltpu.VMEM((W, W), F32),
                pltpu.VMEM(tables[0].shape, BF16),
                pltpu.VMEM(tables[1].shape, BF16),
                pltpu.VMEM((2, H, WIDE), F32),
                pltpu.VMEM((2, W, W), F32),
                pltpu.VMEM((POS, 3, H, LANES), F32),
                pltpu.VMEM((D, 3, W, LANES), F32),
                pltpu.VMEM((D, 3, W, LANES), F32),
                pltpu.VMEM((2, 3, W, LANES), F32),
                pltpu.VMEM((W, WIDE), F32),
                pltpu.VMEM((M, W, WIDE), F32),
                pltpu.VMEM((3, W, LANES), F32),
                pltpu.VMEM((3, W, LANES), F32),
                pltpu.VMEM((D, 2, 3, W, LANES), F32),
                pltpu.VMEM((D, 3, W, LANES), F32),
                pltpu.VMEM((D, 3, W, LANES), F32),
                pltpu.VMEM((POS * half, 3, H, LANES), F32),
                pltpu.VMEM((2, H, WIDE), F32),
                pltpu.VMEM((2, H, WIDE), F32),
                dma((5,)), dma((CH,)), dma((CH,)),
                dma((M - 1,)), dma,
                dma((POS, half)), dma((D, M)),
                dma((D,)), dma((D,)),
                dma((M - 1,)), dma((M - 1,)),
                dma((D,)), dma((D, M, CH)),
                dma((D, M)), dma((POS * half, CH)),
                dma((CH,)), dma((CH,)),
            ],
            compiler_params=pltpu.CompilerParams(
                collective_id=0, has_side_effects=True, vmem_limit_bytes=63 * 1024 * 1024
            ),
        )(positions.T, probe, object_slices, propagator_phase, measured, *tables)

    placed = (
        P("mode", None, None, None),
        P("depth", None, ("dp", "mode"), None),
        P(),
        P("dp", None),
        P("dp", None, None),
    )
    return jax.shard_map(
        body,
        mesh=mesh,
        in_specs=placed,
        out_specs=P("depth", None, ("dp", "mode"), None),
        check_vma=False,
    )
```
